256 devices in a mesh: gx: 16 (over y, x), gy: 16 (over z, core).
Axes of the slice: x: 4, y: 4, z: 8, core: 2. Of those that a mesh axis runs over, the one named last changes fastest.
Arguments:
- rhs: float32 [3, 128, 128, 512], P(None, 'gx', 'gy'), may hold values from -6 to 6
- stiffness: float32 [3, 128, 128, 512], P(None, 'gx', 'gy'), may hold values from 1 to 4
- couplings: bfloat16 [7, 3, 3, 128, 128, 512], P(None, None, None, 'gx', 'gy'), may hold values from -0.59765625 to 0.59765625
- tentative: bfloat16 [3, 6, 128, 128, 512], P(None, None, 'gx', 'gy'), may hold values from -1.1953125 to 1.1953125
- members: int32 [128, 128, 512], P('gx', 'gy'), may hold values from 0 to 1023
- coarse_stiffness: float32 [6, 262144], P(None, ('gx', 'gy')), may hold values from 1 to 4
- coarse_couplings: float32 [27, 36, 262144], P(None, None, ('gx', 'gy')), may hold values from -0.6 to 0.6
- coarse_columns: int32 [27, 262144], P(None, ('gx', 'gy')), may hold values from 0 to 2047
- send_lists: int32 [4, 65536], P(None, ('gx', 'gy')), may hold values from 0 to 1023
- coarse_tentative: float32 [36, 262144], P(None, ('gx', 'gy')), may hold values from -0.3125 to 0.3125
- coarse_members: int32 [262144], P(('gx', 'gy')), may hold values from 0 to 1
- coarsest_inverse: float32 [3072, 3072], P('gy', 'gx'), may hold values from -0.21875 to 0.21875
Outputs:
- solution: float32 [3, 128, 128, 512], P(None, 'gx', 'gy')
- coarse_solution: float32 [6, 262144], P(None, ('gx', 'gy'))
The draws below stay inside these ranges and needn't reach their ends.
All inputs are finite; a program needn't handle non-finite values.
Results may differ from the reference program's by a relative error of at most 0.0015.
Values may be sent and summed in bfloat16 or wider, within the bound.
A program may use at most 128 MiB of HBM per device.

```python
import math
import jax
import jax.numpy as jnp
from jax import lax

FX = 8
FY = 8
NZ = 512
K = 27
A2 = 2
A1 = 1024
H = 256
NX = 128
NY = 128
C1TOT = 262144
HTOT = 65536
N2 = 3072
N_GX = 16
N_GY = 16
DEVICES = 256


def touch_ends(result, own_key, least, largest):
    place = [jax.random.randint(jax.random.fold_in(own_key, axis), (), 0, length) for axis, length in enumerate(result.shape)]
    main_axis = result.shape.index(max(result.shape))
    beside = place[:main_axis] + [(place[main_axis] + 1) % result.shape[main_axis]] + place[main_axis + 1:]
    return result.at[tuple(place)].set(least).at[tuple(beside)].set(largest)


def block_scale(key, shape, split, low, largest):
    def one(axis_at, shards_of):
        steps = jax.random.uniform(jax.random.fold_in(jax.random.fold_in(key, 6), axis_at), (shards_of,), jnp.float32, low / len(split), largest / len(split))
        return jnp.repeat(jnp.exp(steps), shape[axis_at] // shards_of).reshape((-1,) + (1,) * (len(shape) - axis_at - 1))

    level = one(*split[0])
    for cut in split[1:]:
        level = level * one(*cut)
    return level


def scatter_about(key, extent, scale, most, shards=(), kind=jnp.bfloat16):
    drawn = jax.random.normal(key, extent, jnp.float32) * scale
    if len(shards) > 0:
        drawn = block_scale(key, extent, shards, -0.22, 0.18) * drawn
    return jnp.clip(drawn, min=-most, max=most).astype(kind)


def setup_inputs(seed: int = 0) -> dict:
    key_of = jax.random.split(jax.random.key(seed), 13)
    return {
        "rhs": scatter_about(key_of[0], (3, NX, NY, NZ), 1.0, 6.0, ((1, 16), (2, 16)), jnp.float32),
        "stiffness": jnp.clip(jnp.exp(math.log(4.0) - 1.3862944 * jax.random.uniform(key_of[1], (3, NX, NY, NZ), jnp.float32) ** block_scale(key_of[1], (3, NX, NY, NZ), ((1, 16), (2, 16)), -0.2, 0.2)), 1.0, 4.0),
        "couplings": scatter_about(key_of[2], (7, 3, 3, NX, NY, NZ), 0.12, 0.59765625, ((3, 16), (4, 16))),
        "tentative": scatter_about(key_of[3], (3, 6, NX, NY, NZ), 0.4, 1.1953125, ((2, 16), (3, 16))),
        "members": touch_ends(jax.random.randint(key_of[4], (NX, NY, NZ), 0, A1), jax.random.fold_in(key_of[4], 1), 0, A1 - 1).astype(jnp.int32),
        "coarse_stiffness": jnp.clip(jnp.exp(math.log(4.0) - 1.3862944 * jax.random.uniform(key_of[5], (6, C1TOT), jnp.float32) ** block_scale(key_of[5], (6, C1TOT), ((1, 256),), -0.2, 0.2)), 1.0, 4.0),
        "coarse_couplings": scatter_about(key_of[6], (K, 36, C1TOT), 0.1, 0.6, ((2, 256),), jnp.float32),
        "coarse_columns": touch_ends(jax.random.randint(key_of[7], (K, C1TOT), 0, A1 + 4 * H), jax.random.fold_in(key_of[7], 1), 0, (A1 + 4 * H) - 1).astype(jnp.int32),
        "send_lists": touch_ends(jax.random.randint(key_of[8], (4, HTOT), 0, A1), jax.random.fold_in(key_of[8], 1), 0, A1 - 1).astype(jnp.int32),
        "coarse_tentative": scatter_about(key_of[9], (36, C1TOT), ((2 * A1) // (3 * A2)) ** -0.5, 0.3125, ((1, 256),), jnp.float32),
        "coarse_members": touch_ends(jax.random.randint(key_of[10], (C1TOT,), 0, A2), jax.random.fold_in(key_of[10], 1), 0, A2 - 1).astype(jnp.int32),
        "coarsest_inverse": scatter_about(key_of[11], (N2, N2), (N2 // 4) ** -0.5, 0.21875, ((0, 16), (1, 16)), jnp.float32),
    }


damping = 0.6
smoothing = 0.5


def fine_apply(field, stiffness, couplings):
    padded = jnp.pad(field, ((0, 0), (1, 1), (1, 1), (1, 1)))
    views = (padded[:, 1:-1, 1:-1, 1:-1], padded[:, :-2, 1:-1, 1:-1], padded[:, 2:, 1:-1, 1:-1],
             padded[:, 1:-1, :-2, 1:-1], padded[:, 1:-1, 2:, 1:-1],
             padded[:, 1:-1, 1:-1, :-2], padded[:, 1:-1, 1:-1, 2:])
    total = stiffness * field
    for offset in range(7):
        total = total + jnp.sum(couplings[offset].astype(jnp.float32) * views[offset][None], axis=1)
    return total


def coarse_apply(values, coarse_stiffness, coarse_couplings, coarse_columns, send_lists):
    grid = values.reshape(6, N_GX, N_GY, A1)
    sends = send_lists.reshape(4, N_GX, N_GY, H)
    row_index = jnp.arange(N_GX).reshape(N_GX, 1, 1)
    col_index = jnp.arange(N_GY).reshape(1, N_GY, 1)
    sent = [grid[:, row_index, col_index, sends[direction]] for direction in range(4)]
    blank_x = jnp.zeros((6, 1, N_GY, H), jnp.float32)
    blank_y = jnp.zeros((6, N_GX, 1, H), jnp.float32)
    from_low_x = jnp.concatenate([blank_x, sent[0][:, :-1]], axis=1)
    from_high_x = jnp.concatenate([sent[1][:, 1:], blank_x], axis=1)
    from_low_y = jnp.concatenate([blank_y, sent[2][:, :, :-1]], axis=2)
    from_high_y = jnp.concatenate([sent[3][:, :, 1:], blank_y], axis=2)
    extended = jnp.concatenate([grid, from_low_x, from_high_x, from_low_y, from_high_y], axis=3)
    columns = coarse_columns.reshape(K, N_GX, N_GY, A1)
    picked = extended[:, row_index[None], col_index[None], columns]
    picked = jnp.transpose(picked, (1, 0, 2, 3, 4))
    blocks = coarse_couplings.reshape(K, 6, 6, N_GX, N_GY, A1)
    total = jnp.sum(blocks * picked[:, None], axis=(0, 2)).reshape(6, C1TOT)
    return coarse_stiffness * values + total


def reference(rhs, stiffness, couplings, tentative, members, coarse_stiffness, coarse_couplings,
              coarse_columns, send_lists, coarse_tentative, coarse_members, coarsest_inverse):
    xpos = jnp.arange(NX).astype(jnp.int32).reshape(NX, 1, 1)
    ypos = jnp.arange(NY).astype(jnp.int32).reshape(1, NY, 1)
    owners = ((xpos // FX) * N_GY + ypos // FY) * A1 + members
    owners = owners.astype(jnp.int32)

    def apply_fine(field):
        return fine_apply(field, stiffness, couplings)

    def apply_coarse(values):
        return coarse_apply(values, coarse_stiffness, coarse_couplings, coarse_columns, send_lists)

    x1 = damping * rhs / stiffness
    x2 = x1 + damping * (rhs - apply_fine(x1)) / stiffness
    r2 = rhs - apply_fine(x2)
    filtered = r2 - smoothing * apply_fine(r2 / stiffness)
    contrib = jnp.sum(tentative.astype(jnp.float32) * filtered[:, None], axis=0)
    coarse_rhs = jax.ops.segment_sum(contrib.reshape(6, -1).T, owners.reshape(-1), num_segments=C1TOT).T
    y1 = damping * coarse_rhs / coarse_stiffness
    s1 = coarse_rhs - apply_coarse(y1)
    blocks = coarse_tentative.reshape(6, 6, C1TOT)
    contrib2 = jnp.sum(blocks * s1[:, None], axis=0)
    device_of = (jnp.arange(C1TOT) // A1).astype(jnp.int32)
    owners2 = (device_of * A2 + coarse_members).astype(jnp.int32)
    summed = jax.ops.segment_sum(contrib2.T, owners2, num_segments=DEVICES * A2)
    coarsest_rhs = jnp.transpose(summed.reshape(DEVICES, A2, 6), (0, 2, 1)).reshape(-1)
    coarsest = jnp.dot(coarsest_inverse, coarsest_rhs, precision=lax.Precision.HIGHEST)
    spread = coarsest.reshape(DEVICES, 6, A2)[device_of, :, coarse_members].T
    y2 = y1 + jnp.sum(blocks * spread[None], axis=1)
    coarse_solution = y2 + damping * (coarse_rhs - apply_coarse(y2)) / coarse_stiffness
    picked = jnp.take(coarse_solution, owners, axis=1)
    lifted = jnp.sum(tentative.astype(jnp.float32) * picked[None], axis=1)
    x3 = x2 + lifted - smoothing * apply_fine(lifted) / stiffness
    x4 = x3 + damping * (rhs - apply_fine(x3)) / stiffness
    solution = x4 + damping * (rhs - apply_fine(x4)) / stiffness
    return solution, coarse_solution
```

```python
import functools

import jax
import jax.numpy as jnp
from jax import lax
from jax.experimental import pallas as pl
from jax.experimental.pallas import tpu as pltpu
from jax.sharding import PartitionSpec as P

MESH = pl.DeviceIdType.MESH
F32 = jnp.float32
BF16 = jnp.bfloat16

FX = 8
FY = 8
NZ = 512
K = 27
A1 = 1024
H = 256
LANES = 128
FIELDS = 6

damping = 0.6
smoothing = 0.5


def lane_gather(table, index):
    dims = lax.GatherDimensionNumbers(
        offset_dims=(),
        collapsed_slice_dims=(1,),
        start_index_map=(1,),
        operand_batching_dims=(0,),
        start_indices_batching_dims=(0,),
    )
    return lax.gather(
        table, index[..., None], dims, slice_sizes=(1, 1), mode=lax.GatherScatterMode.PROMISE_IN_BOUNDS
    )


def pick(tables, index):
    low = index & (LANES - 1)
    parts = [lane_gather(table, low) for table in tables]
    bit = LANES
    while len(parts) > 1:
        upper = (index & bit) != 0
        parts = [jnp.where(upper, parts[at + 1], parts[at]) for at in range(0, len(parts), 2)]
        bit *= 2
    return parts[0]


def rows_of(piece, rows):
    sub = lax.broadcasted_iota(jnp.int32, (rows, 1), 0)
    first, last = (8 * piece) // 6, min((8 * piece + 7) // 6, 5)
    i = jnp.where(sub < 6 * (first + 1) - 8 * piece, first, last)
    return i, 8 * piece + sub - 6 * i


def kernel(
    nx,
    ny,
    rhs_h,
    stf_h,
    cpl_h,
    ten_h,
    mem_h,
    cst_h,
    ccp_h,
    col_h,
    snd_h,
    ctn_h,
    cmb_h,
    inv_h,
    sol,
    csol,
    rhs,
    stf,
    cpl,
    ten,
    mem,
    cst,
    ccp,
    col,
    snd,
    ctn,
    cmb,
    inv,
    wgt,
    field,
    yout,
    yin,
    acc,
    resid,
    nodes,
    crhs,
    y2,
    ext,
    cout,
    cacc,
    own_row,
    rows,
    part_row,
    parts,
    load_sem,
    fsend,
    frecv,
    csend,
    crecv,
    gsend,
    grecv,
    psend,
    precv,
):
    gx, gy = lax.axis_index("gx"), lax.axis_index("gy")
    near = (
        (gx > 0, {"gx": jnp.maximum(gx - 1, 0), "gy": gy}),
        (gx < nx - 1, {"gx": jnp.minimum(gx + 1, nx - 1), "gy": gy}),
        (gy > 0, {"gx": gx, "gy": jnp.maximum(gy - 1, 0)}),
        (gy < ny - 1, {"gx": gx, "gy": jnp.minimum(gy + 1, ny - 1)}),
    )

    loads = {}
    pairs = [("rhs", rhs_h, rhs), ("stf", stf_h, stf)]
    for offset in (0, 5, 6, 1, 2, 3, 4):
        pairs.append(("cpl%d" % offset, cpl_h.at[pl.ds(9 * offset, 9)], cpl.at[pl.ds(9 * offset, 9)]))
    pairs += [
        ("ten", ten_h, ten),
        ("mem", mem_h, mem),
        ("cst", cst_h, cst),
        ("snd", snd_h, snd),
        ("col", col_h, col),
        ("ccp", ccp_h, ccp),
        ("ctn", ctn_h, ctn),
        ("cmb", cmb_h, cmb),
        ("inv", inv_h, inv),
    ]
    for number, (name, source, target) in enumerate(pairs):
        loads[name] = pltpu.make_async_copy(source, target, load_sem.at[number])
        loads[name].start()

    barrier = pltpu.get_barrier_semaphore()
    for there, device in near:

        @pl.when(there)
        def _():
            pl.semaphore_signal(barrier, inc=1, device_id=device, device_id_type=MESH)

    def greet(step, carry):
        other = lax.rem(gy + step, ny)
        pl.semaphore_signal(barrier, inc=1, device_id={"gx": gx, "gy": other}, device_id_type=MESH)
        return carry

    lax.fori_loop(1, ny, greet, 0)

    def greet_sender(step, carry):
        other = lax.rem(gx + step, nx)

        @pl.when(jnp.logical_not(jnp.logical_and(other == gx, gx == gy)))
        def _():
            pl.semaphore_signal(barrier, inc=1, device_id={"gx": other, "gy": gx}, device_id_type=MESH)

        return carry

    lax.fori_loop(0, nx, greet_sender, 0)

    blank = jnp.zeros((FIELDS, 3, FY, NZ), F32)
    for side, (there, _) in enumerate(near):

        @pl.when(jnp.logical_not(there))
        def _():
            for number in range(FIELDS):
                if side < 2:
                    field[number, :, 0 if side == 0 else FX + 1] = blank[0]
                else:
                    yin[number, side - 2] = blank[0]
            for number in range(2):
                ext[number, :, pl.ds(A1 + H * side, H)] = jnp.zeros((8, H), F32)

    cacc[pl.ds(32, 8), :] = jnp.zeros((8, A1), F32)
    own_row[...] = jnp.zeros_like(own_row)
    part_row[...] = jnp.zeros_like(part_row)

    def halo(number, side):
        if side == 0:
            source, target, at = field.at[number, :, 1], field.at[number, :, FX + 1], 1
        elif side == 1:
            source, target, at = field.at[number, :, FX], field.at[number, :, 0], 0
        elif side == 2:
            source, target, at = yout.at[number, 0], yin.at[number, 1], 3
        else:
            source, target, at = yout.at[number, 1], yin.at[number, 0], 2
        return pltpu.make_async_remote_copy(
            src_ref=source,
            dst_ref=target,
            send_sem=fsend.at[number, side],
            recv_sem=frecv.at[number, at],
            device_id=near[side][1],
            device_id_type=MESH,
        )

    def send_halo(number, side):
        @pl.when(near[side][0])
        def _():
            halo(number, side).start()

    def wait_halo(number):
        for side in range(4):

            @pl.when(near[side][0])
            def _():
                halo(number, side ^ 1).wait_recv()

    def put_field(number, x, values):
        for c in range(3):
            field[number, c, x + 1] = values[c]
            yout[number, 0, c, pl.ds(x, 1), :] = values[c][0:1, :]
            yout[number, 1, c, pl.ds(x, 1), :] = values[c][FY - 1 : FY, :]

    def slabs(number, slab):
        slab(0)
        if number is not None:
            send_halo(number, 0)
        slab(FX - 1)
        if number is not None:
            send_halo(number, 1)

        def inner(x, carry):
            slab(x)
            return carry

        lax.fori_loop(1, FX - 1, inner, 0)
        if number is not None:
            send_halo(number, 2)
            send_halo(number, 3)

    def add(total, offset, x, j, view):
        for i in range(3):
            total[i] = total[i] + cpl[9 * offset + 3 * i + j, x].astype(F32) * view

    def inside(number):
        lane = lax.broadcasted_iota(jnp.int32, (FY, NZ), 1)

        def slab(x):
            total = [stf[i, x] * field[number, i, x + 1] for i in range(3)]
            for j in range(3):
                view = field[number, j, x + 1]
                add(total, 0, x, j, view)
                add(total, 5, x, j, jnp.where(lane == 0, 0.0, pltpu.roll(view, 1, axis=1)))
                add(total, 6, x, j, jnp.where(lane == NZ - 1, 0.0, pltpu.roll(view, NZ - 1, axis=1)))
                if not (isinstance(x, int) and x == 0):
                    add(total, 1, x, j, field[number, j, x])
                if not (isinstance(x, int) and x == FX - 1):
                    add(total, 2, x, j, field[number, j, x + 2])
            for i in range(3):
                acc[i, x] = total[i]

        slabs(None, slab)

    def outside(number, x):
        row = lax.broadcasted_iota(jnp.int32, (FY, NZ), 0)
        total = [acc[i, x] for i in range(3)]
        for j in range(3):
            view = field[number, j, x + 1]
            below = yin[number, 0, j, pl.ds(x, 1), :]
            above = yin[number, 1, j, pl.ds(x, 1), :]
            add(total, 3, x, j, jnp.where(row == 0, below, pltpu.roll(view, 1, axis=0)))
            add(total, 4, x, j, jnp.where(row == FY - 1, above, pltpu.roll(view, FY - 1, axis=0)))
            if isinstance(x, int) and x == 0:
                add(total, 1, x, j, field[number, j, 0])
            if isinstance(x, int) and x == FX - 1:
                add(total, 2, x, j, field[number, j, FX + 1])
        return total

    loads["rhs"].wait()
    loads["stf"].wait()

    def first(x):
        values = []
        for c in range(3):
            weight = 1.0 / stf[c, x]
            wgt[c, x] = weight
            values.append(damping * rhs[c, x] * weight)
        put_field(0, x, values)

    def first_slab(x, carry):
        first(x)
        return carry

    lax.fori_loop(0, FX, first_slab, 0)

    others = (
        sum(there.astype(jnp.int32) for there, _ in near) + (ny - 1) + nx - (gx == gy).astype(jnp.int32)
    )
    pl.semaphore_wait(barrier, others)
    for side in range(4):
        send_halo(0, side)

    for offset in (0, 5, 6, 1, 2, 3, 4):
        loads["cpl%d" % offset].wait()

    def smoothed(number, x):
        total = outside(number, x)
        return [
            field[number, c, x + 1] + damping * (rhs[c, x] - total[c]) * wgt[c, x] for c in range(3)
        ]

    inside(0)
    wait_halo(0)
    slabs(1, lambda x: put_field(1, x, smoothed(0, x)))

    def residual(x):
        total = outside(1, x)
        values = []
        for c in range(3):
            left = rhs[c, x] - total[c]
            resid[c, x] = left
            values.append(left * wgt[c, x])
        put_field(2, x, values)

    inside(1)
    wait_halo(1)
    slabs(2, residual)

    loads["ten"].wait()

    def restrict(x):
        total = outside(2, x)
        filtered = [resid[i, x] - smoothing * total[i] for i in range(3)]
        for c in range(6):
            value = ten[c, x].astype(F32) * filtered[0]
            for i in range(1, 3):
                value = value + ten[6 * i + c, x].astype(F32) * filtered[i]
            for t in range(NZ // LANES):
                part = value[:, LANES * t : LANES * (t + 1)]
                nodes[x, t, pl.ds(8 * c, 8), :] = part
                if c < 2:
                    nodes[x, t, pl.ds(8 * (c + 6), 8), :] = part

    inside(2)
    wait_halo(2)
    slabs(None, restrict)

    loads["mem"].wait()
    count = lax.broadcasted_iota(jnp.int32, (16, NZ), 0).astype(F32).astype(BF16)

    def sums(x, total):
        for y in range(FY):
            value = jnp.concatenate(
                [nodes[x, t, pl.ds(y, 8, stride=8), :] for t in range(NZ // LANES)], axis=1
            )
            rounded = value.astype(BF16).astype(F32)
            both = jnp.concatenate([rounded, value - rounded], axis=0).astype(BF16)
            index = jnp.broadcast_to(mem[x, pl.ds(y, 1), :], (16, NZ))
            low = (index & (LANES - 1)).astype(F32).astype(BF16)
            high = lax.shift_right_logical(index, 7).astype(F32).astype(BF16)
            zero = jnp.zeros((16, NZ), BF16)
            one = jnp.ones((16, NZ), BF16)
            left = jnp.concatenate([jnp.where(high == float(h), both, zero) for h in range(8)], axis=0)
            right = jnp.concatenate(
                [jnp.where(low == count + float(16 * k), one, zero) for k in range(8)], axis=0
            )
            total = total + lax.dot_general(
                left, right, (((1,), (1,)), ((), ())), preferred_element_type=F32
            )
        return total

    gathered = lax.fori_loop(0, FX, sums, jnp.zeros((LANES, LANES), F32))

    loads["cst"].wait()
    loads["snd"].wait()
    for h in range(8):
        span = pl.ds(LANES * h, LANES)
        crhs[:, span] = gathered[16 * h : 16 * h + 8] + gathered[16 * h + 8 : 16 * h + 16]
    cst8 = jnp.concatenate([cst[...], cst[0:2, :]], axis=0)
    ext[0, :, pl.ds(0, A1)] = damping * crhs[...] / cst8

    def coarse_halo(number, side):
        return pltpu.make_async_remote_copy(
            src_ref=cout.at[number, side],
            dst_ref=ext.at[number, :, pl.ds(A1 + H * side, H)],
            send_sem=csend.at[number, side],
            recv_sem=crecv.at[number, side],
            device_id=near[side ^ 1][1],
            device_id_type=MESH,
        )

    def send_coarse(number):
        tables = [ext[number, :, pl.ds(LANES * h, LANES)] for h in range(A1 // LANES)]
        for side in range(4):
            for t in range(H // LANES):
                index = jnp.broadcast_to(snd[side : side + 1, pl.ds(LANES * t, LANES)], (8, LANES))
                cout[number, side, :, pl.ds(LANES * t, LANES)] = pick(tables, index)

            @pl.when(near[side ^ 1][0])
            def _():
                coarse_halo(number, side).start()

    sub = lax.broadcasted_iota(jnp.int32, (8, LANES), 0)

    def coarse_apply(number):
        for side in range(4):

            @pl.when(near[side][0])
            def _():
                coarse_halo(number, side).wait_recv()

        def group(t, carry):
            span = pl.ds(pl.multiple_of(LANES * t, LANES), LANES)
            tables = [ext[number, :, pl.ds(LANES * h, LANES)] for h in range((A1 + 4 * H) // LANES)]
            total = [jnp.zeros((8 if piece < 4 else 4, LANES), F32) for piece in range(5)]
            columns = col[:, span]
            for k in range(K):
                base = pick(tables, jnp.broadcast_to(columns[k : k + 1], (8, LANES)))
                up2, by4, down2 = (pltpu.roll(base, by, axis=0) for by in (6, 4, 2))
                turned = (base, jnp.where(sub < 6, up2, by4), jnp.where(sub < 2, by4, down2))
                for piece in range(5):
                    size = 8 if piece < 4 else 4
                    block = ccp[k, pl.ds(8 * piece, size), span]
                    total[piece] = total[piece] + block * turned[piece % 3][:size]
            for piece in range(5):
                cacc[pl.ds(8 * piece, 8 if piece < 4 else 4), span] = total[piece]
            return carry

        lax.fori_loop(0, A1 // LANES, group, 0)

    fold_row = lax.broadcasted_iota(jnp.int32, (8, 40), 0)
    fold_col = lax.broadcasted_iota(jnp.int32, (8, 40), 1)
    fold_row = jnp.where(fold_row < 6, fold_row, fold_row - 6)
    fold = jnp.logical_and(fold_col >= 6 * fold_row, fold_col < 6 * fold_row + 6).astype(F32)

    def folded():
        return jnp.dot(fold, cacc[...], precision=lax.Precision.HIGHEST, preferred_element_type=F32)

    send_coarse(0)
    loads["col"].wait()
    loads["ccp"].wait()
    coarse_apply(0)
    s1 = crhs[...] - (cst8 * ext[0, :, pl.ds(0, A1)] + folded())

    loads["ctn"].wait()
    loads["cmb"].wait()
    loads["inv"].wait()
    lane = lax.broadcasted_iota(jnp.int32, (1, 2 * LANES), 1)
    upper = cmb[...] != 0
    row = jnp.zeros((1, 2 * LANES), F32)
    for piece in range(5):
        size = 8 if piece < 4 else 4
        i, c = rows_of(piece, size)
        first_i, last_i = (8 * piece) // 6, min((8 * piece + 7) // 6, 5)
        matching = jnp.where(i == first_i, s1[first_i : first_i + 1], s1[last_i : last_i + 1])
        product = ctn[pl.ds(8 * piece, size), :] * matching
        for a in range(2):
            kept = jnp.where(upper, product, 0.0) if a else jnp.where(upper, 0.0, product)
            total = jnp.sum(kept, axis=1, keepdims=True)
            place = 12 * gy + 2 * c + a
            row = row + jnp.sum(jnp.where(lane == place, total, 0.0), axis=0, keepdims=True)
    own_row[...] = row

    def to_row(step):
        other = lax.rem(gy + step, ny)
        return pltpu.make_async_remote_copy(
            src_ref=own_row,
            dst_ref=rows.at[gy],
            send_sem=gsend.at[other],
            recv_sem=grecv.at[gy],
            device_id={"gx": gx, "gy": other},
            device_id_type=MESH,
        )

    def from_row(other):
        return pltpu.make_async_remote_copy(
            src_ref=own_row,
            dst_ref=rows.at[other],
            send_sem=gsend.at[other],
            recv_sem=grecv.at[other],
            device_id={"gx": gx, "gy": other},
            device_id_type=MESH,
        )

    def send_row(step, carry):
        to_row(step).start()
        return carry

    lax.fori_loop(1, ny, send_row, 0)

    def take_row(step, carry):
        from_row(lax.rem(gy + step, ny)).wait_recv()
        return carry

    lax.fori_loop(1, ny, take_row, 0)
    rows[gy] = row
    entries = jnp.sum(rows[...], axis=0)
    block = inv.shape[1]
    values = jnp.broadcast_to(entries[:, :block], (8, block))
    product = lax.dot_general(
        values, inv[...], (((1,), (1,)), ((), ())), precision=lax.Precision.HIGHEST, preferred_element_type=F32
    )
    part_row[:, pl.ds(0, block)] = product[0:1]

    def to_part(other):
        return pltpu.make_async_remote_copy(
            src_ref=part_row,
            dst_ref=parts.at[gx],
            send_sem=psend.at[other],
            recv_sem=precv.at[gx],
            device_id={"gx": gy, "gy": other},
            device_id_type=MESH,
        )

    def from_part(other):
        return pltpu.make_async_remote_copy(
            src_ref=part_row,
            dst_ref=parts.at[other],
            send_sem=psend.at[other],
            recv_sem=precv.at[other],
            device_id={"gx": other, "gy": gx},
            device_id_type=MESH,
        )

    def other_part(other):
        return jnp.logical_not(jnp.logical_and(other == gy, gx == gy))

    def send_part(step, carry):
        other = lax.rem(gy + step, ny)

        @pl.when(other_part(other))
        def _():
            to_part(other).start()

        return carry

    lax.fori_loop(0, ny, send_part, 0)

    def take_part(step, carry):
        other = lax.rem(gx + step, nx)

        @pl.when(jnp.logical_not(jnp.logical_and(other == gx, gx == gy)))
        def _():
            from_part(other).wait_recv()

        return carry

    lax.fori_loop(0, nx, take_part, 0)

    @pl.when(gx == gy)
    def _():
        parts[gx] = part_row[...]

    coarsest = jnp.sum(parts[...], axis=0)

    for piece in range(5):
        size = 8 if piece < 4 else 4
        at = pl.ds(8 * piece, size)
        _, c = rows_of(piece, size)
        spread = [
            jnp.sum(jnp.where(lane == 12 * gy + 2 * c + a, coarsest, 0.0), axis=1, keepdims=True)
            for a in range(2)
        ]
        cacc[at, :] = ctn[at, :] * jnp.where(upper, spread[1], spread[0])
    ext[1, :, pl.ds(0, A1)] = ext[0, :, pl.ds(0, A1)] + folded()
    send_coarse(1)
    coarse_apply(1)
    solved = ext[1, :, pl.ds(0, A1)]
    solved = solved + damping * (crhs[...] - (cst8 * solved + folded())) / cst8
    y2[...] = solved
    csol[...] = solved[0:6]

    def lift(x):
        tables = [y2[:, pl.ds(LANES * h, LANES)] for h in range(A1 // LANES)]
        for y in range(FY):
            for t in range(NZ // LANES):
                span = pl.ds(LANES * t, LANES)
                index = jnp.broadcast_to(mem[x, pl.ds(y, 1), span], (8, LANES))
                nodes[x, t, pl.ds(y, 8, stride=8), :] = pick(tables, index)
        values = []
        for i in range(3):
            value = 0.0
            for c in range(6):
                taken = jnp.concatenate(
                    [nodes[x, t, pl.ds(8 * c, 8), :] for t in range(NZ // LANES)], axis=1
                )
                value = value + ten[6 * i + c, x].astype(F32) * taken
            values.append(value)
        put_field(3, x, values)

    slabs(3, lift)

    def corrected(x):
        total = outside(3, x)
        put_field(
            4,
            x,
            [
                field[1, c, x + 1] + field[3, c, x + 1] - smoothing * total[c] * wgt[c, x]
                for c in range(3)
            ],
        )

    inside(3)
    wait_halo(3)
    slabs(4, corrected)

    inside(4)
    wait_halo(4)
    slabs(5, lambda x: put_field(5, x, smoothed(4, x)))

    def last(x):
        values = smoothed(5, x)
        for c in range(3):
            sol[c, x] = values[c]

    inside(5)
    wait_halo(5)
    slabs(None, last)

    for side in range(4):

        @pl.when(near[side][0])
        def _():
            for number in range(FIELDS):
                halo(number, side).wait_send()
            for number in range(2):
                coarse_halo(number, side ^ 1).wait_send()

    def sent_row(step, carry):
        to_row(step).wait_send()
        return carry

    lax.fori_loop(1, ny, sent_row, 0)

    def sent_part(step, carry):
        other = lax.rem(gy + step, ny)

        @pl.when(other_part(other))
        def _():
            to_part(other).wait_send()

        return carry

    lax.fori_loop(0, ny, sent_part, 0)


def body(nx, ny, rhs, stiffness, couplings, tentative, members, cst, ccp, col, snd, ctn, cmb, inv):
    couplings = couplings.reshape(63, FX, FY, NZ)
    tentative = tentative.reshape(18, FX, FY, NZ)
    cmb = cmb.reshape(1, A1)
    operands = (rhs, stiffness, couplings, tentative, members, cst, ccp, col, snd, ctn, cmb, inv)
    dma = pltpu.SemaphoreType.DMA
    scratch = [pltpu.VMEM(operand.shape, operand.dtype) for operand in operands]
    scratch += [
        pltpu.VMEM((3, FX, FY, NZ), F32),
        pltpu.VMEM((FIELDS, 3, FX + 2, FY, NZ), F32),
        pltpu.VMEM((FIELDS, 2, 3, FX, NZ), F32),
        pltpu.VMEM((FIELDS, 2, 3, FX, NZ), F32),
        pltpu.VMEM((3, FX, FY, NZ), F32),
        pltpu.VMEM((3, FX, FY, NZ), F32),
        pltpu.VMEM((FX, NZ // LANES, 8 * FY, LANES), F32),
        pltpu.VMEM((8, A1), F32),
        pltpu.VMEM((8, A1), F32),
        pltpu.VMEM((2, 8, A1 + 4 * H), F32),
        pltpu.VMEM((2, 4, 8, H), F32),
        pltpu.VMEM((40, A1), F32),
        pltpu.VMEM((1, 2 * LANES), F32),
        pltpu.VMEM((ny, 1, 2 * LANES), F32),
        pltpu.VMEM((1, 2 * LANES), F32),
        pltpu.VMEM((nx, 1, 2 * LANES), F32),
        dma((18,)),
        dma((FIELDS, 4)),
        dma((FIELDS, 4)),
        dma((2, 4)),
        dma((2, 4)),
        dma((ny,)),
        dma((ny,)),
        dma((ny,)),
        dma((nx,)),
    ]
    return pl.pallas_call(
        functools.partial(kernel, nx, ny),
        out_shape=(
            jax.ShapeDtypeStruct((3, FX, FY, NZ), F32),
            jax.ShapeDtypeStruct((6, A1), F32),
        ),
        in_specs=[pl.BlockSpec(memory_space=pl.ANY)] * len(operands),
        out_specs=(pl.BlockSpec(memory_space=pltpu.VMEM),) * 2,
        scratch_shapes=scratch,
        compiler_params=pltpu.CompilerParams(
            collective_id=0, has_side_effects=True, vmem_limit_bytes=60 * 1024 * 1024
        ),
    )(*operands)


def solution(mesh):
    placed = (
        P(None, "gx", "gy", None),
        P(None, "gx", "gy", None),
        P(None, None, None, "gx", "gy", None),
        P(None, None, "gx", "gy", None),
        P("gx", "gy", None),
        P(None, ("gx", "gy")),
        P(None, None, ("gx", "gy")),
        P(None, ("gx", "gy")),
        P(None, ("gx", "gy")),
        P(None, ("gx", "gy")),
        P(("gx", "gy")),
        P("gy", "gx"),
    )
    return jax.shard_map(
        functools.partial(body, mesh.shape["gx"], mesh.shape["gy"]),
        mesh=mesh,
        in_specs=placed,
        out_specs=(P(None, "gx", "gy", None), P(None, ("gx", "gy"))),
        check_vma=False,
    )
```

```python
import functools

import jax
import jax.numpy as jnp
from jax import lax
from jax.experimental import pallas as pl
from jax.experimental.pallas import tpu as pltpu
from jax.sharding import PartitionSpec as P

MESH = pl.DeviceIdType.MESH
F32 = jnp.float32
BF16 = jnp.bfloat16

FX = 8
FY = 8
NZ = 512
K = 27
A1 = 1024
H = 256
LANES = 128
GROUP = 256
WIDE = 2
FIELDS = 6

damping = 0.6
smoothing = 0.5


def lane_gather(table, index):
    dims = lax.GatherDimensionNumbers(
        offset_dims=(),
        collapsed_slice_dims=(1,),
        start_index_map=(1,),
        operand_batching_dims=(0,),
        start_indices_batching_dims=(0,),
    )
    return lax.gather(
        table, index[..., None], dims, slice_sizes=(1, 1), mode=lax.GatherScatterMode.PROMISE_IN_BOUNDS
    )


def pick(tables, index):
    low = index & (LANES - 1)
    parts = [lane_gather(table, low) for table in tables]
    bit = LANES
    while len(parts) > 1:
        upper = (index & bit) != 0
        parts = [jnp.where(upper, parts[at + 1], parts[at]) for at in range(0, len(parts), 2)]
        bit *= 2
    return parts[0]


def rows_of(piece, rows):
    sub = lax.broadcasted_iota(jnp.int32, (rows, 1), 0)
    first, last = (8 * piece) // 6, min((8 * piece + 7) // 6, 5)
    i = jnp.where(sub < 6 * (first + 1) - 8 * piece, first, last)
    return i, 8 * piece + sub - 6 * i


def kernel(
    nx,
    ny,
    rhs_h,
    stf_h,
    cpl_h,
    ten_h,
    mem_h,
    cst_h,
    ccp_h,
    col_h,
    snd_h,
    ctn_h,
    cmb_h,
    inv_h,
    sol_h,
    csol_h,
    rhs,
    stf,
    cpl,
    ten,
    mem,
    cst,
    ccp,
    col,
    snd,
    ctn,
    cmb,
    inv,
    wgt,
    field,
    yout,
    yin,
    hout,
    hin,
    wout,
    win,
    acc,
    resid,
    nodes,
    crhs,
    y2,
    ext,
    cout,
    cacc,
    sol,
    csol,
    ohm,
    ohc,
    own_row,
    rows,
    part_row,
    parts,
    load_sem,
    out_sem,
    fsend,
    frecv,
    csend,
    crecv,
    gsend,
    grecv,
    psend,
    precv,
):
    gx, gy = lax.axis_index("gx"), lax.axis_index("gy")
    near = (
        (gx > 0, {"gx": jnp.maximum(gx - 1, 0), "gy": gy}),
        (gx < nx - 1, {"gx": jnp.minimum(gx + 1, nx - 1), "gy": gy}),
        (gy > 0, {"gx": gx, "gy": jnp.maximum(gy - 1, 0)}),
        (gy < ny - 1, {"gx": gx, "gy": jnp.minimum(gy + 1, ny - 1)}),
    )

    loads = {}
    pairs = [("rhs", rhs_h, rhs), ("stf", stf_h, stf), ("mem", mem_h, mem)]
    for offset in (0, 5, 6, 1, 2, 3, 4):
        pairs.append(("cpl%d" % offset, cpl_h.at[pl.ds(9 * offset, 9)], cpl.at[pl.ds(9 * offset, 9)]))
    pairs += [
        ("col", col_h, col),
        ("ten", ten_h, ten),
        ("cst", cst_h, cst),
        ("snd", snd_h, snd),
        ("ccp", ccp_h, ccp),
        ("ctn", ctn_h, ctn),
        ("cmb", cmb_h, cmb),
        ("inv", inv_h, inv),
    ]
    for number, (name, source, target) in enumerate(pairs):
        loads[name] = pltpu.make_async_copy(source, target, load_sem.at[number])
        loads[name].start()

    barrier = pltpu.get_barrier_semaphore()
    for there, device in near:

        @pl.when(there)
        def _():
            pl.semaphore_signal(barrier, inc=1, device_id=device, device_id_type=MESH)

    def greet(step, carry):
        other = lax.rem(gy + step, ny)
        pl.semaphore_signal(barrier, inc=1, device_id={"gx": gx, "gy": other}, device_id_type=MESH)
        return carry

    lax.fori_loop(1, ny, greet, 0)

    def greet_sender(step, carry):
        other = lax.rem(gx + step, nx)

        @pl.when(jnp.logical_not(jnp.logical_and(other == gx, gx == gy)))
        def _():
            pl.semaphore_signal(barrier, inc=1, device_id={"gx": other, "gy": gx}, device_id_type=MESH)

        return carry

    lax.fori_loop(0, nx, greet_sender, 0)

    def layer_out(number, side):
        return wout.at[number, side] if number < WIDE else hout.at[number - WIDE, side]

    def layer_in(number, side):
        return win.at[number, side] if number < WIDE else hin.at[number - WIDE, side]

    for side, (there, _) in enumerate(near):

        @pl.when(jnp.logical_not(there))
        def _():
            for number in range(FIELDS):
                target = layer_in(number, side)
                target[...] = jnp.zeros(target.shape, target.dtype)
            for number in range(2):
                ext[number, :, pl.ds(A1 + H * side, H)] = jnp.zeros((8, H), F32)

    cacc[pl.ds(32, 8), :] = jnp.zeros((8, A1), F32)
    own_row[...] = jnp.zeros_like(own_row)
    part_row[...] = jnp.zeros_like(part_row)

    def halo(number, side):
        return pltpu.make_async_remote_copy(
            src_ref=layer_out(number, side),
            dst_ref=layer_in(number, side ^ 1),
            send_sem=fsend.at[number, side],
            recv_sem=frecv.at[number, side ^ 1],
            device_id=near[side][1],
            device_id_type=MESH,
        )

    def pack(number, side, c, value):
        target = layer_out(number, side)
        target[c] = jnp.concatenate([value[:, : NZ // 2], value[:, NZ // 2 :]], axis=0).astype(target.dtype)

    def received(number, side, j):
        value = layer_in(number, side)[j].astype(F32)
        return jnp.concatenate([value[:8], value[8:]], axis=1)

    def send_halo(number, side):
        @pl.when(near[side][0])
        def _():
            halo(number, side).start()

    def wait_halo(number):
        for side in range(4):

            @pl.when(near[side][0])
            def _():
                halo(number, side ^ 1).wait_recv()

        for side in range(2):
            for j in range(3):
                yin[side, j] = received(number, side + 2, j)

    def put_field(number, x, values):
        for c in range(3):
            field[number, c, x] = values[c]
            yout[0, c, pl.ds(x, 1), :] = values[c][0:1, :]
            yout[1, c, pl.ds(x, 1), :] = values[c][FY - 1 : FY, :]
            if isinstance(x, int) and x == 0:
                pack(number, 0, c, values[c])
            if isinstance(x, int) and x == FX - 1:
                pack(number, 1, c, values[c])

    def slabs(number, slab):
        slab(0)
        if number is not None:
            send_halo(number, 0)
        slab(FX - 1)
        if number is not None:
            send_halo(number, 1)

        def inner(x, carry):
            slab(x)
            return carry

        lax.fori_loop(1, FX - 1, inner, 0)
        if number is not None:
            for side in range(2):
                for c in range(3):
                    pack(number, side + 2, c, yout[side, c])
                send_halo(number, side + 2)

    def add(total, offset, x, j, view):
        for i in range(3):
            total[i] = total[i] + cpl[9 * offset + 3 * i + j, x].astype(F32) * view

    def inside(number):
        lane = lax.broadcasted_iota(jnp.int32, (FY, NZ), 1)

        def slab(x):
            total = [stf[i, x] * field[number, i, x] for i in range(3)]
            for j in range(3):
                view = field[number, j, x]
                add(total, 0, x, j, view)
                add(total, 5, x, j, jnp.where(lane == 0, 0.0, pltpu.roll(view, 1, axis=1)))
                add(total, 6, x, j, jnp.where(lane == NZ - 1, 0.0, pltpu.roll(view, NZ - 1, axis=1)))
                if not (isinstance(x, int) and x == 0):
                    add(total, 1, x, j, field[number, j, x - 1])
                if not (isinstance(x, int) and x == FX - 1):
                    add(total, 2, x, j, field[number, j, x + 1])
            for i in range(3):
                acc[i, x] = total[i]

        slabs(None, slab)

    def outside(number, x):
        row = lax.broadcasted_iota(jnp.int32, (FY, NZ), 0)
        total = [acc[i, x] for i in range(3)]
        for j in range(3):
            view = field[number, j, x]
            below = yin[0, j, pl.ds(x, 1), :]
            above = yin[1, j, pl.ds(x, 1), :]
            add(total, 3, x, j, jnp.where(row == 0, below, pltpu.roll(view, 1, axis=0)))
            add(total, 4, x, j, jnp.where(row == FY - 1, above, pltpu.roll(view, FY - 1, axis=0)))
            if isinstance(x, int) and x == 0:
                add(total, 1, x, j, received(number, 0, j))
            if isinstance(x, int) and x == FX - 1:
                add(total, 2, x, j, received(number, 1, j))
        return total

    loads["rhs"].wait()
    loads["stf"].wait()

    def first(x):
        values = []
        for c in range(3):
            weight = 1.0 / stf[c, x]
            wgt[c, x] = weight
            values.append(damping * rhs[c, x] * weight)
        put_field(0, x, values)

    others = (
        sum(there.astype(jnp.int32) for there, _ in near) + (ny - 1) + nx - (gx == gy).astype(jnp.int32)
    )
    pl.semaphore_wait(barrier, others)
    slabs(0, first)

    count = lax.broadcasted_iota(jnp.int32, (16, NZ), 0).astype(F32).astype(BF16)

    def one_hot(index):
        width = index.shape[1]
        low = jnp.broadcast_to(index & (LANES - 1), (16, width)).astype(F32).astype(BF16)
        one, zero = jnp.ones((16, width), BF16), jnp.zeros((16, width), BF16)
        return jnp.concatenate(
            [jnp.where(low == count[:, :width] + float(16 * k), one, zero) for k in range(8)], axis=0
        )

    def hot_members(x, carry):
        for y in range(FY):
            ohm[x, :, pl.ds(NZ * y, NZ)] = one_hot(mem[x, pl.ds(y, 1), :])
        return carry

    def hot_columns(t, carry):
        span = pl.ds(pl.multiple_of(GROUP * t, GROUP), GROUP)
        columns = col[:, span]
        for k in range(K):
            ohc[k, :, span] = one_hot(columns[k : k + 1])
        return carry

    def choose(parts, index):
        bit = LANES
        while len(parts) > 1:
            upper = (index & bit) != 0
            parts = [jnp.where(upper, parts[at + 1], parts[at]) for at in range(0, len(parts), 2)]
            bit *= 2
        return parts[0]

    def table(values):
        pieces = [values[:, LANES * h : LANES * (h + 1)] for h in range(values.shape[1] // LANES)]
        value = jnp.concatenate(pieces, axis=0)
        rounded = value.astype(BF16).astype(F32)
        return jnp.concatenate([rounded, value - rounded], axis=1).astype(BF16)

    def look_up(entries, hot, index):
        product = jnp.dot(entries, jnp.concatenate([hot, hot], axis=0), preferred_element_type=F32)
        pieces = [product[8 * h : 8 * h + 8] for h in range(product.shape[0] // 8)]
        return choose(pieces, jnp.broadcast_to(index, (8, index.shape[1])))

    loads["mem"].wait()
    lax.fori_loop(0, FX, hot_members, 0)

    for offset in (0, 5, 6, 1, 2, 3, 4):
        loads["cpl%d" % offset].wait()

    def smoothed(number, x):
        total = outside(number, x)
        return [
            field[number, c, x] + damping * (rhs[c, x] - total[c]) * wgt[c, x] for c in range(3)
        ]

    inside(0)
    wait_halo(0)
    slabs(1, lambda x: put_field(1, x, smoothed(0, x)))

    def residual(x):
        total = outside(1, x)
        values = []
        for c in range(3):
            left = rhs[c, x] - total[c]
            resid[c, x] = left
            values.append(left * wgt[c, x])
        put_field(2, x, values)

    loads["col"].wait()
    lax.fori_loop(0, A1 // GROUP, hot_columns, 0)
    inside(1)
    wait_halo(1)
    slabs(2, residual)

    loads["ten"].wait()

    def restrict(x):
        total = outside(2, x)
        filtered = [resid[i, x] - smoothing * total[i] for i in range(3)]
        for c in range(6):
            value = ten[c, x].astype(F32) * filtered[0]
            for i in range(1, 3):
                value = value + ten[6 * i + c, x].astype(F32) * filtered[i]
            for t in range(NZ // LANES):
                part = value[:, LANES * t : LANES * (t + 1)]
                nodes[x, t, pl.ds(8 * c, 8), :] = part
                if c < 2:
                    nodes[x, t, pl.ds(8 * (c + 6), 8), :] = part

    inside(2)
    wait_halo(2)
    slabs(None, restrict)

    def sums(x, total):
        for y in range(FY):
            value = jnp.concatenate(
                [nodes[x, t, pl.ds(y, 8, stride=8), :] for t in range(NZ // LANES)], axis=1
            )
            rounded = value.astype(BF16).astype(F32)
            both = jnp.concatenate([rounded, value - rounded], axis=0).astype(BF16)
            index = jnp.broadcast_to(mem[x, pl.ds(y, 1), :], (16, NZ))
            high = lax.shift_right_logical(index, 7).astype(F32).astype(BF16)
            zero = jnp.zeros((16, NZ), BF16)
            left = jnp.concatenate([jnp.where(high == float(h), both, zero) for h in range(8)], axis=0)
            right = ohm[x, :, pl.ds(NZ * y, NZ)]
            total = total + lax.dot_general(
                left, right, (((1,), (1,)), ((), ())), preferred_element_type=F32
            )
        return total

    gathered = lax.fori_loop(0, FX, sums, jnp.zeros((LANES, LANES), F32))

    loads["cst"].wait()
    loads["snd"].wait()
    for h in range(8):
        span = pl.ds(LANES * h, LANES)
        crhs[:, span] = gathered[16 * h : 16 * h + 8] + gathered[16 * h + 8 : 16 * h + 16]
    cst8 = jnp.concatenate([cst[...], cst[0:2, :]], axis=0)
    ext[0, :, pl.ds(0, A1)] = damping * crhs[...] / cst8

    def coarse_halo(number, side):
        return pltpu.make_async_remote_copy(
            src_ref=cout.at[number, side],
            dst_ref=ext.at[number, :, pl.ds(A1 + H * side, H)],
            send_sem=csend.at[number, side],
            recv_sem=crecv.at[number, side],
            device_id=near[side ^ 1][1],
            device_id_type=MESH,
        )

    def send_coarse(number):
        tables = [ext[number, :, pl.ds(LANES * h, LANES)] for h in range(A1 // LANES)]
        for side in range(4):
            for t in range(H // LANES):
                index = jnp.broadcast_to(snd[side : side + 1, pl.ds(LANES * t, LANES)], (8, LANES))
                cout[number, side, :, pl.ds(LANES * t, LANES)] = pick(tables, index)

            @pl.when(near[side ^ 1][0])
            def _():
                coarse_halo(number, side).start()

    sub = lax.broadcasted_iota(jnp.int32, (8, GROUP), 0)

    def coarse_apply(number):
        for side in range(4):

            @pl.when(near[side][0])
            def _():
                coarse_halo(number, side).wait_recv()

        entries = table(ext[number])

        def group(t, carry):
            span = pl.ds(pl.multiple_of(GROUP * t, GROUP), GROUP)
            total = [jnp.zeros((8 if piece < 4 else 4, GROUP), F32) for piece in range(5)]
            columns = col[:, span]
            for k in range(K):
                base = look_up(entries, ohc[k, :, span], columns[k : k + 1])
                up2, by4, down2 = (pltpu.roll(base, by, axis=0) for by in (6, 4, 2))
                turned = (base, jnp.where(sub < 6, up2, by4), jnp.where(sub < 2, by4, down2))
                for piece in range(5):
                    size = 8 if piece < 4 else 4
                    block = ccp[k, pl.ds(8 * piece, size), span]
                    total[piece] = total[piece] + block * turned[piece % 3][:size]
            for piece in range(5):
                cacc[pl.ds(8 * piece, 8 if piece < 4 else 4), span] = total[piece]
            return carry

        lax.fori_loop(0, A1 // GROUP, group, 0)

    fold_row = lax.broadcasted_iota(jnp.int32, (8, 40), 0)
    fold_col = lax.broadcasted_iota(jnp.int32, (8, 40), 1)
    fold_row = jnp.where(fold_row < 6, fold_row, fold_row - 6)
    fold = jnp.logical_and(fold_col >= 6 * fold_row, fold_col < 6 * fold_row + 6).astype(F32)

    def folded():
        return jnp.dot(fold, cacc[...], precision=lax.Precision.HIGHEST, preferred_element_type=F32)

    send_coarse(0)
    loads["ccp"].wait()
    coarse_apply(0)
    s1 = crhs[...] - (cst8 * ext[0, :, pl.ds(0, A1)] + folded())

    loads["ctn"].wait()
    loads["cmb"].wait()
    loads["inv"].wait()
    lane = lax.broadcasted_iota(jnp.int32, (1, 2 * LANES), 1)
    upper = cmb[...] != 0
    row = jnp.zeros((1, 2 * LANES), F32)
    for piece in range(5):
        size = 8 if piece < 4 else 4
        i, c = rows_of(piece, size)
        first_i, last_i = (8 * piece) // 6, min((8 * piece + 7) // 6, 5)
        matching = jnp.where(i == first_i, s1[first_i : first_i + 1], s1[last_i : last_i + 1])
        product = ctn[pl.ds(8 * piece, size), :] * matching
        for a in range(2):
            kept = jnp.where(upper, product, 0.0) if a else jnp.where(upper, 0.0, product)
            total = jnp.sum(kept, axis=1, keepdims=True)
            place = 12 * gy + 2 * c + a
            row = row + jnp.sum(jnp.where(lane == place, total, 0.0), axis=0, keepdims=True)
    own_row[...] = row

    def to_row(step):
        other = lax.rem(gy + step, ny)
        return pltpu.make_async_remote_copy(
            src_ref=own_row,
            dst_ref=rows.at[gy],
            send_sem=gsend.at[other],
            recv_sem=grecv.at[gy],
            device_id={"gx": gx, "gy": other},
            device_id_type=MESH,
        )

    def from_row(other):
        return pltpu.make_async_remote_copy(
            src_ref=own_row,
            dst_ref=rows.at[other],
            send_sem=gsend.at[other],
            recv_sem=grecv.at[other],
            device_id={"gx": gx, "gy": other},
            device_id_type=MESH,
        )

    def send_row(step, carry):
        to_row(step).start()
        return carry

    lax.fori_loop(1, ny, send_row, 0)

    def take_row(step, carry):
        from_row(lax.rem(gy + step, ny)).wait_recv()
        return carry

    lax.fori_loop(1, ny, take_row, 0)
    rows[gy] = row
    entries = jnp.sum(rows[...], axis=0)
    block = inv.shape[1]
    values = jnp.broadcast_to(entries[:, :block], (8, block))
    product = lax.dot_general(
        values, inv[...], (((1,), (1,)), ((), ())), precision=lax.Precision.HIGHEST, preferred_element_type=F32
    )
    part_row[:, pl.ds(0, block)] = product[0:1]

    def to_part(other):
        return pltpu.make_async_remote_copy(
            src_ref=part_row,
            dst_ref=parts.at[gx],
            send_sem=psend.at[other],
            recv_sem=precv.at[gx],
            device_id={"gx": gy, "gy": other},
            device_id_type=MESH,
        )

    def from_part(other):
        return pltpu.make_async_remote_copy(
            src_ref=part_row,
            dst_ref=parts.at[other],
            send_sem=psend.at[other],
            recv_sem=precv.at[other],
            device_id={"gx": other, "gy": gx},
            device_id_type=MESH,
        )

    def other_part(other):
        return jnp.logical_not(jnp.logical_and(other == gy, gx == gy))

    def send_part(step, carry):
        other = lax.rem(gy + step, ny)

        @pl.when(other_part(other))
        def _():
            to_part(other).start()

        return carry

    lax.fori_loop(0, ny, send_part, 0)

    def take_part(step, carry):
        other = lax.rem(gx + step, nx)

        @pl.when(jnp.logical_not(jnp.logical_and(other == gx, gx == gy)))
        def _():
            from_part(other).wait_recv()

        return carry

    lax.fori_loop(0, nx, take_part, 0)

    @pl.when(gx == gy)
    def _():
        parts[gx] = part_row[...]

    coarsest = jnp.sum(parts[...], axis=0)

    for piece in range(5):
        size = 8 if piece < 4 else 4
        at = pl.ds(8 * piece, size)
        _, c = rows_of(piece, size)
        spread = [
            jnp.sum(jnp.where(lane == 12 * gy + 2 * c + a, coarsest, 0.0), axis=1, keepdims=True)
            for a in range(2)
        ]
        cacc[at, :] = ctn[at, :] * jnp.where(upper, spread[1], spread[0])
    ext[1, :, pl.ds(0, A1)] = ext[0, :, pl.ds(0, A1)] + folded()
    send_coarse(1)
    coarse_apply(1)
    solved = ext[1, :, pl.ds(0, A1)]
    solved = solved + damping * (crhs[...] - (cst8 * solved + folded())) / cst8
    y2[...] = solved
    csol[...] = solved[0:6]
    csol_out = pltpu.make_async_copy(csol, csol_h, out_sem.at[FX])
    csol_out.start()

    entries = table(y2[...])

    def lift(x):
        for y in range(FY):
            taken = look_up(entries, ohm[x, :, pl.ds(NZ * y, NZ)], mem[x, pl.ds(y, 1), :])
            for t in range(NZ // LANES):
                nodes[x, t, pl.ds(y, 8, stride=8), :] = taken[:, LANES * t : LANES * (t + 1)]
        values = []
        for i in range(3):
            value = 0.0
            for c in range(6):
                taken = jnp.concatenate(
                    [nodes[x, t, pl.ds(8 * c, 8), :] for t in range(NZ // LANES)], axis=1
                )
                value = value + ten[6 * i + c, x].astype(F32) * taken
            values.append(value)
        put_field(3, x, values)

    slabs(3, lift)

    def corrected(x):
        total = outside(3, x)
        put_field(
            4,
            x,
            [
                field[1, c, x] + field[3, c, x] - smoothing * total[c] * wgt[c, x]
                for c in range(3)
            ],
        )

    inside(3)
    wait_halo(3)
    slabs(4, corrected)

    inside(4)
    wait_halo(4)
    slabs(5, lambda x: put_field(5, x, smoothed(4, x)))

    def last(x):
        values = smoothed(5, x)
        for c in range(3):
            sol[c, x] = values[c]
        sol_out(x).start()

    def sol_out(x):
        return pltpu.make_async_copy(sol.at[:, x], sol_h.at[:, x], out_sem.at[x])

    inside(5)
    wait_halo(5)
    slabs(None, last)

    for side in range(4):

        @pl.when(near[side][0])
        def _():
            for number in range(FIELDS):
                halo(number, side).wait_send()
            for number in range(2):
                coarse_halo(number, side ^ 1).wait_send()

    def sent_row(step, carry):
        to_row(step).wait_send()
        return carry

    lax.fori_loop(1, ny, sent_row, 0)

    def sent_part(step, carry):
        other = lax.rem(gy + step, ny)

        @pl.when(other_part(other))
        def _():
            to_part(other).wait_send()

        return carry

    lax.fori_loop(0, ny, sent_part, 0)
    for x in range(FX):
        sol_out(x).wait()
    csol_out.wait()


def write_out(sol, csol, sol_out, csol_out):
    sol_out[...] = sol[...]
    csol_out[...] = csol[...]


def body(nx, ny, rhs, stiffness, couplings, tentative, members, cst, ccp, col, snd, ctn, cmb, inv):
    couplings = couplings.reshape(63, FX, FY, NZ)
    tentative = tentative.reshape(18, FX, FY, NZ)
    cmb = cmb.reshape(1, A1)
    operands = (rhs, stiffness, couplings, tentative, members, cst, ccp, col, snd, ctn, cmb, inv)
    dma = pltpu.SemaphoreType.DMA
    scratch = [pltpu.VMEM(operand.shape, operand.dtype) for operand in operands]
    scratch += [
        pltpu.VMEM((3, FX, FY, NZ), F32),
        pltpu.VMEM((FIELDS, 3, FX, FY, NZ), F32),
        pltpu.VMEM((2, 3, FX, NZ), F32),
        pltpu.VMEM((2, 3, FX, NZ), F32),
        pltpu.VMEM((FIELDS - WIDE, 4, 3, 16, NZ // 2), BF16),
        pltpu.VMEM((FIELDS - WIDE, 4, 3, 16, NZ // 2), BF16),
        pltpu.VMEM((WIDE, 4, 3, 16, NZ // 2), F32),
        pltpu.VMEM((WIDE, 4, 3, 16, NZ // 2), F32),
        pltpu.VMEM((3, FX, FY, NZ), F32),
        pltpu.VMEM((3, FX, FY, NZ), F32),
        pltpu.VMEM((FX, NZ // LANES, 8 * FY, LANES), F32),
        pltpu.VMEM((8, A1), F32),
        pltpu.VMEM((8, A1), F32),
        pltpu.VMEM((2, 8, A1 + 4 * H), F32),
        pltpu.VMEM((2, 4, 8, H), F32),
        pltpu.VMEM((40, A1), F32),
        pltpu.VMEM((3, FX, FY, NZ), F32),
        pltpu.VMEM((6, A1), F32),
        pltpu.VMEM((FX, LANES, FY * NZ), BF16),
        pltpu.VMEM((K, LANES, A1), BF16),
        pltpu.VMEM((1, 2 * LANES), F32),
        pltpu.VMEM((ny, 1, 2 * LANES), F32),
        pltpu.VMEM((1, 2 * LANES), F32),
        pltpu.VMEM((nx, 1, 2 * LANES), F32),
        dma((18,)),
        dma((FX + 1,)),
        dma((FIELDS, 4)),
        dma((FIELDS, 4)),
        dma((2, 4)),
        dma((2, 4)),
        dma((ny,)),
        dma((ny,)),
        dma((ny,)),
        dma((nx,)),
    ]
    results = pl.pallas_call(
        functools.partial(kernel, nx, ny),
        out_shape=(
            jax.ShapeDtypeStruct((3, FX, FY, NZ), F32),
            jax.ShapeDtypeStruct((6, A1), F32),
        ),
        in_specs=[pl.BlockSpec(memory_space=pl.ANY)] * len(operands),
        out_specs=(pl.BlockSpec(memory_space=pl.ANY),) * 2,
        scratch_shapes=scratch,
        compiler_params=pltpu.CompilerParams(
            collective_id=0, has_side_effects=True, vmem_limit_bytes=56 * 1024 * 1024
        ),
    )(*operands)
    return pl.pallas_call(
        write_out,
        out_shape=tuple(jax.ShapeDtypeStruct(result.shape, result.dtype) for result in results),
        in_specs=[pl.BlockSpec(memory_space=pltpu.VMEM)] * 2,
        out_specs=(pl.BlockSpec(memory_space=pltpu.VMEM),) * 2,
        compiler_params=pltpu.CompilerParams(vmem_limit_bytes=60 * 1024 * 1024),
    )(*results)


def solution(mesh):
    placed = (
        P(None, "gx", "gy", None),
        P(None, "gx", "gy", None),
        P(None, None, None, "gx", "gy", None),
        P(None, None, "gx", "gy", None),
        P("gx", "gy", None),
        P(None, ("gx", "gy")),
        P(None, None, ("gx", "gy")),
        P(None, ("gx", "gy")),
        P(None, ("gx", "gy")),
        P(None, ("gx", "gy")),
        P(("gx", "gy")),
        P("gy", "gx"),
    )
    return jax.shard_map(
        functools.partial(body, mesh.shape["gx"], mesh.shape["gy"]),
        mesh=mesh,
        in_specs=placed,
        out_specs=(P(None, "gx", "gy", None), P(None, ("gx", "gy"))),
        check_vma=False,
    )
```

```python
import functools

import jax
import jax.numpy as jnp
from jax import lax
from jax.experimental import pallas as pl
from jax.experimental.pallas import tpu as pltpu
from jax.sharding import PartitionSpec as P

MESH = pl.DeviceIdType.MESH
F32 = jnp.float32
BF16 = jnp.bfloat16

FX = 8
FY = 8
NZ = 512
K = 27
A1 = 1024
H = 256
LANES = 128
GROUP = 512
HALF = 256
WIDE = 2
FIELDS = 6

damping = 0.6
smoothing = 0.5


def lane_gather(table, index):
    dims = lax.GatherDimensionNumbers(
        offset_dims=(),
        collapsed_slice_dims=(1,),
        start_index_map=(1,),
        operand_batching_dims=(0,),
        start_indices_batching_dims=(0,),
    )
    return lax.gather(
        table, index[..., None], dims, slice_sizes=(1, 1), mode=lax.GatherScatterMode.PROMISE_IN_BOUNDS
    )


def pick(tables, index):
    low = index & (LANES - 1)
    parts = [lane_gather(table, low) for table in tables]
    bit = LANES
    while len(parts) > 1:
        upper = (index & bit) != 0
        parts = [jnp.where(upper, parts[at + 1], parts[at]) for at in range(0, len(parts), 2)]
        bit *= 2
    return parts[0]


def rows_of(piece, rows):
    sub = lax.broadcasted_iota(jnp.int32, (rows, 1), 0)
    first, last = (8 * piece) // 6, min((8 * piece + 7) // 6, 5)
    i = jnp.where(sub < 6 * (first + 1) - 8 * piece, first, last)
    return i, 8 * piece + sub - 6 * i


def kernel(
    nx,
    ny,
    rhs_h,
    stf_h,
    cpl_h,
    ten_h,
    mem_h,
    cst_h,
    ccp_h,
    col_h,
    snd_h,
    ctn_h,
    cmb_h,
    inv_h,
    sol_h,
    csol_h,
    rhs,
    stf,
    cpl,
    ten,
    mem,
    cst,
    ccp,
    col,
    snd,
    ctn,
    cmb,
    inv,
    wgt,
    field,
    yout,
    yin,
    hout,
    hin,
    wout,
    win,
    acc,
    resid,
    nodes,
    crhs,
    y2,
    ext,
    cout,
    cacc,
    invs,
    sol,
    csol,
    ohm,
    ohc,
    own_row,
    rows,
    part_row,
    parts,
    wave,
    load_sem,
    out_sem,
    fsend,
    frecv,
    csend,
    crecv,
    gsend,
    grecv,
    psend,
    precv,
):
    gx, gy = lax.axis_index("gx"), lax.axis_index("gy")
    near = (
        (gx > 0, {"gx": jnp.maximum(gx - 1, 0), "gy": gy}),
        (gx < nx - 1, {"gx": jnp.minimum(gx + 1, nx - 1), "gy": gy}),
        (gy > 0, {"gx": gx, "gy": jnp.maximum(gy - 1, 0)}),
        (gy < ny - 1, {"gx": gx, "gy": jnp.minimum(gy + 1, ny - 1)}),
    )

    barrier = pltpu.get_barrier_semaphore()

    def tell(semaphore, steps):
        for device in (
            {"gx": lax.rem(gx + nx - steps, nx), "gy": gy},
            {"gx": lax.rem(gx + steps, nx), "gy": gy},
            {"gx": gx, "gy": lax.rem(gy + ny - steps, ny)},
            {"gx": gx, "gy": lax.rem(gy + steps, ny)},
        ):
            pl.semaphore_signal(semaphore, inc=1, device_id=device, device_id_type=MESH)

    def announce(number):
        if 2 << number < nx:
            tell(wave.at[number], 1 << number)

    def heard(number):
        if 2 << number < nx:
            pl.semaphore_wait(wave.at[number], 4)

    if nx > 1:
        tell(barrier, 1)

    loads = {}
    pairs = [("rhs", rhs_h, rhs), ("stf", stf_h, stf), ("mem", mem_h, mem)]
    for offset in (0, 5, 6, 1, 2, 3, 4):
        pairs.append(("cpl%d" % offset, cpl_h.at[pl.ds(9 * offset, 9)], cpl.at[pl.ds(9 * offset, 9)]))
    pairs += [
        ("col", col_h, col),
        ("ten", ten_h, ten),
        ("cst", cst_h, cst),
        ("snd", snd_h, snd),
        ("ccp", ccp_h, ccp),
        ("ctn", ctn_h, ctn),
        ("cmb", cmb_h, cmb),
        ("inv", inv_h, inv),
    ]
    for number, (name, source, target) in enumerate(pairs):
        loads[name] = pltpu.make_async_copy(source, target, load_sem.at[number])
        loads[name].start()

    def layer_out(number, side):
        return wout.at[number, side] if number < WIDE else hout.at[number - WIDE, side]

    def layer_in(number, side):
        return win.at[number, side] if number < WIDE else hin.at[number - WIDE, side]

    for side, (there, _) in enumerate(near):

        @pl.when(jnp.logical_not(there))
        def _():
            for number in range(FIELDS):
                target = layer_in(number, side)
                target[...] = jnp.zeros(target.shape, target.dtype)
            for number in range(2):
                ext[number, :, pl.ds(A1 + H * side, H)] = jnp.zeros((8, H), F32)

    cacc[pl.ds(32, 8), :] = jnp.zeros((8, A1), F32)
    own_row[...] = jnp.zeros_like(own_row)
    part_row[...] = jnp.zeros_like(part_row)

    def halo(number, side):
        return pltpu.make_async_remote_copy(
            src_ref=layer_out(number, side),
            dst_ref=layer_in(number, side ^ 1),
            send_sem=fsend.at[number, side],
            recv_sem=frecv.at[number, side ^ 1],
            device_id=near[side][1],
            device_id_type=MESH,
        )

    def pack(number, side, c, value):
        target = layer_out(number, side)
        target[c] = jnp.concatenate([value[:, : NZ // 2], value[:, NZ // 2 :]], axis=0).astype(target.dtype)

    def received(number, side, j):
        value = layer_in(number, side)[j].astype(F32)
        return jnp.concatenate([value[:8], value[8:]], axis=1)

    def send_halo(number, side):
        @pl.when(near[side][0])
        def _():
            halo(number, side).start()

    def wait_halo(number):
        for side in range(4):

            @pl.when(near[side][0])
            def _():
                halo(number, side ^ 1).wait_recv()

        for side in range(2):
            for j in range(3):
                yin[side, j] = received(number, side + 2, j)

    def put_field(number, x, values):
        for c in range(3):
            field[number, c, x] = values[c]
            yout[0, c, pl.ds(x, 1), :] = values[c][0:1, :]
            yout[1, c, pl.ds(x, 1), :] = values[c][FY - 1 : FY, :]
            if isinstance(x, int) and x == 0:
                pack(number, 0, c, values[c])
            if isinstance(x, int) and x == FX - 1:
                pack(number, 1, c, values[c])

    def slabs(number, slab):
        slab(0)
        if number is not None:
            send_halo(number, 0)
        slab(FX - 1)
        if number is not None:
            send_halo(number, 1)

        def inner(x, carry):
            slab(x)
            return carry

        lax.fori_loop(1, FX - 1, inner, 0)
        if number is not None:
            for side in range(2):
                for c in range(3):
                    pack(number, side + 2, c, yout[side, c])
                send_halo(number, side + 2)

    def add(total, offset, x, j, view):
        for i in range(3):
            total[i] = total[i] + cpl[9 * offset + 3 * i + j, x].astype(F32) * view

    def inside(number):
        lane = lax.broadcasted_iota(jnp.int32, (FY, NZ), 1)

        def slab(x):
            total = [stf[i, x] * field[number, i, x] for i in range(3)]
            for j in range(3):
                view = field[number, j, x]
                add(total, 0, x, j, view)
                add(total, 5, x, j, jnp.where(lane == 0, 0.0, pltpu.roll(view, 1, axis=1)))
                add(total, 6, x, j, jnp.where(lane == NZ - 1, 0.0, pltpu.roll(view, NZ - 1, axis=1)))
                if not (isinstance(x, int) and x == 0):
                    add(total, 1, x, j, field[number, j, x - 1])
                if not (isinstance(x, int) and x == FX - 1):
                    add(total, 2, x, j, field[number, j, x + 1])
            for i in range(3):
                acc[i, x] = total[i]

        slabs(None, slab)

    def outside(number, x):
        row = lax.broadcasted_iota(jnp.int32, (FY, NZ), 0)
        total = [acc[i, x] for i in range(3)]
        for j in range(3):
            view = field[number, j, x]
            below = yin[0, j, pl.ds(x, 1), :]
            above = yin[1, j, pl.ds(x, 1), :]
            add(total, 3, x, j, jnp.where(row == 0, below, pltpu.roll(view, 1, axis=0)))
            add(total, 4, x, j, jnp.where(row == FY - 1, above, pltpu.roll(view, FY - 1, axis=0)))
            if isinstance(x, int) and x == 0:
                add(total, 1, x, j, received(number, 0, j))
            if isinstance(x, int) and x == FX - 1:
                add(total, 2, x, j, received(number, 1, j))
        return total

    loads["rhs"].wait()
    loads["stf"].wait()

    def first(x):
        values = []
        for c in range(3):
            weight = 1.0 / stf[c, x]
            wgt[c, x] = weight
            values.append(damping * rhs[c, x] * weight)
        put_field(0, x, values)

    if nx > 1:
        pl.semaphore_wait(barrier, 4)
    announce(0)
    slabs(0, first)

    count = lax.broadcasted_iota(jnp.int32, (16, NZ), 0).astype(F32).astype(BF16)

    def one_hot(index):
        width = index.shape[1]
        low = jnp.broadcast_to(index & (LANES - 1), (16, width)).astype(F32).astype(BF16)
        one, zero = jnp.ones((16, width), BF16), jnp.zeros((16, width), BF16)
        return jnp.concatenate(
            [jnp.where(low == count[:, :width] + float(16 * k), one, zero) for k in range(8)], axis=0
        )

    def hot_members(x, carry):
        for y in range(FY):
            ohm[x, :, pl.ds(NZ * y, NZ)] = one_hot(mem[x, pl.ds(y, 1), :])
        return carry

    def hot_columns(t, carry):
        span = pl.ds(pl.multiple_of(GROUP * t, GROUP), GROUP)
        columns = col[:, span]
        for k in range(K):
            ohc[k, :, span] = one_hot(columns[k : k + 1])
        return carry

    def choose(parts, index):
        bit = LANES
        while len(parts) > 1:
            upper = (index & bit) != 0
            parts = [jnp.where(upper, parts[at + 1], parts[at]) for at in range(0, len(parts), 2)]
            bit *= 2
        return parts[0]

    def table(values):
        pieces = [values[:, LANES * h : LANES * (h + 1)] for h in range(values.shape[1] // LANES)]
        value = jnp.concatenate(pieces, axis=0)
        rounded = value.astype(BF16).astype(F32)
        return jnp.concatenate([rounded, value - rounded], axis=1).astype(BF16)

    def look_up(entries, hot, index):
        product = jnp.dot(entries, jnp.concatenate([hot, hot], axis=0), preferred_element_type=F32)
        pieces = [product[8 * h : 8 * h + 8] for h in range(product.shape[0] // 8)]
        return choose(pieces, jnp.broadcast_to(index, (8, index.shape[1])))

    loads["mem"].wait()
    lax.fori_loop(0, FX, hot_members, 0)

    for offset in (0, 5, 6, 1, 2, 3, 4):
        loads["cpl%d" % offset].wait()

    def smoothed(number, x):
        total = outside(number, x)
        return [
            field[number, c, x] + damping * (rhs[c, x] - total[c]) * wgt[c, x] for c in range(3)
        ]

    inside(0)
    heard(0)
    announce(1)
    wait_halo(0)
    slabs(1, lambda x: put_field(1, x, smoothed(0, x)))

    def residual(x):
        total = outside(1, x)
        values = []
        for c in range(3):
            left = rhs[c, x] - total[c]
            resid[c, x] = left
            values.append(left * wgt[c, x])
        put_field(2, x, values)

    inside(1)
    heard(1)
    announce(2)
    wait_halo(1)
    slabs(2, residual)

    loads["ten"].wait()

    def restrict(x):
        total = outside(2, x)
        filtered = [resid[i, x] - smoothing * total[i] for i in range(3)]
        for c in range(6):
            value = ten[c, x].astype(F32) * filtered[0]
            for i in range(1, 3):
                value = value + ten[6 * i + c, x].astype(F32) * filtered[i]
            for t in range(NZ // LANES):
                part = value[:, LANES * t : LANES * (t + 1)]
                nodes[x, t, pl.ds(8 * c, 8), :] = part
                if c < 2:
                    nodes[x, t, pl.ds(8 * (c + 6), 8), :] = part

    loads["inv"].wait()
    whole = inv[...]
    rounded = whole.astype(BF16)
    invs[0] = rounded
    invs[1] = (whole - rounded.astype(F32)).astype(BF16)
    inside(2)
    heard(2)
    wait_halo(2)
    slabs(None, restrict)

    def sums(x, total):
        for y in range(FY):
            value = jnp.concatenate(
                [nodes[x, t, pl.ds(y, 8, stride=8), :] for t in range(NZ // LANES)], axis=1
            )
            rounded = value.astype(BF16).astype(F32)
            both = jnp.concatenate([rounded, value - rounded], axis=0).astype(BF16)
            index = jnp.broadcast_to(mem[x, pl.ds(y, 1), :], (16, NZ))
            high = lax.shift_right_logical(index, 7).astype(F32).astype(BF16)
            zero = jnp.zeros((16, NZ), BF16)
            left = jnp.concatenate([jnp.where(high == float(h), both, zero) for h in range(8)], axis=0)
            right = ohm[x, :, pl.ds(NZ * y, NZ)]
            total = total + lax.dot_general(
                left, right, (((1,), (1,)), ((), ())), preferred_element_type=F32
            )
        return total

    gathered = lax.fori_loop(0, FX, sums, jnp.zeros((LANES, LANES), F32))

    loads["cst"].wait()
    loads["snd"].wait()
    for h in range(8):
        span = pl.ds(LANES * h, LANES)
        crhs[:, span] = gathered[16 * h : 16 * h + 8] + gathered[16 * h + 8 : 16 * h + 16]
    cst8 = jnp.concatenate([cst[...], cst[0:2, :]], axis=0)
    ext[0, :, pl.ds(0, A1)] = damping * crhs[...] / cst8

    def coarse_halo(number, side):
        return pltpu.make_async_remote_copy(
            src_ref=cout.at[number, side],
            dst_ref=ext.at[number, :, pl.ds(A1 + H * side, H)],
            send_sem=csend.at[number, side],
            recv_sem=crecv.at[number, side],
            device_id=near[side ^ 1][1],
            device_id_type=MESH,
        )

    def send_coarse(number):
        tables = [ext[number, :, pl.ds(LANES * h, LANES)] for h in range(A1 // LANES)]
        for side in range(4):
            for t in range(H // LANES):
                index = jnp.broadcast_to(snd[side : side + 1, pl.ds(LANES * t, LANES)], (8, LANES))
                cout[number, side, :, pl.ds(LANES * t, LANES)] = pick(tables, index)

            @pl.when(near[side ^ 1][0])
            def _():
                coarse_halo(number, side).start()

    sub = lax.broadcasted_iota(jnp.int32, (8, GROUP), 0)

    def coarse_apply(number):
        for side in range(4):

            @pl.when(near[side][0])
            def _():
                coarse_halo(number, side).wait_recv()

        entries = table(ext[number])

        def group(t, carry):
            span = pl.ds(pl.multiple_of(GROUP * t, GROUP), GROUP)
            total = [jnp.zeros((8 if piece < 4 else 4, GROUP), F32) for piece in range(5)]
            columns = col[:, span]
            for k in range(K):
                base = look_up(entries, ohc[k, :, span], columns[k : k + 1])
                up2, by4, down2 = (pltpu.roll(base, by, axis=0) for by in (6, 4, 2))
                turned = (base, jnp.where(sub < 6, up2, by4), jnp.where(sub < 2, by4, down2))
                for piece in range(5):
                    size = 8 if piece < 4 else 4
                    block = ccp[k, pl.ds(8 * piece, size), span]
                    total[piece] = total[piece] + block * turned[piece % 3][:size]
            for piece in range(5):
                cacc[pl.ds(8 * piece, 8 if piece < 4 else 4), span] = total[piece]
            return carry

        lax.fori_loop(0, A1 // GROUP, group, 0)

    fold_row = lax.broadcasted_iota(jnp.int32, (8, 40), 0)
    fold_col = lax.broadcasted_iota(jnp.int32, (8, 40), 1)
    fold_row = jnp.where(fold_row < 6, fold_row, fold_row - 6)
    fold = jnp.logical_and(fold_col >= 6 * fold_row, fold_col < 6 * fold_row + 6).astype(F32)

    def folded():
        return jnp.dot(fold, cacc[...], precision=lax.Precision.HIGHEST, preferred_element_type=F32)

    send_coarse(0)
    loads["col"].wait()
    lax.fori_loop(0, A1 // GROUP, hot_columns, 0)
    loads["ccp"].wait()
    coarse_apply(0)
    s1 = crhs[...] - (cst8 * ext[0, :, pl.ds(0, A1)] + folded())

    loads["ctn"].wait()
    loads["cmb"].wait()
    lane = lax.broadcasted_iota(jnp.int32, (1, 2 * LANES), 1)
    upper = cmb[...] != 0
    row = jnp.zeros((1, 2 * LANES), F32)
    for piece in range(5):
        size = 8 if piece < 4 else 4
        i, c = rows_of(piece, size)
        first_i, last_i = (8 * piece) // 6, min((8 * piece + 7) // 6, 5)
        matching = jnp.where(i == first_i, s1[first_i : first_i + 1], s1[last_i : last_i + 1])
        product = ctn[pl.ds(8 * piece, size), :] * matching
        for a in range(2):
            kept = jnp.where(upper, product, 0.0) if a else jnp.where(upper, 0.0, product)
            total = jnp.sum(kept, axis=1, keepdims=True)
            place = 12 * gy + 2 * c + a
            row = row + jnp.sum(jnp.where(lane == place, total, 0.0), axis=0, keepdims=True)
    own_row[...] = row

    def to_row(step):
        other = lax.rem(gy + step, ny)
        return pltpu.make_async_remote_copy(
            src_ref=own_row,
            dst_ref=rows.at[gy],
            send_sem=gsend.at[other],
            recv_sem=grecv.at[gy],
            device_id={"gx": gx, "gy": other},
            device_id_type=MESH,
        )

    def from_row(other):
        return pltpu.make_async_remote_copy(
            src_ref=own_row,
            dst_ref=rows.at[other],
            send_sem=gsend.at[other],
            recv_sem=grecv.at[other],
            device_id={"gx": gx, "gy": other},
            device_id_type=MESH,
        )

    for step in range(1, ny):
        to_row(step).start()
    for step in range(1, ny):
        from_row(lax.rem(gy + step, ny)).wait_recv()
    rows[gy] = row
    entries = jnp.sum(rows[...], axis=0)
    block = inv.shape[1]
    values = entries[:, :block]
    rounded = values.astype(BF16).astype(F32)
    values = jnp.concatenate(
        [jnp.broadcast_to(rounded, (8, block)), jnp.broadcast_to(values - rounded, (8, block))], axis=0
    ).astype(BF16)
    upper_part, lower_part = (
        lax.dot_general(values, invs[at], (((1,), (1,)), ((), ())), preferred_element_type=F32) for at in range(2)
    )
    product = upper_part[0:1] + (upper_part[8:9] + lower_part[0:1] + lower_part[8:9])
    part_row[:, pl.ds(0, block)] = product

    def to_part(other):
        return pltpu.make_async_remote_copy(
            src_ref=part_row,
            dst_ref=parts.at[gx],
            send_sem=psend.at[other],
            recv_sem=precv.at[gx],
            device_id={"gx": gy, "gy": other},
            device_id_type=MESH,
        )

    def from_part(other):
        return pltpu.make_async_remote_copy(
            src_ref=part_row,
            dst_ref=parts.at[other],
            send_sem=psend.at[other],
            recv_sem=precv.at[other],
            device_id={"gx": other, "gy": gx},
            device_id_type=MESH,
        )

    for step in range(1, ny):
        to_part(lax.rem(gy + step, ny)).start()

    @pl.when(gx != gy)
    def _():
        to_part(gy).start()

    @pl.when(gx == gy)
    def _():
        parts[gx] = part_row[...]

    for step in range(1, nx):
        from_part(lax.rem(gx + step, nx)).wait_recv()

    @pl.when(gx != gy)
    def _():
        from_part(gx).wait_recv()

    coarsest = jnp.sum(parts[...], axis=0)

    for piece in range(5):
        size = 8 if piece < 4 else 4
        at = pl.ds(8 * piece, size)
        _, c = rows_of(piece, size)
        spread = [
            jnp.sum(jnp.where(lane == 12 * gy + 2 * c + a, coarsest, 0.0), axis=1, keepdims=True)
            for a in range(2)
        ]
        cacc[at, :] = ctn[at, :] * jnp.where(upper, spread[1], spread[0])
    ext[1, :, pl.ds(0, A1)] = ext[0, :, pl.ds(0, A1)] + folded()
    send_coarse(1)
    coarse_apply(1)
    solved = ext[1, :, pl.ds(0, A1)]
    solved = solved + damping * (crhs[...] - (cst8 * solved + folded())) / cst8
    y2[...] = solved
    csol[...] = solved[0:6]
    csol_out = pltpu.make_async_copy(csol, csol_h, out_sem.at[FX])
    csol_out.start()

    entries = table(y2[...])
    tables = [y2[:, pl.ds(LANES * h, LANES)] for h in range(A1 // LANES)]

    def lift(x):
        for y in range(FY):
            taken = look_up(entries, ohm[x, :, pl.ds(NZ * y, HALF)], mem[x, pl.ds(y, 1), pl.ds(0, HALF)])
            for t in range(NZ // LANES):
                if t < HALF // LANES:
                    value = taken[:, LANES * t : LANES * (t + 1)]
                else:
                    index = mem[x, pl.ds(y, 1), pl.ds(LANES * t, LANES)]
                    value = pick(tables, jnp.broadcast_to(index, (8, LANES)))
                nodes[x, t, pl.ds(y, 8, stride=8), :] = value
        values = []
        for i in range(3):
            value = 0.0
            for c in range(6):
                taken = jnp.concatenate(
                    [nodes[x, t, pl.ds(8 * c, 8), :] for t in range(NZ // LANES)], axis=1
                )
                value = value + ten[6 * i + c, x].astype(F32) * taken
            values.append(value)
        put_field(3, x, values)

    slabs(3, lift)

    def corrected(x):
        total = outside(3, x)
        put_field(
            4,
            x,
            [
                field[1, c, x] + field[3, c, x] - smoothing * total[c] * wgt[c, x]
                for c in range(3)
            ],
        )

    inside(3)
    wait_halo(3)
    slabs(4, corrected)

    inside(4)
    wait_halo(4)
    slabs(5, lambda x: put_field(5, x, smoothed(4, x)))

    def last(x):
        values = smoothed(5, x)
        for c in range(3):
            sol[c, x] = values[c]
        sol_out(x).start()

    def sol_out(x):
        return pltpu.make_async_copy(sol.at[:, x], sol_h.at[:, x], out_sem.at[x])

    inside(5)
    wait_halo(5)
    slabs(None, last)

    for side in range(4):

        @pl.when(near[side][0])
        def _():
            for number in range(FIELDS):
                halo(number, side).wait_send()
            for number in range(2):
                coarse_halo(number, side ^ 1).wait_send()

    for step in range(1, ny):
        to_row(step).wait_send()
        to_part(lax.rem(gy + step, ny)).wait_send()

    @pl.when(gx != gy)
    def _():
        to_part(gy).wait_send()

    for x in range(FX):
        sol_out(x).wait()
    csol_out.wait()


def write_out(sol, csol, sol_out, csol_out):
    sol_out[...] = sol[...]
    csol_out[...] = csol[...]


def body(nx, ny, rhs, stiffness, couplings, tentative, members, cst, ccp, col, snd, ctn, cmb, inv):
    couplings = couplings.reshape(63, FX, FY, NZ)
    tentative = tentative.reshape(18, FX, FY, NZ)
    cmb = cmb.reshape(1, A1)
    operands = (rhs, stiffness, couplings, tentative, members, cst, ccp, col, snd, ctn, cmb, inv)
    dma = pltpu.SemaphoreType.DMA
    scratch = [pltpu.VMEM(operand.shape, operand.dtype) for operand in operands]
    scratch += [
        pltpu.VMEM((3, FX, FY, NZ), F32),
        pltpu.VMEM((FIELDS, 3, FX, FY, NZ), F32),
        pltpu.VMEM((2, 3, FX, NZ), F32),
        pltpu.VMEM((2, 3, FX, NZ), F32),
        pltpu.VMEM((FIELDS - WIDE, 4, 3, 16, NZ // 2), BF16),
        pltpu.VMEM((FIELDS - WIDE, 4, 3, 16, NZ // 2), BF16),
        pltpu.VMEM((WIDE, 4, 3, 16, NZ // 2), F32),
        pltpu.VMEM((WIDE, 4, 3, 16, NZ // 2), F32),
        pltpu.VMEM((3, FX, FY, NZ), F32),
        pltpu.VMEM((3, FX, FY, NZ), F32),
        pltpu.VMEM((FX, NZ // LANES, 8 * FY, LANES), F32),
        pltpu.VMEM((8, A1), F32),
        pltpu.VMEM((8, A1), F32),
        pltpu.VMEM((2, 8, A1 + 4 * H), F32),
        pltpu.VMEM((2, 4, 8, H), F32),
        pltpu.VMEM((40, A1), F32),
        pltpu.VMEM((2, *inv.shape), BF16),
        pltpu.VMEM((3, FX, FY, NZ), F32),
        pltpu.VMEM((6, A1), F32),
        pltpu.VMEM((FX, LANES, FY * NZ), BF16),
        pltpu.VMEM((K, LANES, A1), BF16),
        pltpu.VMEM((1, 2 * LANES), F32),
        pltpu.VMEM((ny, 1, 2 * LANES), F32),
        pltpu.VMEM((1, 2 * LANES), F32),
        pltpu.VMEM((nx, 1, 2 * LANES), F32),
        pltpu.SemaphoreType.REGULAR((3,)),
        dma((18,)),
        dma((FX + 1,)),
        dma((FIELDS, 4)),
        dma((FIELDS, 4)),
        dma((2, 4)),
        dma((2, 4)),
        dma((ny,)),
        dma((ny,)),
        dma((ny,)),
        dma((nx,)),
    ]
    results = pl.pallas_call(
        functools.partial(kernel, nx, ny),
        out_shape=(
            jax.ShapeDtypeStruct((3, FX, FY, NZ), F32),
            jax.ShapeDtypeStruct((6, A1), F32),
        ),
        in_specs=[pl.BlockSpec(memory_space=pl.ANY)] * len(operands),
        out_specs=(pl.BlockSpec(memory_space=pl.ANY),) * 2,
        scratch_shapes=scratch,
        compiler_params=pltpu.CompilerParams(
            collective_id=0, has_side_effects=True, vmem_limit_bytes=56 * 1024 * 1024
        ),
    )(*operands)
    return pl.pallas_call(
        write_out,
        out_shape=tuple(jax.ShapeDtypeStruct(result.shape, result.dtype) for result in results),
        in_specs=[pl.BlockSpec(memory_space=pltpu.VMEM)] * 2,
        out_specs=(pl.BlockSpec(memory_space=pltpu.VMEM),) * 2,
        compiler_params=pltpu.CompilerParams(vmem_limit_bytes=60 * 1024 * 1024),
    )(*results)


def solution(mesh):
    placed = (
        P(None, "gx", "gy", None),
        P(None, "gx", "gy", None),
        P(None, None, None, "gx", "gy", None),
        P(None, None, "gx", "gy", None),
        P("gx", "gy", None),
        P(None, ("gx", "gy")),
        P(None, None, ("gx", "gy")),
        P(None, ("gx", "gy")),
        P(None, ("gx", "gy")),
        P(None, ("gx", "gy")),
        P(("gx", "gy")),
        P("gy", "gx"),
    )
    return jax.shard_map(
        functools.partial(body, mesh.shape["gx"], mesh.shape["gy"]),
        mesh=mesh,
        in_specs=placed,
        out_specs=(P(None, "gx", "gy", None), P(None, ("gx", "gy"))),
        check_vma=False,
    )
```

```python
import functools

import jax
import jax.numpy as jnp
from jax import lax
from jax.experimental import pallas as pl
from jax.experimental.pallas import tpu as pltpu
from jax.sharding import PartitionSpec as P

MESH = pl.DeviceIdType.MESH
F32 = jnp.float32
BF16 = jnp.bfloat16

FX = 8
FY = 8
NZ = 512
K = 27
A1 = 1024
H = 256
LANES = 128
GROUP = 512
HALF = 256
WIDE = 2
FIELDS = 6

damping = 0.6
smoothing = 0.5


def lane_gather(table, index):
    dims = lax.GatherDimensionNumbers(
        offset_dims=(),
        collapsed_slice_dims=(1,),
        start_index_map=(1,),
        operand_batching_dims=(0,),
        start_indices_batching_dims=(0,),
    )
    return lax.gather(
        table, index[..., None], dims, slice_sizes=(1, 1), mode=lax.GatherScatterMode.PROMISE_IN_BOUNDS
    )


def pick(tables, index):
    low = index & (LANES - 1)
    parts = [lane_gather(table, low) for table in tables]
    bit = LANES
    while len(parts) > 1:
        upper = (index & bit) != 0
        parts = [jnp.where(upper, parts[at + 1], parts[at]) for at in range(0, len(parts), 2)]
        bit *= 2
    return parts[0]


def rows_of(piece, rows):
    sub = lax.broadcasted_iota(jnp.int32, (rows, 1), 0)
    first, last = (8 * piece) // 6, min((8 * piece + 7) // 6, 5)
    i = jnp.where(sub < 6 * (first + 1) - 8 * piece, first, last)
    return i, 8 * piece + sub - 6 * i


def kernel(
    nx,
    ny,
    rhs_h,
    stf_h,
    cpl_h,
    ten_h,
    mem_h,
    cst_h,
    ccp_h,
    col_h,
    snd_h,
    ctn_h,
    cmb_h,
    inv_h,
    sol_h,
    csol_h,
    rhs,
    stf,
    cpl,
    ten,
    mem,
    cst,
    ccp,
    col,
    snd,
    ctn,
    cmb,
    inv,
    wgt,
    field,
    yout,
    yin,
    hout,
    hin,
    wout,
    win,
    acc,
    resid,
    nodes,
    crhs,
    y2,
    ext,
    cout,
    cacc,
    lift1,
    lout,
    invs,
    sol,
    csol,
    ohm,
    ohc,
    own_row,
    rows,
    part_row,
    parts,
    wave,
    load_sem,
    out_sem,
    fsend,
    frecv,
    csend,
    crecv,
    gsend,
    grecv,
    psend,
    precv,
):
    gx, gy = lax.axis_index("gx"), lax.axis_index("gy")
    near = (
        (gx > 0, {"gx": jnp.maximum(gx - 1, 0), "gy": gy}),
        (gx < nx - 1, {"gx": jnp.minimum(gx + 1, nx - 1), "gy": gy}),
        (gy > 0, {"gx": gx, "gy": jnp.maximum(gy - 1, 0)}),
        (gy < ny - 1, {"gx": gx, "gy": jnp.minimum(gy + 1, ny - 1)}),
    )

    barrier = pltpu.get_barrier_semaphore()

    def tell(semaphore, steps):
        for device in (
            {"gx": lax.rem(gx + nx - steps, nx), "gy": gy},
            {"gx": lax.rem(gx + steps, nx), "gy": gy},
            {"gx": gx, "gy": lax.rem(gy + ny - steps, ny)},
            {"gx": gx, "gy": lax.rem(gy + steps, ny)},
        ):
            pl.semaphore_signal(semaphore, inc=1, device_id=device, device_id_type=MESH)

    def announce(number):
        if 2 << number < nx:
            tell(wave.at[number], 1 << number)

    def heard(number):
        if 2 << number < nx:
            pl.semaphore_wait(wave.at[number], 4)

    if nx > 1:
        tell(barrier, 1)

    loads = {}
    pairs = [("rhs", rhs_h, rhs), ("stf", stf_h, stf), ("mem", mem_h, mem)]
    for offset in (0, 5, 6, 1, 2, 3, 4):
        pairs.append(("cpl%d" % offset, cpl_h.at[pl.ds(9 * offset, 9)], cpl.at[pl.ds(9 * offset, 9)]))
    pairs += [
        ("snd", snd_h, snd),
        ("ctn", ctn_h, ctn),
        ("cmb", cmb_h, cmb),
        ("col", col_h, col),
        ("ten", ten_h, ten),
        ("cst", cst_h, cst),
        ("ccp", ccp_h, ccp),
        ("inv", inv_h, inv),
    ]
    for number, (name, source, target) in enumerate(pairs):
        loads[name] = pltpu.make_async_copy(source, target, load_sem.at[number])
        loads[name].start()

    def layer_out(number, side):
        return wout.at[number, side] if number < WIDE else hout.at[number - WIDE, side]

    def layer_in(number, side):
        return win.at[number, side] if number < WIDE else hin.at[number - WIDE, side]

    for side, (there, _) in enumerate(near):

        @pl.when(jnp.logical_not(there))
        def _():
            for number in range(FIELDS):
                target = layer_in(number, side)
                target[...] = jnp.zeros(target.shape, target.dtype)
            ext[0, :, pl.ds(A1 + H * side, H)] = jnp.zeros((8, H), F32)
            lift1[:, pl.ds(A1 + H * side, H)] = jnp.zeros((40, H), F32)
            if side < 2:
                parts[2 * side] = jnp.zeros(parts.shape[1:], F32)

    cacc[pl.ds(32, 8), :] = jnp.zeros((8, A1 + 4 * H), F32)
    own_row[...] = jnp.zeros_like(own_row)
    part_row[...] = jnp.zeros_like(part_row)

    def halo(number, side):
        return pltpu.make_async_remote_copy(
            src_ref=layer_out(number, side),
            dst_ref=layer_in(number, side ^ 1),
            send_sem=fsend.at[number, side],
            recv_sem=frecv.at[number, side ^ 1],
            device_id=near[side][1],
            device_id_type=MESH,
        )

    def pack(number, side, c, value):
        target = layer_out(number, side)
        target[c] = jnp.concatenate([value[:, : NZ // 2], value[:, NZ // 2 :]], axis=0).astype(target.dtype)

    def received(number, side, j):
        value = layer_in(number, side)[j].astype(F32)
        return jnp.concatenate([value[:8], value[8:]], axis=1)

    def send_halo(number, side):
        @pl.when(near[side][0])
        def _():
            halo(number, side).start()

    def wait_halo(number):
        for side in range(4):

            @pl.when(near[side][0])
            def _():
                halo(number, side ^ 1).wait_recv()

        for side in range(2):
            for j in range(3):
                yin[side, j] = received(number, side + 2, j)

    def put_field(number, x, values):
        for c in range(3):
            field[number, c, x] = values[c]
            yout[0, c, pl.ds(x, 1), :] = values[c][0:1, :]
            yout[1, c, pl.ds(x, 1), :] = values[c][FY - 1 : FY, :]
            if isinstance(x, int) and x == 0:
                pack(number, 0, c, values[c])
            if isinstance(x, int) and x == FX - 1:
                pack(number, 1, c, values[c])

    def slabs(number, slab):
        slab(0)
        if number is not None:
            send_halo(number, 0)
        slab(FX - 1)
        if number is not None:
            send_halo(number, 1)

        def inner(x, carry):
            slab(x)
            return carry

        lax.fori_loop(1, FX - 1, inner, 0)
        if number is not None:
            for side in range(2):
                for c in range(3):
                    pack(number, side + 2, c, yout[side, c])
                send_halo(number, side + 2)

    def add(total, offset, x, j, view):
        for i in range(3):
            total[i] = total[i] + cpl[9 * offset + 3 * i + j, x].astype(F32) * view

    def inside(number):
        lane = lax.broadcasted_iota(jnp.int32, (FY, NZ), 1)

        def slab(x):
            total = [stf[i, x] * field[number, i, x] for i in range(3)]
            for j in range(3):
                view = field[number, j, x]
                add(total, 0, x, j, view)
                add(total, 5, x, j, jnp.where(lane == 0, 0.0, pltpu.roll(view, 1, axis=1)))
                add(total, 6, x, j, jnp.where(lane == NZ - 1, 0.0, pltpu.roll(view, NZ - 1, axis=1)))
                if not (isinstance(x, int) and x == 0):
                    add(total, 1, x, j, field[number, j, x - 1])
                if not (isinstance(x, int) and x == FX - 1):
                    add(total, 2, x, j, field[number, j, x + 1])
            for i in range(3):
                acc[i, x] = total[i]

        slabs(None, slab)

    def outside(number, x):
        row = lax.broadcasted_iota(jnp.int32, (FY, NZ), 0)
        total = [acc[i, x] for i in range(3)]
        for j in range(3):
            view = field[number, j, x]
            below = yin[0, j, pl.ds(x, 1), :]
            above = yin[1, j, pl.ds(x, 1), :]
            add(total, 3, x, j, jnp.where(row == 0, below, pltpu.roll(view, 1, axis=0)))
            add(total, 4, x, j, jnp.where(row == FY - 1, above, pltpu.roll(view, FY - 1, axis=0)))
            if isinstance(x, int) and x == 0:
                add(total, 1, x, j, received(number, 0, j))
            if isinstance(x, int) and x == FX - 1:
                add(total, 2, x, j, received(number, 1, j))
        return total

    def coarse_halo(number, side):
        span = pl.ds(A1 + H * side, H)
        return pltpu.make_async_remote_copy(
            src_ref=lout.at[side] if number else cout.at[side],
            dst_ref=lift1.at[:, span] if number else ext.at[0, :, span],
            send_sem=csend.at[number, side],
            recv_sem=crecv.at[number, side],
            device_id=near[side ^ 1][1],
            device_id_type=MESH,
        )

    def wait_coarse(number):
        for side in range(4):

            @pl.when(near[side][0])
            def _():
                coarse_halo(number, side).wait_recv()

    def send_lift():
        lift1[pl.ds(0, 32), pl.ds(0, A1)] = ctn[pl.ds(0, 32), :]
        members = jnp.broadcast_to(cmb[...].astype(F32), (4, A1))
        lift1[pl.ds(32, 8), pl.ds(0, A1)] = jnp.concatenate([ctn[pl.ds(32, 4), :], members], axis=0)

        def one(piece, carry):
            rows8 = pl.ds(pl.multiple_of(8 * piece, 8), 8)
            tables = [lift1[rows8, pl.ds(LANES * h, LANES)] for h in range(A1 // LANES)]
            for side in range(4):
                for t in range(H // LANES):
                    span = pl.ds(LANES * t, LANES)
                    lout[side, rows8, span] = pick(tables, jnp.broadcast_to(snd[side : side + 1, span], (8, LANES)))
            return carry

        lax.fori_loop(0, 5, one, 0)
        for side in range(4):

            @pl.when(near[side ^ 1][0])
            def _():
                coarse_halo(1, side).start()

    loads["rhs"].wait()
    loads["stf"].wait()

    def first(x):
        values = []
        for c in range(3):
            weight = 1.0 / stf[c, x]
            wgt[c, x] = weight
            values.append(damping * rhs[c, x] * weight)
        put_field(0, x, values)

    if nx > 1:
        pl.semaphore_wait(barrier, 4)
    announce(0)
    slabs(0, first)

    count = lax.broadcasted_iota(jnp.int32, (16, NZ), 0).astype(F32).astype(BF16)

    def one_hot(index):
        width = index.shape[1]
        low = jnp.broadcast_to(index & (LANES - 1), (16, width)).astype(F32).astype(BF16)
        one, zero = jnp.ones((16, width), BF16), jnp.zeros((16, width), BF16)
        return jnp.concatenate(
            [jnp.where(low == count[:, :width] + float(16 * k), one, zero) for k in range(8)], axis=0
        )

    def hot_members(x, carry):
        for y in range(FY):
            ohm[x, :, pl.ds(NZ * y, NZ)] = one_hot(mem[x, pl.ds(y, 1), :])
        return carry

    def hot_columns(t, carry):
        span = pl.ds(pl.multiple_of(GROUP * t, GROUP), GROUP)
        columns = col[:, span]
        for k in range(K):
            ohc[k, :, span] = one_hot(columns[k : k + 1])
        return carry

    def choose(parts, index):
        bit = LANES
        while len(parts) > 1:
            upper = (index & bit) != 0
            parts = [jnp.where(upper, parts[at + 1], parts[at]) for at in range(0, len(parts), 2)]
            bit *= 2
        return parts[0]

    def table(values):
        pieces = [values[:, LANES * h : LANES * (h + 1)] for h in range(values.shape[1] // LANES)]
        value = jnp.concatenate(pieces, axis=0)
        rounded = value.astype(BF16).astype(F32)
        return jnp.concatenate([rounded, value - rounded], axis=1).astype(BF16)

    def look_up(entries, hot, index):
        product = jnp.dot(entries, jnp.concatenate([hot, hot], axis=0), preferred_element_type=F32)
        pieces = [product[8 * h : 8 * h + 8] for h in range(product.shape[0] // 8)]
        return choose(pieces, jnp.broadcast_to(index, (8, index.shape[1])))

    loads["mem"].wait()
    lax.fori_loop(0, FX, hot_members, 0)

    for offset in (0, 5, 6, 1, 2, 3, 4):
        loads["cpl%d" % offset].wait()

    def smoothed(number, x):
        total = outside(number, x)
        return [
            field[number, c, x] + damping * (rhs[c, x] - total[c]) * wgt[c, x] for c in range(3)
        ]

    inside(0)
    heard(0)
    announce(1)
    wait_halo(0)
    slabs(1, lambda x: put_field(1, x, smoothed(0, x)))

    def residual(x):
        total = outside(1, x)
        values = []
        for c in range(3):
            left = rhs[c, x] - total[c]
            resid[c, x] = left
            values.append(left * wgt[c, x])
        put_field(2, x, values)

    loads["snd"].wait()
    loads["ctn"].wait()
    loads["cmb"].wait()
    send_lift()
    inside(1)
    heard(1)
    announce(2)
    wait_halo(1)
    slabs(2, residual)

    loads["ten"].wait()

    def restrict(x):
        total = outside(2, x)
        filtered = [resid[i, x] - smoothing * total[i] for i in range(3)]
        for c in range(6):
            value = ten[c, x].astype(F32) * filtered[0]
            for i in range(1, 3):
                value = value + ten[6 * i + c, x].astype(F32) * filtered[i]
            for t in range(NZ // LANES):
                part = value[:, LANES * t : LANES * (t + 1)]
                nodes[x, t, pl.ds(8 * c, 8), :] = part
                if c < 2:
                    nodes[x, t, pl.ds(8 * (c + 6), 8), :] = part

    loads["inv"].wait()
    whole = inv[...]
    rounded = whole.astype(BF16)
    invs[0] = rounded
    invs[1] = (whole - rounded.astype(F32)).astype(BF16)
    inside(2)
    heard(2)
    wait_halo(2)
    wait_coarse(1)
    slabs(None, restrict)

    def sums(x, total):
        for y in range(FY):
            value = jnp.concatenate(
                [nodes[x, t, pl.ds(y, 8, stride=8), :] for t in range(NZ // LANES)], axis=1
            )
            rounded = value.astype(BF16).astype(F32)
            both = jnp.concatenate([rounded, value - rounded], axis=0).astype(BF16)
            index = jnp.broadcast_to(mem[x, pl.ds(y, 1), :], (16, NZ))
            high = lax.shift_right_logical(index, 7).astype(F32).astype(BF16)
            zero = jnp.zeros((16, NZ), BF16)
            left = jnp.concatenate([jnp.where(high == float(h), both, zero) for h in range(8)], axis=0)
            right = ohm[x, :, pl.ds(NZ * y, NZ)]
            total = total + lax.dot_general(
                left, right, (((1,), (1,)), ((), ())), preferred_element_type=F32
            )
        return total

    gathered = lax.fori_loop(0, FX, sums, jnp.zeros((LANES, LANES), F32))

    loads["cst"].wait()
    for h in range(8):
        span = pl.ds(LANES * h, LANES)
        crhs[:, span] = gathered[16 * h : 16 * h + 8] + gathered[16 * h + 8 : 16 * h + 16]
    cst8 = jnp.concatenate([cst[...], cst[0:2, :]], axis=0)
    ext[0, :, pl.ds(0, A1)] = damping * crhs[...] / cst8

    def send_coarse():
        tables = [ext[0, :, pl.ds(LANES * h, LANES)] for h in range(A1 // LANES)]
        for side in range(4):
            for t in range(H // LANES):
                index = jnp.broadcast_to(snd[side : side + 1, pl.ds(LANES * t, LANES)], (8, LANES))
                cout[side, :, pl.ds(LANES * t, LANES)] = pick(tables, index)

            @pl.when(near[side ^ 1][0])
            def _():
                coarse_halo(0, side).start()

    sub = lax.broadcasted_iota(jnp.int32, (8, GROUP), 0)

    def coarse_apply(number):
        entries = table(ext[number])

        def group(t, carry):
            span = pl.ds(pl.multiple_of(GROUP * t, GROUP), GROUP)
            total = [jnp.zeros((8 if piece < 4 else 4, GROUP), F32) for piece in range(5)]
            columns = col[:, span]
            for k in range(K):
                base = look_up(entries, ohc[k, :, span], columns[k : k + 1])
                up2, by4, down2 = (pltpu.roll(base, by, axis=0) for by in (6, 4, 2))
                turned = (base, jnp.where(sub < 6, up2, by4), jnp.where(sub < 2, by4, down2))
                for piece in range(5):
                    size = 8 if piece < 4 else 4
                    block = ccp[k, pl.ds(8 * piece, size), span]
                    total[piece] = total[piece] + block * turned[piece % 3][:size]
            for piece in range(5):
                cacc[pl.ds(8 * piece, 8 if piece < 4 else 4), span] = total[piece]
            return carry

        lax.fori_loop(0, A1 // GROUP, group, 0)

    fold_row = lax.broadcasted_iota(jnp.int32, (8, 40), 0)
    fold_col = lax.broadcasted_iota(jnp.int32, (8, 40), 1)
    fold_row = jnp.where(fold_row < 6, fold_row, fold_row - 6)
    fold = jnp.logical_and(fold_col >= 6 * fold_row, fold_col < 6 * fold_row + 6).astype(F32)

    def folded():
        return jnp.dot(fold, cacc[:, pl.ds(0, A1)], precision=lax.Precision.HIGHEST, preferred_element_type=F32)

    send_coarse()
    loads["col"].wait()
    lax.fori_loop(0, A1 // GROUP, hot_columns, 0)
    loads["ccp"].wait()
    wait_coarse(0)
    coarse_apply(0)
    s1 = crhs[...] - (cst8 * ext[0, :, pl.ds(0, A1)] + folded())

    lane = lax.broadcasted_iota(jnp.int32, (1, 2 * LANES), 1)
    upper = cmb[...] != 0
    row = jnp.zeros((1, 2 * LANES), F32)
    for piece in range(5):
        size = 8 if piece < 4 else 4
        i, c = rows_of(piece, size)
        first_i, last_i = (8 * piece) // 6, min((8 * piece + 7) // 6, 5)
        matching = jnp.where(i == first_i, s1[first_i : first_i + 1], s1[last_i : last_i + 1])
        product = ctn[pl.ds(8 * piece, size), :] * matching
        for a in range(2):
            kept = jnp.where(upper, product, 0.0) if a else jnp.where(upper, 0.0, product)
            total = jnp.sum(kept, axis=1, keepdims=True)
            place = 12 * gy + 2 * c + a
            row = row + jnp.sum(jnp.where(lane == place, total, 0.0), axis=0, keepdims=True)
    own_row[...] = row

    def to_row(step):
        other = lax.rem(gy + step, ny)
        return pltpu.make_async_remote_copy(
            src_ref=own_row,
            dst_ref=rows.at[gy],
            send_sem=gsend.at[other],
            recv_sem=grecv.at[gy],
            device_id={"gx": gx, "gy": other},
            device_id_type=MESH,
        )

    def from_row(other):
        return pltpu.make_async_remote_copy(
            src_ref=own_row,
            dst_ref=rows.at[other],
            send_sem=gsend.at[other],
            recv_sem=grecv.at[other],
            device_id={"gx": gx, "gy": other},
            device_id_type=MESH,
        )

    for step in range(1, ny):
        to_row(step).start()
    for step in range(1, ny):
        from_row(lax.rem(gy + step, ny)).wait_recv()
    rows[gy] = row
    entries = jnp.sum(rows[...], axis=0)
    block = inv.shape[1]
    values = entries[:, :block]
    rounded = values.astype(BF16).astype(F32)
    values = jnp.concatenate(
        [jnp.broadcast_to(rounded, (8, block)), jnp.broadcast_to(values - rounded, (8, block))], axis=0
    ).astype(BF16)
    upper_part, lower_part = (
        lax.dot_general(values, invs[at], (((1,), (1,)), ((), ())), preferred_element_type=F32) for at in range(2)
    )
    product = upper_part[0:1] + (upper_part[8:9] + lower_part[0:1] + lower_part[8:9])
    part_row[:, pl.ds(0, block)] = product

    def part(at, row_of, semaphore, device):
        return pltpu.make_async_remote_copy(
            src_ref=part_row,
            dst_ref=parts.at[at, row_of],
            send_sem=psend.at[at, semaphore],
            recv_sem=precv.at[at, row_of],
            device_id=device,
            device_id_type=MESH,
        )

    def to_part(at, step):
        other = lax.rem(gy + step, ny)
        return part(at, gx, step, {"gx": jnp.clip(gy + 1 - at, 0, nx - 1), "gy": other})

    def from_part(at, step):
        other = lax.rem(gx + step, nx)
        return part(at, other, 0, {"gx": other, "gy": jnp.clip(gx + at - 1, 0, ny - 1)})

    for at in (1, 0, 2):
        target, held = gy + 1 - at, gx + at - 1

        @pl.when(jnp.logical_and(target >= 0, target < nx))
        def _():
            for step in range(1, ny):
                to_part(at, step).start()

            @pl.when(gx != target)
            def _():
                to_part(at, 0).start()

            @pl.when(gx == target)
            def _():
                parts[at, gx] = part_row[...]

    for at in (1, 0, 2):
        target, held = gy + 1 - at, gx + at - 1

        @pl.when(jnp.logical_and(held >= 0, held < ny))
        def _():
            for step in range(1, nx):
                from_part(at, step).wait_recv()

            @pl.when(gy != held)
            def _():
                from_part(at, 0).wait_recv()

    coarsest = [jnp.sum(parts[at], axis=0) for at in range(3)]

    places = (
        (0, A1, 1, gy),
        (A1, H, 0, gy),
        (A1 + H, H, 2, gy),
        (A1 + 2 * H, H, 1, gy - 1),
        (A1 + 3 * H, H, 1, gy + 1),
    )
    for start, length, at, owner in places:
        span = pl.ds(start, length)
        one = lift1[36:37, span] != 0.0
        for piece in range(5):
            size = 8 if piece < 4 else 4
            _, c = rows_of(piece, size)
            spread = [
                jnp.sum(jnp.where(lane == 12 * owner + 2 * c + a, coarsest[at], 0.0), axis=1, keepdims=True)
                for a in range(2)
            ]
            here = pl.ds(8 * piece, size)
            cacc[here, span] = lift1[here, span] * jnp.where(one, spread[1], spread[0])
    ext[1] = ext[0] + jnp.dot(fold, cacc[...], precision=lax.Precision.HIGHEST, preferred_element_type=F32)
    coarse_apply(1)
    solved = ext[1, :, pl.ds(0, A1)]
    solved = solved + damping * (crhs[...] - (cst8 * solved + folded())) / cst8
    y2[...] = solved
    csol[...] = solved[0:6]
    csol_out = pltpu.make_async_copy(csol, csol_h, out_sem.at[FX])
    csol_out.start()

    entries = table(y2[...])
    tables = [y2[:, pl.ds(LANES * h, LANES)] for h in range(A1 // LANES)]

    def lift(x):
        for y in range(FY):
            taken = look_up(entries, ohm[x, :, pl.ds(NZ * y, HALF)], mem[x, pl.ds(y, 1), pl.ds(0, HALF)])
            for t in range(NZ // LANES):
                if t < HALF // LANES:
                    value = taken[:, LANES * t : LANES * (t + 1)]
                else:
                    index = mem[x, pl.ds(y, 1), pl.ds(LANES * t, LANES)]
                    value = pick(tables, jnp.broadcast_to(index, (8, LANES)))
                nodes[x, t, pl.ds(y, 8, stride=8), :] = value
        values = []
        for i in range(3):
            value = 0.0
            for c in range(6):
                taken = jnp.concatenate(
                    [nodes[x, t, pl.ds(8 * c, 8), :] for t in range(NZ // LANES)], axis=1
                )
                value = value + ten[6 * i + c, x].astype(F32) * taken
            values.append(value)
        put_field(3, x, values)

    slabs(3, lift)

    def corrected(x):
        total = outside(3, x)
        put_field(
            4,
            x,
            [
                field[1, c, x] + field[3, c, x] - smoothing * total[c] * wgt[c, x]
                for c in range(3)
            ],
        )

    inside(3)
    wait_halo(3)
    slabs(4, corrected)

    inside(4)
    wait_halo(4)
    slabs(5, lambda x: put_field(5, x, smoothed(4, x)))

    def last(x):
        values = smoothed(5, x)
        for c in range(3):
            sol[c, x] = values[c]
        sol_out(x).start()

    def sol_out(x):
        return pltpu.make_async_copy(sol.at[:, x], sol_h.at[:, x], out_sem.at[x])

    inside(5)
    wait_halo(5)
    slabs(None, last)

    for side in range(4):

        @pl.when(near[side][0])
        def _():
            for number in range(FIELDS):
                halo(number, side).wait_send()
            for number in range(2):
                coarse_halo(number, side ^ 1).wait_send()

    for step in range(1, ny):
        to_row(step).wait_send()
    for at in range(3):
        target = gy + 1 - at

        @pl.when(jnp.logical_and(target >= 0, target < nx))
        def _():
            for step in range(1, ny):
                to_part(at, step).wait_send()

            @pl.when(gx != target)
            def _():
                to_part(at, 0).wait_send()

    for x in range(FX):
        sol_out(x).wait()
    csol_out.wait()


def write_out(sol, csol, sol_out, csol_out):
    sol_out[...] = sol[...]
    csol_out[...] = csol[...]


def body(nx, ny, rhs, stiffness, couplings, tentative, members, cst, ccp, col, snd, ctn, cmb, inv):
    couplings = couplings.reshape(63, FX, FY, NZ)
    tentative = tentative.reshape(18, FX, FY, NZ)
    cmb = cmb.reshape(1, A1)
    operands = (rhs, stiffness, couplings, tentative, members, cst, ccp, col, snd, ctn, cmb, inv)
    dma = pltpu.SemaphoreType.DMA
    scratch = [pltpu.VMEM(operand.shape, operand.dtype) for operand in operands]
    scratch += [
        pltpu.VMEM((3, FX, FY, NZ), F32),
        pltpu.VMEM((FIELDS, 3, FX, FY, NZ), F32),
        pltpu.VMEM((2, 3, FX, NZ), F32),
        pltpu.VMEM((2, 3, FX, NZ), F32),
        pltpu.VMEM((FIELDS - WIDE, 4, 3, 16, NZ // 2), BF16),
        pltpu.VMEM((FIELDS - WIDE, 4, 3, 16, NZ // 2), BF16),
        pltpu.VMEM((WIDE, 4, 3, 16, NZ // 2), F32),
        pltpu.VMEM((WIDE, 4, 3, 16, NZ // 2), F32),
        pltpu.VMEM((3, FX, FY, NZ), F32),
        pltpu.VMEM((3, FX, FY, NZ), F32),
        pltpu.VMEM((FX, NZ // LANES, 8 * FY, LANES), F32),
        pltpu.VMEM((8, A1), F32),
        pltpu.VMEM((8, A1), F32),
        pltpu.VMEM((2, 8, A1 + 4 * H), F32),
        pltpu.VMEM((4, 8, H), F32),
        pltpu.VMEM((40, A1 + 4 * H), F32),
        pltpu.VMEM((40, A1 + 4 * H), F32),
        pltpu.VMEM((4, 40, H), F32),
        pltpu.VMEM((2, *inv.shape), BF16),
        pltpu.VMEM((3, FX, FY, NZ), F32),
        pltpu.VMEM((6, A1), F32),
        pltpu.VMEM((FX, LANES, FY * NZ), BF16),
        pltpu.VMEM((K, LANES, A1), BF16),
        pltpu.VMEM((1, 2 * LANES), F32),
        pltpu.VMEM((ny, 1, 2 * LANES), F32),
        pltpu.VMEM((1, 2 * LANES), F32),
        pltpu.VMEM((3, nx, 1, 2 * LANES), F32),
        pltpu.SemaphoreType.REGULAR((3,)),
        dma((18,)),
        dma((FX + 1,)),
        dma((FIELDS, 4)),
        dma((FIELDS, 4)),
        dma((2, 4)),
        dma((2, 4)),
        dma((ny,)),
        dma((ny,)),
        dma((3, ny)),
        dma((3, nx)),
    ]
    results = pl.pallas_call(
        functools.partial(kernel, nx, ny),
        out_shape=(
            jax.ShapeDtypeStruct((3, FX, FY, NZ), F32),
            jax.ShapeDtypeStruct((6, A1), F32),
        ),
        in_specs=[pl.BlockSpec(memory_space=pl.ANY)] * len(operands),
        out_specs=(pl.BlockSpec(memory_space=pl.ANY),) * 2,
        scratch_shapes=scratch,
        compiler_params=pltpu.CompilerParams(
            collective_id=0, has_side_effects=True, vmem_limit_bytes=56 * 1024 * 1024
        ),
    )(*operands)
    return pl.pallas_call(
        write_out,
        out_shape=tuple(jax.ShapeDtypeStruct(result.shape, result.dtype) for result in results),
        in_specs=[pl.BlockSpec(memory_space=pltpu.VMEM)] * 2,
        out_specs=(pl.BlockSpec(memory_space=pltpu.VMEM),) * 2,
        compiler_params=pltpu.CompilerParams(vmem_limit_bytes=60 * 1024 * 1024),
    )(*results)


def solution(mesh):
    placed = (
        P(None, "gx", "gy", None),
        P(None, "gx", "gy", None),
        P(None, None, None, "gx", "gy", None),
        P(None, None, "gx", "gy", None),
        P("gx", "gy", None),
        P(None, ("gx", "gy")),
        P(None, None, ("gx", "gy")),
        P(None, ("gx", "gy")),
        P(None, ("gx", "gy")),
        P(None, ("gx", "gy")),
        P(("gx", "gy")),
        P("gy", "gx"),
    )
    return jax.shard_map(
        functools.partial(body, mesh.shape["gx"], mesh.shape["gy"]),
        mesh=mesh,
        in_specs=placed,
        out_specs=(P(None, "gx", "gy", None), P(None, ("gx", "gy"))),
        check_vma=False,
    )
```

```python
import functools

import jax
import jax.numpy as jnp
from jax import lax
from jax.experimental import pallas as pl
from jax.experimental.pallas import tpu as pltpu
from jax.sharding import PartitionSpec as P

MESH = pl.DeviceIdType.MESH
F32 = jnp.float32
BF16 = jnp.bfloat16

FX = 8
FY = 8
NZ = 512
K = 27
A1 = 1024
H = 256
LANES = 128
GROUP = 512
HALF = 256
WIDE = 2
FIELDS = 6

damping = 0.6
smoothing = 0.5


def lane_gather(table, index):
    dims = lax.GatherDimensionNumbers(
        offset_dims=(),
        collapsed_slice_dims=(1,),
        start_index_map=(1,),
        operand_batching_dims=(0,),
        start_indices_batching_dims=(0,),
    )
    return lax.gather(
        table, index[..., None], dims, slice_sizes=(1, 1), mode=lax.GatherScatterMode.PROMISE_IN_BOUNDS
    )


def pick(tables, index):
    low = index & (LANES - 1)
    parts = [lane_gather(table, low) for table in tables]
    bit = LANES
    while len(parts) > 1:
        upper = (index & bit) != 0
        parts = [jnp.where(upper, parts[at + 1], parts[at]) for at in range(0, len(parts), 2)]
        bit *= 2
    return parts[0]


def rows_of(piece, rows):
    sub = lax.broadcasted_iota(jnp.int32, (rows, 1), 0)
    first, last = (8 * piece) // 6, min((8 * piece + 7) // 6, 5)
    i = jnp.where(sub < 6 * (first + 1) - 8 * piece, first, last)
    return i, 8 * piece + sub - 6 * i


def kernel(
    nx,
    ny,
    rhs_h,
    stf_h,
    cpl_h,
    ten_h,
    mem_h,
    cst_h,
    ccp_h,
    col_h,
    snd_h,
    ctn_h,
    cmb_h,
    inv_h,
    sol,
    csol,
    rhs,
    stf,
    cpl,
    ten,
    mem,
    cst,
    ccp,
    col,
    snd,
    ctn,
    cmb,
    inv,
    wgt,
    field,
    yout,
    yin,
    hout,
    hin,
    wout,
    win,
    acc,
    resid,
    nodes,
    crhs,
    y2,
    ext,
    cout,
    cacc,
    lift1,
    lout,
    invs,
    ohm,
    ohc,
    own_row,
    rows,
    part_row,
    parts,
    wave,
    load_sem,
    fsend,
    frecv,
    csend,
    crecv,
    gsend,
    grecv,
    psend,
    precv,
):
    gx, gy = lax.axis_index("gx"), lax.axis_index("gy")
    near = (
        (gx > 0, {"gx": jnp.maximum(gx - 1, 0), "gy": gy}),
        (gx < nx - 1, {"gx": jnp.minimum(gx + 1, nx - 1), "gy": gy}),
        (gy > 0, {"gx": gx, "gy": jnp.maximum(gy - 1, 0)}),
        (gy < ny - 1, {"gx": gx, "gy": jnp.minimum(gy + 1, ny - 1)}),
    )

    barrier = pltpu.get_barrier_semaphore()

    def tell(semaphore, steps):
        for device in (
            {"gx": lax.rem(gx + nx - steps, nx), "gy": gy},
            {"gx": lax.rem(gx + steps, nx), "gy": gy},
            {"gx": gx, "gy": lax.rem(gy + ny - steps, ny)},
            {"gx": gx, "gy": lax.rem(gy + steps, ny)},
        ):
            pl.semaphore_signal(semaphore, inc=1, device_id=device, device_id_type=MESH)

    def announce(number):
        if 2 << number < nx:
            tell(wave.at[number], 1 << number)

    def heard(number):
        if 2 << number < nx:
            pl.semaphore_wait(wave.at[number], 4)

    if nx > 1:
        tell(barrier, 1)

    loads = {}
    pairs = [("rhs", rhs_h, rhs), ("stf", stf_h, stf), ("mem", mem_h, mem)]
    for offset in (0, 5, 6, 1, 2, 3, 4):
        pairs.append(("cpl%d" % offset, cpl_h.at[pl.ds(9 * offset, 9)], cpl.at[pl.ds(9 * offset, 9)]))
    pairs += [
        ("snd", snd_h, snd),
        ("ctn", ctn_h, ctn),
        ("cmb", cmb_h, cmb),
        ("col", col_h, col),
        ("ten", ten_h, ten),
        ("cst", cst_h, cst),
        ("ccp", ccp_h, ccp),
        ("inv", inv_h, inv),
    ]
    for number, (name, source, target) in enumerate(pairs):
        loads[name] = pltpu.make_async_copy(source, target, load_sem.at[number])
        loads[name].start()

    def layer_out(number, side):
        return wout.at[number, side] if number < WIDE else hout.at[number - WIDE, side]

    def layer_in(number, side):
        return win.at[number, side] if number < WIDE else hin.at[number - WIDE, side]

    for side, (there, _) in enumerate(near):

        @pl.when(jnp.logical_not(there))
        def _():
            for number in range(FIELDS):
                target = layer_in(number, side)
                target[...] = jnp.zeros(target.shape, target.dtype)
            ext[0, :, pl.ds(A1 + H * side, H)] = jnp.zeros((8, H), F32)
            lift1[:, pl.ds(A1 + H * side, H)] = jnp.zeros((40, H), F32)
            if side < 2:
                parts[2 * side] = jnp.zeros(parts.shape[1:], F32)

    cacc[pl.ds(32, 8), :] = jnp.zeros((8, A1 + 4 * H), F32)
    own_row[...] = jnp.zeros_like(own_row)
    part_row[...] = jnp.zeros_like(part_row)

    def halo(number, side):
        return pltpu.make_async_remote_copy(
            src_ref=layer_out(number, side),
            dst_ref=layer_in(number, side ^ 1),
            send_sem=fsend.at[number, side],
            recv_sem=frecv.at[number, side ^ 1],
            device_id=near[side][1],
            device_id_type=MESH,
        )

    def pack(number, side, c, value):
        target = layer_out(number, side)
        target[c] = jnp.concatenate([value[:, : NZ // 2], value[:, NZ // 2 :]], axis=0).astype(target.dtype)

    def received(number, side, j):
        value = layer_in(number, side)[j].astype(F32)
        return jnp.concatenate([value[:8], value[8:]], axis=1)

    def send_halo(number, side):
        @pl.when(near[side][0])
        def _():
            halo(number, side).start()

    def wait_halo(number):
        for side in range(4):

            @pl.when(near[side][0])
            def _():
                halo(number, side ^ 1).wait_recv()

        for side in range(2):
            for j in range(3):
                yin[side, j] = received(number, side + 2, j)

    def put_field(number, x, values):
        for c in range(3):
            field[number, c, x] = values[c]
            yout[0, c, pl.ds(x, 1), :] = values[c][0:1, :]
            yout[1, c, pl.ds(x, 1), :] = values[c][FY - 1 : FY, :]
            if isinstance(x, int) and x == 0:
                pack(number, 0, c, values[c])
            if isinstance(x, int) and x == FX - 1:
                pack(number, 1, c, values[c])

    def slabs(number, slab):
        slab(0)
        if number is not None:
            send_halo(number, 0)
        slab(FX - 1)
        if number is not None:
            send_halo(number, 1)

        def inner(x, carry):
            slab(x)
            return carry

        lax.fori_loop(1, FX - 1, inner, 0)
        if number is not None:
            for side in range(2):
                for c in range(3):
                    pack(number, side + 2, c, yout[side, c])
                send_halo(number, side + 2)

    def add(total, offset, x, j, view):
        for i in range(3):
            total[i] = total[i] + cpl[9 * offset + 3 * i + j, x].astype(F32) * view

    def inside(number):
        lane = lax.broadcasted_iota(jnp.int32, (FY, NZ), 1)

        def slab(x):
            total = [stf[i, x] * field[number, i, x] for i in range(3)]
            for j in range(3):
                view = field[number, j, x]
                add(total, 0, x, j, view)
                add(total, 5, x, j, jnp.where(lane == 0, 0.0, pltpu.roll(view, 1, axis=1)))
                add(total, 6, x, j, jnp.where(lane == NZ - 1, 0.0, pltpu.roll(view, NZ - 1, axis=1)))
                if not (isinstance(x, int) and x == 0):
                    add(total, 1, x, j, field[number, j, x - 1])
                if not (isinstance(x, int) and x == FX - 1):
                    add(total, 2, x, j, field[number, j, x + 1])
            for i in range(3):
                acc[i, x] = total[i]

        slabs(None, slab)

    def outside(number, x):
        row = lax.broadcasted_iota(jnp.int32, (FY, NZ), 0)
        total = [acc[i, x] for i in range(3)]
        for j in range(3):
            view = field[number, j, x]
            below = yin[0, j, pl.ds(x, 1), :]
            above = yin[1, j, pl.ds(x, 1), :]
            add(total, 3, x, j, jnp.where(row == 0, below, pltpu.roll(view, 1, axis=0)))
            add(total, 4, x, j, jnp.where(row == FY - 1, above, pltpu.roll(view, FY - 1, axis=0)))
            if isinstance(x, int) and x == 0:
                add(total, 1, x, j, received(number, 0, j))
            if isinstance(x, int) and x == FX - 1:
                add(total, 2, x, j, received(number, 1, j))
        return total

    def coarse_halo(number, side):
        span = pl.ds(A1 + H * side, H)
        return pltpu.make_async_remote_copy(
            src_ref=lout.at[side] if number else cout.at[side],
            dst_ref=lift1.at[:, span] if number else ext.at[0, :, span],
            send_sem=csend.at[number, side],
            recv_sem=crecv.at[number, side],
            device_id=near[side ^ 1][1],
            device_id_type=MESH,
        )

    def wait_coarse(number):
        for side in range(4):

            @pl.when(near[side][0])
            def _():
                coarse_halo(number, side).wait_recv()

    def send_lift():
        lift1[pl.ds(0, 32), pl.ds(0, A1)] = ctn[pl.ds(0, 32), :]
        members = jnp.broadcast_to(cmb[...].astype(F32), (4, A1))
        lift1[pl.ds(32, 8), pl.ds(0, A1)] = jnp.concatenate([ctn[pl.ds(32, 4), :], members], axis=0)

        def one(piece, carry):
            rows8 = pl.ds(pl.multiple_of(8 * piece, 8), 8)
            tables = [lift1[rows8, pl.ds(LANES * h, LANES)] for h in range(A1 // LANES)]
            for side in range(4):
                for t in range(H // LANES):
                    span = pl.ds(LANES * t, LANES)
                    lout[side, rows8, span] = pick(tables, jnp.broadcast_to(snd[side : side + 1, span], (8, LANES)))
            return carry

        lax.fori_loop(0, 5, one, 0)
        for side in range(4):

            @pl.when(near[side ^ 1][0])
            def _():
                coarse_halo(1, side).start()

    loads["rhs"].wait()
    loads["stf"].wait()

    def first(x):
        values = []
        for c in range(3):
            weight = 1.0 / stf[c, x]
            wgt[c, x] = weight
            values.append(damping * rhs[c, x] * weight)
        put_field(0, x, values)

    if nx > 1:
        pl.semaphore_wait(barrier, 4)
    announce(0)
    slabs(0, first)

    count = lax.broadcasted_iota(jnp.int32, (16, NZ), 0).astype(F32).astype(BF16)

    def one_hot(index):
        width = index.shape[1]
        low = jnp.broadcast_to(index & (LANES - 1), (16, width)).astype(F32).astype(BF16)
        one, zero = jnp.ones((16, width), BF16), jnp.zeros((16, width), BF16)
        return jnp.concatenate(
            [jnp.where(low == count[:, :width] + float(16 * k), one, zero) for k in range(8)], axis=0
        )

    def hot_members(x, carry):
        for y in range(FY):
            ohm[x, :, pl.ds(NZ * y, NZ)] = one_hot(mem[x, pl.ds(y, 1), :])
        return carry

    def hot_columns(t, carry):
        span = pl.ds(pl.multiple_of(GROUP * t, GROUP), GROUP)
        columns = col[:, span]
        for k in range(K):
            ohc[k, :, span] = one_hot(columns[k : k + 1])
        return carry

    def choose(parts, index):
        bit = LANES
        while len(parts) > 1:
            upper = (index & bit) != 0
            parts = [jnp.where(upper, parts[at + 1], parts[at]) for at in range(0, len(parts), 2)]
            bit *= 2
        return parts[0]

    def table(values):
        pieces = [values[:, LANES * h : LANES * (h + 1)] for h in range(values.shape[1] // LANES)]
        value = jnp.concatenate(pieces, axis=0)
        rounded = value.astype(BF16).astype(F32)
        return jnp.concatenate([rounded, value - rounded], axis=1).astype(BF16)

    def look_up(entries, hot, index):
        product = jnp.dot(entries, jnp.concatenate([hot, hot], axis=0), preferred_element_type=F32)
        pieces = [product[8 * h : 8 * h + 8] for h in range(product.shape[0] // 8)]
        return choose(pieces, jnp.broadcast_to(index, (8, index.shape[1])))

    loads["mem"].wait()
    lax.fori_loop(0, FX, hot_members, 0)

    for offset in (0, 5, 6, 1, 2, 3, 4):
        loads["cpl%d" % offset].wait()

    def smoothed(number, x):
        total = outside(number, x)
        return [
            field[number, c, x] + damping * (rhs[c, x] - total[c]) * wgt[c, x] for c in range(3)
        ]

    inside(0)
    heard(0)
    announce(1)
    wait_halo(0)
    slabs(1, lambda x: put_field(1, x, smoothed(0, x)))

    def residual(x):
        total = outside(1, x)
        values = []
        for c in range(3):
            left = rhs[c, x] - total[c]
            resid[c, x] = left
            values.append(left * wgt[c, x])
        put_field(2, x, values)

    loads["snd"].wait()
    loads["ctn"].wait()
    loads["cmb"].wait()
    send_lift()
    inside(1)
    heard(1)
    announce(2)
    wait_halo(1)
    slabs(2, residual)

    loads["ten"].wait()

    def restrict(x):
        total = outside(2, x)
        filtered = [resid[i, x] - smoothing * total[i] for i in range(3)]
        for c in range(6):
            value = ten[c, x].astype(F32) * filtered[0]
            for i in range(1, 3):
                value = value + ten[6 * i + c, x].astype(F32) * filtered[i]
            for t in range(NZ // LANES):
                part = value[:, LANES * t : LANES * (t + 1)]
                nodes[x, t, pl.ds(8 * c, 8), :] = part
                if c < 2:
                    nodes[x, t, pl.ds(8 * (c + 6), 8), :] = part

    loads["inv"].wait()
    whole = inv[...]
    rounded = whole.astype(BF16)
    invs[0] = rounded
    invs[1] = (whole - rounded.astype(F32)).astype(BF16)
    inside(2)
    heard(2)
    wait_halo(2)
    wait_coarse(1)
    slabs(None, restrict)

    def sums(x, total):
        for y in range(FY):
            value = jnp.concatenate(
                [nodes[x, t, pl.ds(y, 8, stride=8), :] for t in range(NZ // LANES)], axis=1
            )
            rounded = value.astype(BF16).astype(F32)
            both = jnp.concatenate([rounded, value - rounded], axis=0).astype(BF16)
            index = jnp.broadcast_to(mem[x, pl.ds(y, 1), :], (16, NZ))
            high = lax.shift_right_logical(index, 7).astype(F32).astype(BF16)
            zero = jnp.zeros((16, NZ), BF16)
            left = jnp.concatenate([jnp.where(high == float(h), both, zero) for h in range(8)], axis=0)
            right = ohm[x, :, pl.ds(NZ * y, NZ)]
            total = total + lax.dot_general(
                left, right, (((1,), (1,)), ((), ())), preferred_element_type=F32
            )
        return total

    gathered = lax.fori_loop(0, FX, sums, jnp.zeros((LANES, LANES), F32))

    loads["cst"].wait()
    for h in range(8):
        span = pl.ds(LANES * h, LANES)
        crhs[:, span] = gathered[16 * h : 16 * h + 8] + gathered[16 * h + 8 : 16 * h + 16]
    cst8 = jnp.concatenate([cst[...], cst[0:2, :]], axis=0)
    ext[0, :, pl.ds(0, A1)] = damping * crhs[...] / cst8

    def send_coarse():
        tables = [ext[0, :, pl.ds(LANES * h, LANES)] for h in range(A1 // LANES)]
        for side in range(4):
            for t in range(H // LANES):
                index = jnp.broadcast_to(snd[side : side + 1, pl.ds(LANES * t, LANES)], (8, LANES))
                cout[side, :, pl.ds(LANES * t, LANES)] = pick(tables, index)

            @pl.when(near[side ^ 1][0])
            def _():
                coarse_halo(0, side).start()

    sub = lax.broadcasted_iota(jnp.int32, (8, GROUP), 0)

    def coarse_apply(number):
        entries = table(ext[number])

        def group(t, carry):
            span = pl.ds(pl.multiple_of(GROUP * t, GROUP), GROUP)
            total = [jnp.zeros((8 if piece < 4 else 4, GROUP), F32) for piece in range(5)]
            columns = col[:, span]
            for k in range(K):
                base = look_up(entries, ohc[k, :, span], columns[k : k + 1])
                up2, by4, down2 = (pltpu.roll(base, by, axis=0) for by in (6, 4, 2))
                turned = (base, jnp.where(sub < 6, up2, by4), jnp.where(sub < 2, by4, down2))
                for piece in range(5):
                    size = 8 if piece < 4 else 4
                    block = ccp[k, pl.ds(8 * piece, size), span]
                    total[piece] = total[piece] + block * turned[piece % 3][:size]
            for piece in range(5):
                cacc[pl.ds(8 * piece, 8 if piece < 4 else 4), span] = total[piece]
            return carry

        lax.fori_loop(0, A1 // GROUP, group, 0)

    fold_row = lax.broadcasted_iota(jnp.int32, (8, 40), 0)
    fold_col = lax.broadcasted_iota(jnp.int32, (8, 40), 1)
    fold_row = jnp.where(fold_row < 6, fold_row, fold_row - 6)
    fold = jnp.logical_and(fold_col >= 6 * fold_row, fold_col < 6 * fold_row + 6).astype(F32)

    fold = fold.astype(BF16)

    def fold_rows(values):
        rounded = values.astype(BF16)
        rest = (values - rounded.astype(F32)).astype(BF16)
        return jnp.dot(fold, rounded, preferred_element_type=F32) + jnp.dot(fold, rest, preferred_element_type=F32)

    def folded():
        return fold_rows(cacc[:, pl.ds(0, A1)])

    send_coarse()
    loads["col"].wait()
    lax.fori_loop(0, A1 // GROUP, hot_columns, 0)
    loads["ccp"].wait()
    wait_coarse(0)
    coarse_apply(0)
    s1 = crhs[...] - (cst8 * ext[0, :, pl.ds(0, A1)] + folded())

    lane = lax.broadcasted_iota(jnp.int32, (1, 2 * LANES), 1)
    upper = cmb[...] != 0
    row = jnp.zeros((1, 2 * LANES), F32)
    for piece in range(5):
        size = 8 if piece < 4 else 4
        i, c = rows_of(piece, size)
        first_i, last_i = (8 * piece) // 6, min((8 * piece + 7) // 6, 5)
        matching = jnp.where(i == first_i, s1[first_i : first_i + 1], s1[last_i : last_i + 1])
        product = ctn[pl.ds(8 * piece, size), :] * matching
        for a in range(2):
            kept = jnp.where(upper, product, 0.0) if a else jnp.where(upper, 0.0, product)
            total = jnp.sum(kept, axis=1, keepdims=True)
            place = 12 * gy + 2 * c + a
            row = row + jnp.sum(jnp.where(lane == place, total, 0.0), axis=0, keepdims=True)
    own_row[...] = row

    def to_row(step):
        other = lax.rem(gy + step, ny)
        return pltpu.make_async_remote_copy(
            src_ref=own_row,
            dst_ref=rows.at[gy],
            send_sem=gsend.at[other],
            recv_sem=grecv.at[gy],
            device_id={"gx": gx, "gy": other},
            device_id_type=MESH,
        )

    def from_row(other):
        return pltpu.make_async_remote_copy(
            src_ref=own_row,
            dst_ref=rows.at[other],
            send_sem=gsend.at[other],
            recv_sem=grecv.at[other],
            device_id={"gx": gx, "gy": other},
            device_id_type=MESH,
        )

    for step in range(1, ny):
        to_row(step).start()
    for step in range(1, ny):
        from_row(lax.rem(gy + step, ny)).wait_recv()
    rows[gy] = row
    entries = jnp.sum(rows[...], axis=0)
    block = inv.shape[1]
    values = entries[:, :block]
    rounded = values.astype(BF16).astype(F32)
    values = jnp.concatenate(
        [jnp.broadcast_to(rounded, (8, block)), jnp.broadcast_to(values - rounded, (8, block))], axis=0
    ).astype(BF16)
    upper_part, lower_part = (
        lax.dot_general(values, invs[at], (((1,), (1,)), ((), ())), preferred_element_type=F32) for at in range(2)
    )
    product = upper_part[0:1] + (upper_part[8:9] + lower_part[0:1] + lower_part[8:9])
    part_row[:, pl.ds(0, block)] = product

    def part(at, row_of, semaphore, device):
        return pltpu.make_async_remote_copy(
            src_ref=part_row,
            dst_ref=parts.at[at, row_of],
            send_sem=psend.at[at, semaphore],
            recv_sem=precv.at[at, row_of],
            device_id=device,
            device_id_type=MESH,
        )

    def to_part(at, step):
        other = lax.rem(gy + step, ny)
        return part(at, gx, step, {"gx": jnp.clip(gy + 1 - at, 0, nx - 1), "gy": other})

    def from_part(at, step):
        other = lax.rem(gx + step, nx)
        return part(at, other, 0, {"gx": other, "gy": jnp.clip(gx + at - 1, 0, ny - 1)})

    for at in (1, 0, 2):
        target, held = gy + 1 - at, gx + at - 1

        @pl.when(jnp.logical_and(target >= 0, target < nx))
        def _():
            for step in range(1, ny):
                to_part(at, step).start()

            @pl.when(gx != target)
            def _():
                to_part(at, 0).start()

            @pl.when(gx == target)
            def _():
                parts[at, gx] = part_row[...]

    for at in (1, 0, 2):
        target, held = gy + 1 - at, gx + at - 1

        @pl.when(jnp.logical_and(held >= 0, held < ny))
        def _():
            for step in range(1, nx):
                from_part(at, step).wait_recv()

            @pl.when(gy != held)
            def _():
                from_part(at, 0).wait_recv()

    coarsest = [jnp.sum(parts[at], axis=0) for at in range(3)]

    places = (
        (0, A1, 1, gy),
        (A1, H, 0, gy),
        (A1 + H, H, 2, gy),
        (A1 + 2 * H, H, 1, gy - 1),
        (A1 + 3 * H, H, 1, gy + 1),
    )
    for start, length, at, owner in places:
        span = pl.ds(start, length)
        one = lift1[36:37, span] != 0.0
        for piece in range(5):
            size = 8 if piece < 4 else 4
            _, c = rows_of(piece, size)
            spread = [
                jnp.sum(jnp.where(lane == 12 * owner + 2 * c + a, coarsest[at], 0.0), axis=1, keepdims=True)
                for a in range(2)
            ]
            here = pl.ds(8 * piece, size)
            cacc[here, span] = lift1[here, span] * jnp.where(one, spread[1], spread[0])
    ext[1] = ext[0] + fold_rows(cacc[...])
    coarse_apply(1)
    solved = ext[1, :, pl.ds(0, A1)]
    solved = solved + damping * (crhs[...] - (cst8 * solved + folded())) / cst8
    y2[...] = solved
    csol[...] = solved[0:6]

    entries = table(y2[...])
    tables = [y2[:, pl.ds(LANES * h, LANES)] for h in range(A1 // LANES)]

    def lift(x):
        for y in range(FY):
            taken = look_up(entries, ohm[x, :, pl.ds(NZ * y, HALF)], mem[x, pl.ds(y, 1), pl.ds(0, HALF)])
            for t in range(NZ // LANES):
                if t < HALF // LANES:
                    value = taken[:, LANES * t : LANES * (t + 1)]
                else:
                    index = mem[x, pl.ds(y, 1), pl.ds(LANES * t, LANES)]
                    value = pick(tables, jnp.broadcast_to(index, (8, LANES)))
                nodes[x, t, pl.ds(y, 8, stride=8), :] = value
        values = []
        for i in range(3):
            value = 0.0
            for c in range(6):
                taken = jnp.concatenate(
                    [nodes[x, t, pl.ds(8 * c, 8), :] for t in range(NZ // LANES)], axis=1
                )
                value = value + ten[6 * i + c, x].astype(F32) * taken
            values.append(value)
        put_field(3, x, values)

    slabs(3, lift)

    def corrected(x):
        total = outside(3, x)
        put_field(
            4,
            x,
            [
                field[1, c, x] + field[3, c, x] - smoothing * total[c] * wgt[c, x]
                for c in range(3)
            ],
        )

    inside(3)
    wait_halo(3)
    slabs(4, corrected)

    inside(4)
    wait_halo(4)
    slabs(5, lambda x: put_field(5, x, smoothed(4, x)))

    def last(x):
        values = smoothed(5, x)
        for c in range(3):
            sol[c, x] = values[c]

    inside(5)
    wait_halo(5)
    slabs(None, last)

    for side in range(4):

        @pl.when(near[side][0])
        def _():
            for number in range(FIELDS):
                halo(number, side).wait_send()
            for number in range(2):
                coarse_halo(number, side ^ 1).wait_send()

    for step in range(1, ny):
        to_row(step).wait_send()
    for at in range(3):
        target = gy + 1 - at

        @pl.when(jnp.logical_and(target >= 0, target < nx))
        def _():
            for step in range(1, ny):
                to_part(at, step).wait_send()

            @pl.when(gx != target)
            def _():
                to_part(at, 0).wait_send()


def write_out(sol, csol, sol_h, csol_h, sem):
    copies = [pltpu.make_async_copy(sol, sol_h, sem.at[0]), pltpu.make_async_copy(csol, csol_h, sem.at[1])]
    for copy in copies:
        copy.start()
    for copy in copies:
        copy.wait()


def body(nx, ny, rhs, stiffness, couplings, tentative, members, cst, ccp, col, snd, ctn, cmb, inv):
    couplings = couplings.reshape(63, FX, FY, NZ)
    tentative = tentative.reshape(18, FX, FY, NZ)
    cmb = cmb.reshape(1, A1)
    operands = (rhs, stiffness, couplings, tentative, members, cst, ccp, col, snd, ctn, cmb, inv)
    dma = pltpu.SemaphoreType.DMA
    scratch = [pltpu.VMEM(operand.shape, operand.dtype) for operand in operands]
    scratch += [
        pltpu.VMEM((3, FX, FY, NZ), F32),
        pltpu.VMEM((FIELDS, 3, FX, FY, NZ), F32),
        pltpu.VMEM((2, 3, FX, NZ), F32),
        pltpu.VMEM((2, 3, FX, NZ), F32),
        pltpu.VMEM((FIELDS - WIDE, 4, 3, 16, NZ // 2), BF16),
        pltpu.VMEM((FIELDS - WIDE, 4, 3, 16, NZ // 2), BF16),
        pltpu.VMEM((WIDE, 4, 3, 16, NZ // 2), F32),
        pltpu.VMEM((WIDE, 4, 3, 16, NZ // 2), F32),
        pltpu.VMEM((3, FX, FY, NZ), F32),
        pltpu.VMEM((3, FX, FY, NZ), F32),
        pltpu.VMEM((FX, NZ // LANES, 8 * FY, LANES), F32),
        pltpu.VMEM((8, A1), F32),
        pltpu.VMEM((8, A1), F32),
        pltpu.VMEM((2, 8, A1 + 4 * H), F32),
        pltpu.VMEM((4, 8, H), F32),
        pltpu.VMEM((40, A1 + 4 * H), F32),
        pltpu.VMEM((40, A1 + 4 * H), F32),
        pltpu.VMEM((4, 40, H), F32),
        pltpu.VMEM((2, *inv.shape), BF16),
        pltpu.VMEM((FX, LANES, FY * NZ), BF16),
        pltpu.VMEM((K, LANES, A1), BF16),
        pltpu.VMEM((1, 2 * LANES), F32),
        pltpu.VMEM((ny, 1, 2 * LANES), F32),
        pltpu.VMEM((1, 2 * LANES), F32),
        pltpu.VMEM((3, nx, 1, 2 * LANES), F32),
        pltpu.SemaphoreType.REGULAR((3,)),
        dma((18,)),
        dma((FIELDS, 4)),
        dma((FIELDS, 4)),
        dma((2, 4)),
        dma((2, 4)),
        dma((ny,)),
        dma((ny,)),
        dma((3, ny)),
        dma((3, nx)),
    ]
    results = pl.pallas_call(
        functools.partial(kernel, nx, ny),
        out_shape=(pltpu.VMEM((3, FX, FY, NZ), F32), pltpu.VMEM((6, A1), F32)),
        in_specs=[pl.BlockSpec(memory_space=pl.ANY)] * len(operands),
        out_specs=(pl.BlockSpec(memory_space=pltpu.VMEM),) * 2,
        scratch_shapes=scratch,
        compiler_params=pltpu.CompilerParams(
            collective_id=0, has_side_effects=True, vmem_limit_bytes=56 * 1024 * 1024
        ),
    )(*operands)
    return pl.pallas_call(
        write_out,
        out_shape=tuple(jax.ShapeDtypeStruct(result.shape, result.dtype) for result in results),
        in_specs=[pl.BlockSpec(memory_space=pltpu.VMEM)] * 2,
        out_specs=(pl.BlockSpec(memory_space=pl.ANY),) * 2,
        scratch_shapes=[dma((2,))],
        compiler_params=pltpu.CompilerParams(vmem_limit_bytes=60 * 1024 * 1024),
    )(*[pltpu.with_memory_space_constraint(result, pltpu.VMEM) for result in results])


def solution(mesh):
    placed = (
        P(None, "gx", "gy", None),
        P(None, "gx", "gy", None),
        P(None, None, None, "gx", "gy", None),
        P(None, None, "gx", "gy", None),
        P("gx", "gy", None),
        P(None, ("gx", "gy")),
        P(None, None, ("gx", "gy")),
        P(None, ("gx", "gy")),
        P(None, ("gx", "gy")),
        P(None, ("gx", "gy")),
        P(("gx", "gy")),
        P("gy", "gx"),
    )
    return jax.shard_map(
        functools.partial(body, mesh.shape["gx"], mesh.shape["gy"]),
        mesh=mesh,
        in_specs=placed,
        out_specs=(P(None, "gx", "gy", None), P(None, ("gx", "gy"))),
        check_vma=False,
    )
```

```python
import functools

import jax
import jax.numpy as jnp
from jax import lax
from jax.experimental import pallas as pl
from jax.experimental.pallas import tpu as pltpu
from jax.sharding import PartitionSpec as P

MESH = pl.DeviceIdType.MESH
F32 = jnp.float32
BF16 = jnp.bfloat16

FX = 8
FY = 8
NZ = 512
K = 27
A1 = 1024
H = 256
LANES = 128
GROUP = 512
HALF = 256
WIDE = 2
FIELDS = 6

damping = 0.6
smoothing = 0.5


def lane_gather(table, index):
    dims = lax.GatherDimensionNumbers(
        offset_dims=(),
        collapsed_slice_dims=(1,),
        start_index_map=(1,),
        operand_batching_dims=(0,),
        start_indices_batching_dims=(0,),
    )
    return lax.gather(
        table, index[..., None], dims, slice_sizes=(1, 1), mode=lax.GatherScatterMode.PROMISE_IN_BOUNDS
    )


def pick(tables, index):
    low = index & (LANES - 1)
    parts = [lane_gather(table, low) for table in tables]
    bit = LANES
    while len(parts) > 1:
        upper = (index & bit) != 0
        parts = [jnp.where(upper, parts[at + 1], parts[at]) for at in range(0, len(parts), 2)]
        bit *= 2
    return parts[0]


def rows_of(piece, rows):
    sub = lax.broadcasted_iota(jnp.int32, (rows, 1), 0)
    first, last = (8 * piece) // 6, min((8 * piece + 7) // 6, 5)
    i = jnp.where(sub < 6 * (first + 1) - 8 * piece, first, last)
    return i, 8 * piece + sub - 6 * i


def kernel(
    nx,
    ny,
    rhs_h,
    stf_h,
    cpl_h,
    ten_h,
    mem_h,
    cst_h,
    ccp_h,
    col_h,
    snd_h,
    ctn_h,
    cmb_h,
    inv_h,
    sol,
    csol,
    rhs,
    stf,
    cpl,
    ten,
    mem,
    cst,
    ccp,
    col,
    snd,
    ctn,
    cmb,
    inv,
    wgt,
    field,
    yout,
    yin,
    hout,
    hin,
    wout,
    win,
    acc,
    resid,
    nodes,
    crhs,
    y2,
    ext,
    cout,
    cacc,
    lift1,
    lout,
    invs,
    ohm,
    ohc,
    own_row,
    rows,
    part_row,
    parts,
    wave,
    load_sem,
    fsend,
    frecv,
    csend,
    crecv,
    gsend,
    grecv,
    psend,
    precv,
):
    gx, gy = lax.axis_index("gx"), lax.axis_index("gy")
    near = (
        (gx > 0, {"gx": jnp.maximum(gx - 1, 0), "gy": gy}),
        (gx < nx - 1, {"gx": jnp.minimum(gx + 1, nx - 1), "gy": gy}),
        (gy > 0, {"gx": gx, "gy": jnp.maximum(gy - 1, 0)}),
        (gy < ny - 1, {"gx": gx, "gy": jnp.minimum(gy + 1, ny - 1)}),
    )

    barrier = pltpu.get_barrier_semaphore()

    def tell(semaphore, steps):
        for device in (
            {"gx": lax.rem(gx + nx - steps, nx), "gy": gy},
            {"gx": lax.rem(gx + steps, nx), "gy": gy},
            {"gx": gx, "gy": lax.rem(gy + ny - steps, ny)},
            {"gx": gx, "gy": lax.rem(gy + steps, ny)},
        ):
            pl.semaphore_signal(semaphore, inc=1, device_id=device, device_id_type=MESH)

    def announce(number):
        if 2 << number < nx:
            tell(wave.at[number], 1 << number)

    def heard(number):
        if 2 << number < nx:
            pl.semaphore_wait(wave.at[number], 4)

    if nx > 1:
        tell(barrier, 1)

    loads = {}
    pairs = [("rhs", rhs_h, rhs), ("stf", stf_h, stf), ("mem", mem_h, mem)]
    for offset in (0, 5, 6, 1, 2, 3, 4):
        pairs.append(("cpl%d" % offset, cpl_h.at[pl.ds(9 * offset, 9)], cpl.at[pl.ds(9 * offset, 9)]))
    pairs += [
        ("snd", snd_h, snd),
        ("ctn", ctn_h, ctn),
        ("cmb", cmb_h, cmb),
        ("col", col_h, col),
        ("ten", ten_h, ten),
        ("cst", cst_h, cst),
        ("ccp", ccp_h, ccp),
        ("inv", inv_h, inv),
    ]
    for number, (name, source, target) in enumerate(pairs):
        loads[name] = pltpu.make_async_copy(source, target, load_sem.at[number])
        loads[name].start()

    def layer_out(number, side):
        return wout.at[number, side] if number < WIDE else hout.at[number - WIDE, side]

    def layer_in(number, side):
        return win.at[number, side] if number < WIDE else hin.at[number - WIDE, side]

    for side, (there, _) in enumerate(near):

        @pl.when(jnp.logical_not(there))
        def _():
            for number in range(FIELDS):
                target = layer_in(number, side)
                target[...] = jnp.zeros(target.shape, target.dtype)
            ext[0, :, pl.ds(A1 + H * side, H)] = jnp.zeros((8, H), F32)
            lift1[:, pl.ds(A1 + H * side, H)] = jnp.zeros((40, H), F32)
            if side < 2:
                parts[2 * side] = jnp.zeros(parts.shape[1:], F32)

    cacc[pl.ds(32, 8), :] = jnp.zeros((8, A1 + 4 * H), F32)
    own_row[...] = jnp.zeros_like(own_row)
    part_row[...] = jnp.zeros_like(part_row)

    def halo(number, side):
        return pltpu.make_async_remote_copy(
            src_ref=layer_out(number, side),
            dst_ref=layer_in(number, side ^ 1),
            send_sem=fsend.at[number, side],
            recv_sem=frecv.at[number, side ^ 1],
            device_id=near[side][1],
            device_id_type=MESH,
        )

    def pack(number, side, c, value):
        target = layer_out(number, side)
        target[c] = jnp.concatenate([value[:, : NZ // 2], value[:, NZ // 2 :]], axis=0).astype(target.dtype)

    def received(number, side, j):
        value = layer_in(number, side)[j].astype(F32)
        return jnp.concatenate([value[:8], value[8:]], axis=1)

    def send_halo(number, side):
        @pl.when(near[side][0])
        def _():
            halo(number, side).start()

    def wait_halo(number):
        for side in range(4):

            @pl.when(near[side][0])
            def _():
                halo(number, side ^ 1).wait_recv()

        for side in range(2):
            for j in range(3):
                yin[side, j] = received(number, side + 2, j)

    def put_field(number, x, values):
        for c in range(3):
            field[number, c, x] = values[c]
            yout[0, c, pl.ds(x, 1), :] = values[c][0:1, :]
            yout[1, c, pl.ds(x, 1), :] = values[c][FY - 1 : FY, :]
            if isinstance(x, int) and x == 0:
                pack(number, 0, c, values[c])
            if isinstance(x, int) and x == FX - 1:
                pack(number, 1, c, values[c])

    def slabs(number, slab):
        slab(0)
        if number is not None:
            send_halo(number, 0)
        slab(FX - 1)
        if number is not None:
            send_halo(number, 1)

        def inner(x, carry):
            slab(x)
            return carry

        lax.fori_loop(1, FX - 1, inner, 0)
        if number is not None:
            for side in range(2):
                for c in range(3):
                    pack(number, side + 2, c, yout[side, c])
                send_halo(number, side + 2)

    def add(total, offset, x, j, view):
        for i in range(3):
            total[i] = total[i] + cpl[9 * offset + 3 * i + j, x].astype(F32) * view

    def inside(number):
        lane = lax.broadcasted_iota(jnp.int32, (FY, NZ), 1)

        def slab(x):
            total = [stf[i, x] * field[number, i, x] for i in range(3)]
            for j in range(3):
                view = field[number, j, x]
                add(total, 0, x, j, view)
                add(total, 5, x, j, jnp.where(lane == 0, 0.0, pltpu.roll(view, 1, axis=1)))
                add(total, 6, x, j, jnp.where(lane == NZ - 1, 0.0, pltpu.roll(view, NZ - 1, axis=1)))
                if not (isinstance(x, int) and x == 0):
                    add(total, 1, x, j, field[number, j, x - 1])
                if not (isinstance(x, int) and x == FX - 1):
                    add(total, 2, x, j, field[number, j, x + 1])
            for i in range(3):
                acc[i, x] = total[i]

        slabs(None, slab)

    def outside(number, x):
        row = lax.broadcasted_iota(jnp.int32, (FY, NZ), 0)
        total = [acc[i, x] for i in range(3)]
        for j in range(3):
            view = field[number, j, x]
            below = yin[0, j, pl.ds(x, 1), :]
            above = yin[1, j, pl.ds(x, 1), :]
            add(total, 3, x, j, jnp.where(row == 0, below, pltpu.roll(view, 1, axis=0)))
            add(total, 4, x, j, jnp.where(row == FY - 1, above, pltpu.roll(view, FY - 1, axis=0)))
            if isinstance(x, int) and x == 0:
                add(total, 1, x, j, received(number, 0, j))
            if isinstance(x, int) and x == FX - 1:
                add(total, 2, x, j, received(number, 1, j))
        return total

    def coarse_halo(number, side):
        span = pl.ds(A1 + H * side, H)
        return pltpu.make_async_remote_copy(
            src_ref=lout.at[side] if number else cout.at[side],
            dst_ref=lift1.at[:, span] if number else ext.at[0, :, span],
            send_sem=csend.at[number, side],
            recv_sem=crecv.at[number, side],
            device_id=near[side ^ 1][1],
            device_id_type=MESH,
        )

    def wait_coarse(number):
        for side in range(4):

            @pl.when(near[side][0])
            def _():
                coarse_halo(number, side).wait_recv()

    def send_lift():
        lift1[pl.ds(0, 32), pl.ds(0, A1)] = ctn[pl.ds(0, 32), :]
        members = jnp.broadcast_to(cmb[...].astype(F32), (4, A1))
        lift1[pl.ds(32, 8), pl.ds(0, A1)] = jnp.concatenate([ctn[pl.ds(32, 4), :], members], axis=0)

        def one(piece, carry):
            rows8 = pl.ds(pl.multiple_of(8 * piece, 8), 8)
            tables = [lift1[rows8, pl.ds(LANES * h, LANES)] for h in range(A1 // LANES)]
            for side in range(4):
                for t in range(H // LANES):
                    span = pl.ds(LANES * t, LANES)
                    lout[side, rows8, span] = pick(tables, jnp.broadcast_to(snd[side : side + 1, span], (8, LANES)))
            return carry

        lax.fori_loop(0, 5, one, 0)
        for side in range(4):

            @pl.when(near[side ^ 1][0])
            def _():
                coarse_halo(1, side).start()

    loads["rhs"].wait()
    loads["stf"].wait()

    def first(x):
        values = []
        for c in range(3):
            weight = 1.0 / stf[c, x]
            wgt[c, x] = weight
            values.append(damping * rhs[c, x] * weight)
        put_field(0, x, values)

    if nx > 1:
        pl.semaphore_wait(barrier, 4)
    announce(0)
    slabs(0, first)

    count = lax.broadcasted_iota(jnp.int32, (16, NZ), 0).astype(F32).astype(BF16)

    def one_hot(index):
        width = index.shape[1]
        low = jnp.broadcast_to(index & (LANES - 1), (16, width)).astype(F32).astype(BF16)
        one, zero = jnp.ones((16, width), BF16), jnp.zeros((16, width), BF16)
        return jnp.concatenate(
            [jnp.where(low == count[:, :width] + float(16 * k), one, zero) for k in range(8)], axis=0
        )

    def hot_members(x, carry):
        for y in range(FY):
            ohm[x, :, pl.ds(NZ * y, NZ)] = one_hot(mem[x, pl.ds(y, 1), :])
        return carry

    def hot_columns(t, carry):
        span = pl.ds(pl.multiple_of(GROUP * t, GROUP), GROUP)
        columns = col[:, span]
        for k in range(K):
            ohc[k, :, span] = one_hot(columns[k : k + 1])
        return carry

    def choose(parts, index):
        bit = LANES
        while len(parts) > 1:
            upper = (index & bit) != 0
            parts = [jnp.where(upper, parts[at + 1], parts[at]) for at in range(0, len(parts), 2)]
            bit *= 2
        return parts[0]

    def table(values):
        pieces = [values[:, LANES * h : LANES * (h + 1)] for h in range(values.shape[1] // LANES)]
        value = jnp.concatenate(pieces, axis=0)
        rounded = value.astype(BF16).astype(F32)
        return jnp.concatenate([rounded, value - rounded], axis=1).astype(BF16)

    def look_up(entries, hot, index):
        product = jnp.dot(entries, jnp.concatenate([hot, hot], axis=0), preferred_element_type=F32)
        pieces = [product[8 * h : 8 * h + 8] for h in range(product.shape[0] // 8)]
        return choose(pieces, jnp.broadcast_to(index, (8, index.shape[1])))

    loads["mem"].wait()
    lax.fori_loop(0, FX, hot_members, 0)

    for offset in (0, 5, 6, 1, 2, 3, 4):
        loads["cpl%d" % offset].wait()

    def smoothed(number, x):
        total = outside(number, x)
        return [
            field[number, c, x] + damping * (rhs[c, x] - total[c]) * wgt[c, x] for c in range(3)
        ]

    inside(0)
    heard(0)
    announce(1)
    wait_halo(0)
    slabs(1, lambda x: put_field(1, x, smoothed(0, x)))

    def residual(x):
        total = outside(1, x)
        values = []
        for c in range(3):
            left = rhs[c, x] - total[c]
            resid[c, x] = left
            values.append(left * wgt[c, x])
        put_field(2, x, values)

    loads["snd"].wait()
    loads["ctn"].wait()
    loads["cmb"].wait()
    send_lift()
    inside(1)
    heard(1)
    announce(2)
    wait_halo(1)
    slabs(2, residual)

    loads["ten"].wait()

    def restrict(x):
        total = outside(2, x)
        filtered = [resid[i, x] - smoothing * total[i] for i in range(3)]
        for c in range(6):
            value = ten[c, x].astype(F32) * filtered[0]
            for i in range(1, 3):
                value = value + ten[6 * i + c, x].astype(F32) * filtered[i]
            for t in range(NZ // LANES):
                part = value[:, LANES * t : LANES * (t + 1)]
                nodes[x, t, pl.ds(8 * c, 8), :] = part
                if c < 2:
                    nodes[x, t, pl.ds(8 * (c + 6), 8), :] = part

    loads["inv"].wait()
    whole = inv[...]
    rounded = whole.astype(BF16)
    invs[0] = rounded
    invs[1] = (whole - rounded.astype(F32)).astype(BF16)
    inside(2)
    heard(2)
    wait_halo(2)
    wait_coarse(1)
    slabs(None, restrict)

    def sums(x, total):
        for y in range(FY):
            value = jnp.concatenate(
                [nodes[x, t, pl.ds(y, 8, stride=8), :] for t in range(NZ // LANES)], axis=1
            )
            rounded = value.astype(BF16).astype(F32)
            both = jnp.concatenate([rounded, value - rounded], axis=0).astype(BF16)
            index = jnp.broadcast_to(mem[x, pl.ds(y, 1), :], (16, NZ))
            high = lax.shift_right_logical(index, 7).astype(F32).astype(BF16)
            zero = jnp.zeros((16, NZ), BF16)
            left = jnp.concatenate([jnp.where(high == float(h), both, zero) for h in range(8)], axis=0)
            right = ohm[x, :, pl.ds(NZ * y, NZ)]
            total = total + lax.dot_general(
                left, right, (((1,), (1,)), ((), ())), preferred_element_type=F32
            )
        return total

    gathered = lax.fori_loop(0, FX, sums, jnp.zeros((LANES, LANES), F32))

    loads["cst"].wait()
    for h in range(8):
        span = pl.ds(LANES * h, LANES)
        crhs[:, span] = gathered[16 * h : 16 * h + 8] + gathered[16 * h + 8 : 16 * h + 16]
    cst8 = jnp.concatenate([cst[...], cst[0:2, :]], axis=0)
    ext[0, :, pl.ds(0, A1)] = damping * crhs[...] / cst8

    def send_coarse():
        tables = [ext[0, :, pl.ds(LANES * h, LANES)] for h in range(A1 // LANES)]
        for side in range(4):
            for t in range(H // LANES):
                index = jnp.broadcast_to(snd[side : side + 1, pl.ds(LANES * t, LANES)], (8, LANES))
                cout[side, :, pl.ds(LANES * t, LANES)] = pick(tables, index)

            @pl.when(near[side ^ 1][0])
            def _():
                coarse_halo(0, side).start()

    sub = lax.broadcasted_iota(jnp.int32, (8, GROUP), 0)

    def coarse_apply(number):
        entries = table(ext[number])

        def group(t, carry):
            span = pl.ds(pl.multiple_of(GROUP * t, GROUP), GROUP)
            total = [jnp.zeros((8 if piece < 4 else 4, GROUP), F32) for piece in range(5)]
            columns = col[:, span]
            for k in range(K):
                base = look_up(entries, ohc[k, :, span], columns[k : k + 1])
                up2, by4, down2 = (pltpu.roll(base, by, axis=0) for by in (6, 4, 2))
                turned = (base, jnp.where(sub < 6, up2, by4), jnp.where(sub < 2, by4, down2))
                for piece in range(5):
                    size = 8 if piece < 4 else 4
                    block = ccp[k, pl.ds(8 * piece, size), span]
                    total[piece] = total[piece] + block * turned[piece % 3][:size]
            for piece in range(5):
                cacc[pl.ds(8 * piece, 8 if piece < 4 else 4), span] = total[piece]
            return carry

        lax.fori_loop(0, A1 // GROUP, group, 0)

    fold_row = lax.broadcasted_iota(jnp.int32, (8, 40), 0)
    fold_col = lax.broadcasted_iota(jnp.int32, (8, 40), 1)
    fold_row = jnp.where(fold_row < 6, fold_row, fold_row - 6)
    fold = jnp.logical_and(fold_col >= 6 * fold_row, fold_col < 6 * fold_row + 6).astype(F32)

    fold = fold.astype(BF16)

    def fold_rows(values):
        rounded = values.astype(BF16)
        rest = (values - rounded.astype(F32)).astype(BF16)
        return jnp.dot(fold, rounded, preferred_element_type=F32) + jnp.dot(fold, rest, preferred_element_type=F32)

    def folded():
        return fold_rows(cacc[:, pl.ds(0, A1)])

    send_coarse()
    loads["col"].wait()
    lax.fori_loop(0, A1 // GROUP, hot_columns, 0)
    loads["ccp"].wait()
    wait_coarse(0)
    coarse_apply(0)
    s1 = crhs[...] - (cst8 * ext[0, :, pl.ds(0, A1)] + folded())

    lane = lax.broadcasted_iota(jnp.int32, (1, 2 * LANES), 1)
    upper = cmb[...] != 0
    row = jnp.zeros((1, 2 * LANES), F32)
    for piece in range(5):
        size = 8 if piece < 4 else 4
        i, c = rows_of(piece, size)
        first_i, last_i = (8 * piece) // 6, min((8 * piece + 7) // 6, 5)
        matching = jnp.where(i == first_i, s1[first_i : first_i + 1], s1[last_i : last_i + 1])
        product = ctn[pl.ds(8 * piece, size), :] * matching
        for a in range(2):
            kept = jnp.where(upper, product, 0.0) if a else jnp.where(upper, 0.0, product)
            total = jnp.sum(kept, axis=1, keepdims=True)
            place = 12 * gy + 2 * c + a
            row = row + jnp.sum(jnp.where(lane == place, total, 0.0), axis=0, keepdims=True)
    own_row[...] = row

    def to_row(step):
        other = lax.rem(gy + step, ny)
        return pltpu.make_async_remote_copy(
            src_ref=own_row,
            dst_ref=rows.at[gy],
            send_sem=gsend.at[other],
            recv_sem=grecv.at[gy],
            device_id={"gx": gx, "gy": other},
            device_id_type=MESH,
        )

    def from_row(other):
        return pltpu.make_async_remote_copy(
            src_ref=own_row,
            dst_ref=rows.at[other],
            send_sem=gsend.at[other],
            recv_sem=grecv.at[other],
            device_id={"gx": gx, "gy": other},
            device_id_type=MESH,
        )

    far_first = sorted(range(1, ny), key=lambda step: -min(step, ny - step))
    for step in far_first:
        to_row(step).start()
    for step in range(1, ny):
        from_row(lax.rem(gy + step, ny)).wait_recv()
    rows[gy] = row
    entries = jnp.sum(rows[...], axis=0)
    block = inv.shape[1]
    values = entries[:, :block]
    rounded = values.astype(BF16).astype(F32)
    values = jnp.concatenate(
        [jnp.broadcast_to(rounded, (8, block)), jnp.broadcast_to(values - rounded, (8, block))], axis=0
    ).astype(BF16)
    upper_part, lower_part = (
        lax.dot_general(values, invs[at], (((1,), (1,)), ((), ())), preferred_element_type=F32) for at in range(2)
    )
    product = upper_part[0:1] + (upper_part[8:9] + lower_part[0:1] + lower_part[8:9])
    part_row[:, pl.ds(0, block)] = product

    def part(at, row_of, semaphore, device):
        return pltpu.make_async_remote_copy(
            src_ref=part_row,
            dst_ref=parts.at[at, row_of],
            send_sem=psend.at[at, semaphore],
            recv_sem=precv.at[at, row_of],
            device_id=device,
            device_id_type=MESH,
        )

    def to_part(at, step):
        other = lax.rem(gy + step, ny)
        return part(at, gx, step, {"gx": jnp.clip(gy + 1 - at, 0, nx - 1), "gy": other})

    def from_part(at, step):
        other = lax.rem(gx + step, nx)
        return part(at, other, 0, {"gx": other, "gy": jnp.clip(gx + at - 1, 0, ny - 1)})

    for steps in (far_first[: ny // 2], far_first[ny // 2 :]):
        for at in (0, 2, 1):
            target = gy + 1 - at

            @pl.when(jnp.logical_and(target >= 0, target < nx))
            def _():
                for step in steps:
                    to_part(at, step).start()

    for at in (0, 2, 1):
        target = gy + 1 - at

        @pl.when(jnp.logical_and(target >= 0, target < nx))
        def _():
            @pl.when(gx != target)
            def _():
                to_part(at, 0).start()

            @pl.when(gx == target)
            def _():
                parts[at, gx] = part_row[...]

    for at in (1, 0, 2):
        held = gx + at - 1

        @pl.when(jnp.logical_and(held >= 0, held < ny))
        def _():
            for step in range(1, nx):
                from_part(at, step).wait_recv()

            @pl.when(gy != held)
            def _():
                from_part(at, 0).wait_recv()

    coarsest = [jnp.sum(parts[at], axis=0) for at in range(3)]

    places = (
        (0, A1, 1, gy),
        (A1, H, 0, gy),
        (A1 + H, H, 2, gy),
        (A1 + 2 * H, H, 1, gy - 1),
        (A1 + 3 * H, H, 1, gy + 1),
    )
    for start, length, at, owner in places:
        span = pl.ds(start, length)
        one = lift1[36:37, span] != 0.0
        for piece in range(5):
            size = 8 if piece < 4 else 4
            _, c = rows_of(piece, size)
            spread = [
                jnp.sum(jnp.where(lane == 12 * owner + 2 * c + a, coarsest[at], 0.0), axis=1, keepdims=True)
                for a in range(2)
            ]
            here = pl.ds(8 * piece, size)
            cacc[here, span] = lift1[here, span] * jnp.where(one, spread[1], spread[0])
    ext[1] = ext[0] + fold_rows(cacc[...])
    coarse_apply(1)
    solved = ext[1, :, pl.ds(0, A1)]
    solved = solved + damping * (crhs[...] - (cst8 * solved + folded())) / cst8
    y2[...] = solved
    csol[...] = solved[0:6]

    entries = table(y2[...])
    tables = [y2[:, pl.ds(LANES * h, LANES)] for h in range(A1 // LANES)]

    def lift(x):
        for y in range(FY):
            taken = look_up(entries, ohm[x, :, pl.ds(NZ * y, HALF)], mem[x, pl.ds(y, 1), pl.ds(0, HALF)])
            for t in range(NZ // LANES):
                if t < HALF // LANES:
                    value = taken[:, LANES * t : LANES * (t + 1)]
                else:
                    index = mem[x, pl.ds(y, 1), pl.ds(LANES * t, LANES)]
                    value = pick(tables, jnp.broadcast_to(index, (8, LANES)))
                nodes[x, t, pl.ds(y, 8, stride=8), :] = value
        values = []
        for i in range(3):
            value = 0.0
            for c in range(6):
                taken = jnp.concatenate(
                    [nodes[x, t, pl.ds(8 * c, 8), :] for t in range(NZ // LANES)], axis=1
                )
                value = value + ten[6 * i + c, x].astype(F32) * taken
            values.append(value)
        put_field(3, x, values)

    slabs(3, lift)

    def sent_halos(first_number, last_number):
        for side in range(4):

            @pl.when(near[side][0])
            def _():
                for number in range(first_number, last_number):
                    halo(number, side).wait_send()

    def sent_lists():
        for side in range(4):

            @pl.when(near[side][0])
            def _():
                for number in range(2):
                    coarse_halo(number, side ^ 1).wait_send()

        for step in range(1, ny):
            to_row(step).wait_send()

    def sent_parts():
        for at in range(3):
            target = gy + 1 - at

            @pl.when(jnp.logical_and(target >= 0, target < nx))
            def _():
                for step in range(1, ny):
                    to_part(at, step).wait_send()

                @pl.when(gx != target)
                def _():
                    to_part(at, 0).wait_send()

    def corrected(x):
        total = outside(3, x)
        put_field(
            4,
            x,
            [
                field[1, c, x] + field[3, c, x] - smoothing * total[c] * wgt[c, x]
                for c in range(3)
            ],
        )

    inside(3)
    wait_halo(3)
    slabs(4, corrected)

    inside(4)
    sent_lists()
    sent_halos(0, 4)
    wait_halo(4)
    slabs(5, lambda x: put_field(5, x, smoothed(4, x)))

    def last(x):
        values = smoothed(5, x)
        for c in range(3):
            sol[c, x] = values[c]

    inside(5)
    sent_parts()
    wait_halo(5)
    slabs(None, last)

    sent_halos(4, 6)


def write_out(sol, csol, sol_h, csol_h, sem):
    copies = [pltpu.make_async_copy(sol, sol_h, sem.at[0]), pltpu.make_async_copy(csol, csol_h, sem.at[1])]
    for copy in copies:
        copy.start()
    for copy in copies:
        copy.wait()


def body(nx, ny, rhs, stiffness, couplings, tentative, members, cst, ccp, col, snd, ctn, cmb, inv):
    couplings = couplings.reshape(63, FX, FY, NZ)
    tentative = tentative.reshape(18, FX, FY, NZ)
    cmb = cmb.reshape(1, A1)
    operands = (rhs, stiffness, couplings, tentative, members, cst, ccp, col, snd, ctn, cmb, inv)
    dma = pltpu.SemaphoreType.DMA
    scratch = [pltpu.VMEM(operand.shape, operand.dtype) for operand in operands]
    scratch += [
        pltpu.VMEM((3, FX, FY, NZ), F32),
        pltpu.VMEM((FIELDS, 3, FX, FY, NZ), F32),
        pltpu.VMEM((2, 3, FX, NZ), F32),
        pltpu.VMEM((2, 3, FX, NZ), F32),
        pltpu.VMEM((FIELDS - WIDE, 4, 3, 16, NZ // 2), BF16),
        pltpu.VMEM((FIELDS - WIDE, 4, 3, 16, NZ // 2), BF16),
        pltpu.VMEM((WIDE, 4, 3, 16, NZ // 2), F32),
        pltpu.VMEM((WIDE, 4, 3, 16, NZ // 2), F32),
        pltpu.VMEM((3, FX, FY, NZ), F32),
        pltpu.VMEM((3, FX, FY, NZ), F32),
        pltpu.VMEM((FX, NZ // LANES, 8 * FY, LANES), F32),
        pltpu.VMEM((8, A1), F32),
        pltpu.VMEM((8, A1), F32),
        pltpu.VMEM((2, 8, A1 + 4 * H), F32),
        pltpu.VMEM((4, 8, H), F32),
        pltpu.VMEM((40, A1 + 4 * H), F32),
        pltpu.VMEM((40, A1 + 4 * H), F32),
        pltpu.VMEM((4, 40, H), F32),
        pltpu.VMEM((2, *inv.shape), BF16),
        pltpu.VMEM((FX, LANES, FY * NZ), BF16),
        pltpu.VMEM((K, LANES, A1), BF16),
        pltpu.VMEM((1, 2 * LANES), F32),
        pltpu.VMEM((ny, 1, 2 * LANES), F32),
        pltpu.VMEM((1, 2 * LANES), F32),
        pltpu.VMEM((3, nx, 1, 2 * LANES), F32),
        pltpu.SemaphoreType.REGULAR((3,)),
        dma((18,)),
        dma((FIELDS, 4)),
        dma((FIELDS, 4)),
        dma((2, 4)),
        dma((2, 4)),
        dma((ny,)),
        dma((ny,)),
        dma((3, ny)),
        dma((3, nx)),
    ]
    results = pl.pallas_call(
        functools.partial(kernel, nx, ny),
        out_shape=(pltpu.VMEM((3, FX, FY, NZ), F32), pltpu.VMEM((6, A1), F32)),
        in_specs=[pl.BlockSpec(memory_space=pl.ANY)] * len(operands),
        out_specs=(pl.BlockSpec(memory_space=pltpu.VMEM),) * 2,
        scratch_shapes=scratch,
        compiler_params=pltpu.CompilerParams(
            collective_id=0, has_side_effects=True, vmem_limit_bytes=56 * 1024 * 1024
        ),
    )(*operands)
    return pl.pallas_call(
        write_out,
        out_shape=tuple(jax.ShapeDtypeStruct(result.shape, result.dtype) for result in results),
        in_specs=[pl.BlockSpec(memory_space=pltpu.VMEM)] * 2,
        out_specs=(pl.BlockSpec(memory_space=pl.ANY),) * 2,
        scratch_shapes=[dma((2,))],
        compiler_params=pltpu.CompilerParams(vmem_limit_bytes=60 * 1024 * 1024),
    )(*[pltpu.with_memory_space_constraint(result, pltpu.VMEM) for result in results])


def solution(mesh):
    placed = (
        P(None, "gx", "gy", None),
        P(None, "gx", "gy", None),
        P(None, None, None, "gx", "gy", None),
        P(None, None, "gx", "gy", None),
        P("gx", "gy", None),
        P(None, ("gx", "gy")),
        P(None, None, ("gx", "gy")),
        P(None, ("gx", "gy")),
        P(None, ("gx", "gy")),
        P(None, ("gx", "gy")),
        P(("gx", "gy")),
        P("gy", "gx"),
    )
    return jax.shard_map(
        functools.partial(body, mesh.shape["gx"], mesh.shape["gy"]),
        mesh=mesh,
        in_specs=placed,
        out_specs=(P(None, "gx", "gy", None), P(None, ("gx", "gy"))),
        check_vma=False,
    )
```

```python
import functools

import jax
import jax.numpy as jnp
from jax import lax
from jax.experimental import pallas as pl
from jax.experimental.pallas import tpu as pltpu
from jax.sharding import PartitionSpec as P

MESH = pl.DeviceIdType.MESH
F32 = jnp.float32
BF16 = jnp.bfloat16

FX = 8
FY = 8
NZ = 512
K = 27
A1 = 1024
H = 256
LANES = 128
GROUP = 512
HALF = 256
WIDE = 2
FIELDS = 6

damping = 0.6
smoothing = 0.5


def lane_gather(table, index):
    dims = lax.GatherDimensionNumbers(
        offset_dims=(),
        collapsed_slice_dims=(1,),
        start_index_map=(1,),
        operand_batching_dims=(0,),
        start_indices_batching_dims=(0,),
    )
    return lax.gather(
        table, index[..., None], dims, slice_sizes=(1, 1), mode=lax.GatherScatterMode.PROMISE_IN_BOUNDS
    )


def pick(tables, index):
    low = index & (LANES - 1)
    parts = [lane_gather(table, low) for table in tables]
    bit = LANES
    while len(parts) > 1:
        upper = (index & bit) != 0
        parts = [jnp.where(upper, parts[at + 1], parts[at]) for at in range(0, len(parts), 2)]
        bit *= 2
    return parts[0]


def rows_of(piece, rows):
    sub = lax.broadcasted_iota(jnp.int32, (rows, 1), 0)
    first, last = (8 * piece) // 6, min((8 * piece + 7) // 6, 5)
    i = jnp.where(sub < 6 * (first + 1) - 8 * piece, first, last)
    return i, 8 * piece + sub - 6 * i


def kernel(
    nx,
    ny,
    rhs_h,
    stf_h,
    cpl_h,
    ten_h,
    mem_h,
    cst_h,
    ccp_h,
    col_h,
    snd_h,
    ctn_h,
    cmb_h,
    inv_h,
    sol,
    csol,
    rhs,
    stf,
    cpl,
    ten,
    mem,
    cst,
    ccp,
    col,
    snd,
    ctn,
    cmb,
    inv,
    wgt,
    field,
    yout,
    yin,
    hout,
    hin,
    wout,
    win,
    acc,
    resid,
    nodes,
    crhs,
    y2,
    ext,
    cout,
    cacc,
    lift1,
    lout,
    invs,
    ohm,
    ohc,
    own_row,
    rows,
    part_row,
    parts,
    wave,
    load_sem,
    fsend,
    frecv,
    csend,
    crecv,
    gsend,
    grecv,
    psend,
    precv,
):
    gx, gy = lax.axis_index("gx"), lax.axis_index("gy")
    near = (
        (gx > 0, {"gx": jnp.maximum(gx - 1, 0), "gy": gy}),
        (gx < nx - 1, {"gx": jnp.minimum(gx + 1, nx - 1), "gy": gy}),
        (gy > 0, {"gx": gx, "gy": jnp.maximum(gy - 1, 0)}),
        (gy < ny - 1, {"gx": gx, "gy": jnp.minimum(gy + 1, ny - 1)}),
    )

    barrier = pltpu.get_barrier_semaphore()

    def tell(semaphore, steps):
        for device in (
            {"gx": lax.rem(gx + nx - steps, nx), "gy": gy},
            {"gx": lax.rem(gx + steps, nx), "gy": gy},
            {"gx": gx, "gy": lax.rem(gy + ny - steps, ny)},
            {"gx": gx, "gy": lax.rem(gy + steps, ny)},
        ):
            pl.semaphore_signal(semaphore, inc=1, device_id=device, device_id_type=MESH)

    def announce(number):
        if 2 << number < nx:
            tell(wave.at[number], 1 << number)

    def heard(number):
        if 2 << number < nx:
            pl.semaphore_wait(wave.at[number], 4)

    if nx > 1:
        tell(barrier, 1)

    loads = {}
    pairs = [("rhs", rhs_h, rhs), ("stf", stf_h, stf), ("mem", mem_h, mem)]
    for offset in (0, 5, 6, 1, 2, 3, 4):
        pairs.append(("cpl%d" % offset, cpl_h.at[pl.ds(9 * offset, 9)], cpl.at[pl.ds(9 * offset, 9)]))
    pairs += [
        ("snd", snd_h, snd),
        ("ctn", ctn_h, ctn),
        ("cmb", cmb_h, cmb),
        ("col", col_h, col),
        ("ten", ten_h, ten),
        ("cst", cst_h, cst),
        ("ccp", ccp_h, ccp),
        ("inv", inv_h, inv),
    ]
    for number, (name, source, target) in enumerate(pairs):
        loads[name] = pltpu.make_async_copy(source, target, load_sem.at[number])
        loads[name].start()

    def layer_out(number, side):
        return wout.at[number, side] if number < WIDE else hout.at[number - WIDE, side]

    def layer_in(number, side):
        return win.at[number, side] if number < WIDE else hin.at[number - WIDE, side]

    for side, (there, _) in enumerate(near):

        @pl.when(jnp.logical_not(there))
        def _():
            for number in range(FIELDS):
                target = layer_in(number, side)
                target[...] = jnp.zeros(target.shape, target.dtype)
            ext[0, :, pl.ds(A1 + H * side, H)] = jnp.zeros((8, H), F32)
            lift1[:, pl.ds(A1 + H * side, H)] = jnp.zeros((40, H), F32)
            if side < 2:
                parts[2 * side] = jnp.zeros(parts.shape[1:], F32)

    cacc[pl.ds(32, 8), :] = jnp.zeros((8, A1 + 4 * H), F32)
    own_row[...] = jnp.zeros_like(own_row)
    part_row[...] = jnp.zeros_like(part_row)

    def halo(number, side):
        return pltpu.make_async_remote_copy(
            src_ref=layer_out(number, side),
            dst_ref=layer_in(number, side ^ 1),
            send_sem=fsend.at[number, side],
            recv_sem=frecv.at[number, side ^ 1],
            device_id=near[side][1],
            device_id_type=MESH,
        )

    def pack(number, side, c, value):
        target = layer_out(number, side)
        target[c] = jnp.concatenate([value[:, : NZ // 2], value[:, NZ // 2 :]], axis=0).astype(target.dtype)

    def received(number, side, j):
        value = layer_in(number, side)[j].astype(F32)
        return jnp.concatenate([value[:8], value[8:]], axis=1)

    def send_halo(number, side):
        @pl.when(near[side][0])
        def _():
            halo(number, side).start()

    def wait_halo(number):
        for side in range(4):

            @pl.when(near[side][0])
            def _():
                halo(number, side ^ 1).wait_recv()

        for side in range(2):
            for j in range(3):
                yin[side, j] = received(number, side + 2, j)

    def put_field(number, x, values):
        for c in range(3):
            field[number, c, x] = values[c]
            yout[0, c, pl.ds(x, 1), :] = values[c][0:1, :]
            yout[1, c, pl.ds(x, 1), :] = values[c][FY - 1 : FY, :]
            if isinstance(x, int) and x == 0:
                pack(number, 0, c, values[c])
            if isinstance(x, int) and x == FX - 1:
                pack(number, 1, c, values[c])

    def slabs(number, slab):
        slab(0)
        if number is not None:
            send_halo(number, 0)
        slab(FX - 1)
        if number is not None:
            send_halo(number, 1)

        def inner(x, carry):
            slab(x)
            return carry

        lax.fori_loop(1, FX - 1, inner, 0)
        if number is not None:
            for side in range(2):
                for c in range(3):
                    pack(number, side + 2, c, yout[side, c])
                send_halo(number, side + 2)

    def add(total, offset, x, j, view):
        for i in range(3):
            total[i] = total[i] + cpl[9 * offset + 3 * i + j, x].astype(F32) * view

    def inside(number):
        lane = lax.broadcasted_iota(jnp.int32, (FY, NZ), 1)

        def slab(x):
            total = [stf[i, x] * field[number, i, x] for i in range(3)]
            for j in range(3):
                view = field[number, j, x]
                add(total, 0, x, j, view)
                add(total, 5, x, j, jnp.where(lane == 0, 0.0, pltpu.roll(view, 1, axis=1)))
                add(total, 6, x, j, jnp.where(lane == NZ - 1, 0.0, pltpu.roll(view, NZ - 1, axis=1)))
                if not (isinstance(x, int) and x == 0):
                    add(total, 1, x, j, field[number, j, x - 1])
                if not (isinstance(x, int) and x == FX - 1):
                    add(total, 2, x, j, field[number, j, x + 1])
            for i in range(3):
                acc[i, x] = total[i]

        slabs(None, slab)

    def outside(number, x):
        row = lax.broadcasted_iota(jnp.int32, (FY, NZ), 0)
        total = [acc[i, x] for i in range(3)]
        for j in range(3):
            view = field[number, j, x]
            below = yin[0, j, pl.ds(x, 1), :]
            above = yin[1, j, pl.ds(x, 1), :]
            add(total, 3, x, j, jnp.where(row == 0, below, pltpu.roll(view, 1, axis=0)))
            add(total, 4, x, j, jnp.where(row == FY - 1, above, pltpu.roll(view, FY - 1, axis=0)))
            if isinstance(x, int) and x == 0:
                add(total, 1, x, j, received(number, 0, j))
            if isinstance(x, int) and x == FX - 1:
                add(total, 2, x, j, received(number, 1, j))
        return total

    def coarse_halo(number, side):
        span = pl.ds(A1 + H * side, H)
        return pltpu.make_async_remote_copy(
            src_ref=lout.at[side] if number else cout.at[side],
            dst_ref=lift1.at[:, span] if number else ext.at[0, :, span],
            send_sem=csend.at[number, side],
            recv_sem=crecv.at[number, side],
            device_id=near[side ^ 1][1],
            device_id_type=MESH,
        )

    def wait_coarse(number):
        for side in range(4):

            @pl.when(near[side][0])
            def _():
                coarse_halo(number, side).wait_recv()

    def send_lift():
        lift1[pl.ds(0, 32), pl.ds(0, A1)] = ctn[pl.ds(0, 32), :]
        members = jnp.broadcast_to(cmb[...].astype(F32), (4, A1))
        lift1[pl.ds(32, 8), pl.ds(0, A1)] = jnp.concatenate([ctn[pl.ds(32, 4), :], members], axis=0)

        def one(piece, carry):
            rows8 = pl.ds(pl.multiple_of(8 * piece, 8), 8)
            tables = [lift1[rows8, pl.ds(LANES * h, LANES)] for h in range(A1 // LANES)]
            for side in range(4):
                for t in range(H // LANES):
                    span = pl.ds(LANES * t, LANES)
                    lout[side, rows8, span] = pick(tables, jnp.broadcast_to(snd[side : side + 1, span], (8, LANES)))
            return carry

        lax.fori_loop(0, 5, one, 0)
        for side in range(4):

            @pl.when(near[side ^ 1][0])
            def _():
                coarse_halo(1, side).start()

    loads["rhs"].wait()
    loads["stf"].wait()

    def first(x):
        values = []
        for c in range(3):
            weight = 1.0 / stf[c, x]
            wgt[c, x] = weight
            values.append(damping * rhs[c, x] * weight)
        put_field(0, x, values)

    if nx > 1:
        pl.semaphore_wait(barrier, 4)
    announce(0)
    slabs(0, first)

    count = lax.broadcasted_iota(jnp.int32, (16, NZ), 0).astype(F32).astype(BF16)

    def one_hot(index):
        width = index.shape[1]
        low = jnp.broadcast_to(index & (LANES - 1), (16, width)).astype(F32).astype(BF16)
        one, zero = jnp.ones((16, width), BF16), jnp.zeros((16, width), BF16)
        return jnp.concatenate(
            [jnp.where(low == count[:, :width] + float(16 * k), one, zero) for k in range(8)], axis=0
        )

    def hot_members(x, carry):
        for y in range(FY):
            ohm[x, :, pl.ds(NZ * y, NZ)] = one_hot(mem[x, pl.ds(y, 1), :])
        return carry

    def hot_columns(t, carry):
        span = pl.ds(pl.multiple_of(GROUP * t, GROUP), GROUP)
        columns = col[:, span]
        for k in range(K):
            ohc[k, :, span] = one_hot(columns[k : k + 1])
        return carry

    def choose(parts, index):
        bit = LANES
        while len(parts) > 1:
            upper = (index & bit) != 0
            parts = [jnp.where(upper, parts[at + 1], parts[at]) for at in range(0, len(parts), 2)]
            bit *= 2
        return parts[0]

    def table(values):
        pieces = [values[:, LANES * h : LANES * (h + 1)] for h in range(values.shape[1] // LANES)]
        value = jnp.concatenate(pieces, axis=0)
        rounded = value.astype(BF16).astype(F32)
        return jnp.concatenate([rounded, value - rounded], axis=1).astype(BF16)

    def look_up(entries, hot, index):
        product = jnp.dot(entries, jnp.concatenate([hot, hot], axis=0), preferred_element_type=F32)
        pieces = [product[8 * h : 8 * h + 8] for h in range(product.shape[0] // 8)]
        return choose(pieces, jnp.broadcast_to(index, (8, index.shape[1])))

    loads["mem"].wait()
    lax.fori_loop(0, FX, hot_members, 0)

    for offset in (0, 5, 6, 1, 2, 3, 4):
        loads["cpl%d" % offset].wait()

    def smoothed(number, x):
        total = outside(number, x)
        return [
            field[number, c, x] + damping * (rhs[c, x] - total[c]) * wgt[c, x] for c in range(3)
        ]

    inside(0)
    heard(0)
    announce(1)
    wait_halo(0)
    slabs(1, lambda x: put_field(1, x, smoothed(0, x)))

    def residual(x):
        total = outside(1, x)
        values = []
        for c in range(3):
            left = rhs[c, x] - total[c]
            resid[c, x] = left
            values.append(left * wgt[c, x])
        put_field(2, x, values)

    loads["snd"].wait()
    loads["ctn"].wait()
    loads["cmb"].wait()
    send_lift()
    inside(1)
    heard(1)
    announce(2)
    wait_halo(1)
    slabs(2, residual)

    loads["ten"].wait()

    fine_row = lax.broadcasted_iota(jnp.int32, (FY, NZ), 0)

    def restrict_own(x):
        total = [acc[i, x] for i in range(3)]
        for j in range(3):
            view = field[2, j, x]
            add(total, 3, x, j, jnp.where(fine_row == 0, 0.0, pltpu.roll(view, 1, axis=0)))
            add(total, 4, x, j, jnp.where(fine_row == FY - 1, 0.0, pltpu.roll(view, FY - 1, axis=0)))
        restrict(x, [resid[i, x] - smoothing * total[i] for i in range(3)])

    def restrict_rest(x):
        total = [jnp.zeros((FY, NZ), F32) for _ in range(3)]
        for j in range(3):
            below = yin[0, j, pl.ds(x, 1), :]
            above = yin[1, j, pl.ds(x, 1), :]
            add(total, 3, x, j, jnp.where(fine_row == 0, below, 0.0))
            add(total, 4, x, j, jnp.where(fine_row == FY - 1, above, 0.0))
            if isinstance(x, int) and x == 0:
                add(total, 1, x, j, received(2, 0, j))
            if isinstance(x, int) and x == FX - 1:
                add(total, 2, x, j, received(2, 1, j))
        restrict(x, [-smoothing * total[i] for i in range(3)])

    def restrict(x, filtered):
        for c in range(6):
            value = ten[c, x].astype(F32) * filtered[0]
            for i in range(1, 3):
                value = value + ten[6 * i + c, x].astype(F32) * filtered[i]
            for t in range(NZ // LANES):
                part = value[:, LANES * t : LANES * (t + 1)]
                nodes[x, t, pl.ds(8 * c, 8), :] = part
                if c < 2:
                    nodes[x, t, pl.ds(8 * (c + 6), 8), :] = part

    loads["inv"].wait()
    whole = inv[...]
    rounded = whole.astype(BF16)
    invs[0] = rounded
    invs[1] = (whole - rounded.astype(F32)).astype(BF16)
    inside(2)
    slabs(None, restrict_own)

    def sums(x, total, ys):
        for y in ys:
            value = jnp.concatenate(
                [nodes[x, t, pl.ds(y, 8, stride=8), :] for t in range(NZ // LANES)], axis=1
            )
            rounded = value.astype(BF16).astype(F32)
            both = jnp.concatenate([rounded, value - rounded], axis=0).astype(BF16)
            index = jnp.broadcast_to(mem[x, pl.ds(y, 1), :], (16, NZ))
            high = lax.shift_right_logical(index, 7).astype(F32).astype(BF16)
            zero = jnp.zeros((16, NZ), BF16)
            left = jnp.concatenate([jnp.where(high == float(h), both, zero) for h in range(8)], axis=0)
            right = ohm[x, :, pl.ds(NZ * y, NZ)]
            total = total + lax.dot_general(
                left, right, (((1,), (1,)), ((), ())), preferred_element_type=F32
            )
        return total

    gathered = lax.fori_loop(
        0, FX, lambda x, total: sums(x, total, range(FY)), jnp.zeros((16 * A1 // LANES, LANES), F32)
    )
    heard(2)
    wait_halo(2)
    wait_coarse(1)
    slabs(None, restrict_rest)
    gathered = sums(FX - 1, sums(0, gathered, range(FY)), range(FY))
    gathered = lax.fori_loop(1, FX - 1, lambda x, total: sums(x, total, (0, FY - 1)), gathered)

    loads["cst"].wait()
    for h in range(8):
        span = pl.ds(LANES * h, LANES)
        crhs[:, span] = gathered[16 * h : 16 * h + 8] + gathered[16 * h + 8 : 16 * h + 16]
    cst8 = jnp.concatenate([cst[...], cst[0:2, :]], axis=0)
    ext[0, :, pl.ds(0, A1)] = damping * crhs[...] / cst8

    def send_coarse():
        tables = [ext[0, :, pl.ds(LANES * h, LANES)] for h in range(A1 // LANES)]
        for side in range(4):
            for t in range(H // LANES):
                index = jnp.broadcast_to(snd[side : side + 1, pl.ds(LANES * t, LANES)], (8, LANES))
                cout[side, :, pl.ds(LANES * t, LANES)] = pick(tables, index)

            @pl.when(near[side ^ 1][0])
            def _():
                coarse_halo(0, side).start()

    sub = lax.broadcasted_iota(jnp.int32, (8, GROUP), 0)

    def coarse_apply(number):
        entries = table(ext[number])

        def group(t, carry):
            span = pl.ds(pl.multiple_of(GROUP * t, GROUP), GROUP)
            total = [jnp.zeros((8 if piece < 4 else 4, GROUP), F32) for piece in range(5)]
            columns = col[:, span]
            for k in range(K):
                base = look_up(entries, ohc[k, :, span], columns[k : k + 1])
                up2, by4, down2 = (pltpu.roll(base, by, axis=0) for by in (6, 4, 2))
                turned = (base, jnp.where(sub < 6, up2, by4), jnp.where(sub < 2, by4, down2))
                for piece in range(5):
                    size = 8 if piece < 4 else 4
                    block = ccp[k, pl.ds(8 * piece, size), span]
                    total[piece] = total[piece] + block * turned[piece % 3][:size]
            for piece in range(5):
                cacc[pl.ds(8 * piece, 8 if piece < 4 else 4), span] = total[piece]
            return carry

        lax.fori_loop(0, A1 // GROUP, group, 0)

    fold_row = lax.broadcasted_iota(jnp.int32, (8, 40), 0)
    fold_col = lax.broadcasted_iota(jnp.int32, (8, 40), 1)
    fold_row = jnp.where(fold_row < 6, fold_row, fold_row - 6)
    fold = jnp.logical_and(fold_col >= 6 * fold_row, fold_col < 6 * fold_row + 6).astype(F32)

    fold = fold.astype(BF16)

    def fold_rows(values):
        rounded = values.astype(BF16)
        rest = (values - rounded.astype(F32)).astype(BF16)
        return jnp.dot(fold, rounded, preferred_element_type=F32) + jnp.dot(fold, rest, preferred_element_type=F32)

    def folded():
        return fold_rows(cacc[:, pl.ds(0, A1)])

    send_coarse()
    loads["col"].wait()
    lax.fori_loop(0, A1 // GROUP, hot_columns, 0)
    loads["ccp"].wait()
    wait_coarse(0)
    coarse_apply(0)
    s1 = crhs[...] - (cst8 * ext[0, :, pl.ds(0, A1)] + folded())

    lane = lax.broadcasted_iota(jnp.int32, (1, 2 * LANES), 1)
    upper = cmb[...] != 0
    row = jnp.zeros((1, 2 * LANES), F32)
    for piece in range(5):
        size = 8 if piece < 4 else 4
        i, c = rows_of(piece, size)
        first_i, last_i = (8 * piece) // 6, min((8 * piece + 7) // 6, 5)
        matching = jnp.where(i == first_i, s1[first_i : first_i + 1], s1[last_i : last_i + 1])
        product = ctn[pl.ds(8 * piece, size), :] * matching
        for a in range(2):
            kept = jnp.where(upper, product, 0.0) if a else jnp.where(upper, 0.0, product)
            total = jnp.sum(kept, axis=1, keepdims=True)
            place = 12 * gy + 2 * c + a
            row = row + jnp.sum(jnp.where(lane == place, total, 0.0), axis=0, keepdims=True)
    own_row[...] = row

    def to_row(step):
        other = lax.rem(gy + step, ny)
        return pltpu.make_async_remote_copy(
            src_ref=own_row,
            dst_ref=rows.at[gy],
            send_sem=gsend.at[other],
            recv_sem=grecv.at[gy],
            device_id={"gx": gx, "gy": other},
            device_id_type=MESH,
        )

    def from_row(other):
        return pltpu.make_async_remote_copy(
            src_ref=own_row,
            dst_ref=rows.at[other],
            send_sem=gsend.at[other],
            recv_sem=grecv.at[other],
            device_id={"gx": gx, "gy": other},
            device_id_type=MESH,
        )

    far_first = sorted(range(1, ny), key=lambda step: -min(step, ny - step))
    for step in far_first:
        to_row(step).start()
    for step in range(1, ny):
        from_row(lax.rem(gy + step, ny)).wait_recv()
    rows[gy] = row
    entries = jnp.sum(rows[...], axis=0)
    block = inv.shape[1]
    values = entries[:, :block]
    rounded = values.astype(BF16).astype(F32)
    values = jnp.concatenate(
        [jnp.broadcast_to(rounded, (8, block)), jnp.broadcast_to(values - rounded, (8, block))], axis=0
    ).astype(BF16)
    upper_part, lower_part = (
        lax.dot_general(values, invs[at], (((1,), (1,)), ((), ())), preferred_element_type=F32) for at in range(2)
    )
    product = upper_part[0:1] + (upper_part[8:9] + lower_part[0:1] + lower_part[8:9])
    part_row[:, pl.ds(0, block)] = product

    def part(at, row_of, semaphore, device):
        return pltpu.make_async_remote_copy(
            src_ref=part_row,
            dst_ref=parts.at[at, row_of],
            send_sem=psend.at[at, semaphore],
            recv_sem=precv.at[at, row_of],
            device_id=device,
            device_id_type=MESH,
        )

    def to_part(at, step):
        other = lax.rem(gy + step, ny)
        return part(at, gx, step, {"gx": jnp.clip(gy + 1 - at, 0, nx - 1), "gy": other})

    def from_part(at, step):
        other = lax.rem(gx + step, nx)
        return part(at, other, 0, {"gx": other, "gy": jnp.clip(gx + at - 1, 0, ny - 1)})

    for steps in (far_first[: ny // 2], far_first[ny // 2 :]):
        for at in (0, 2, 1):
            target = gy + 1 - at

            @pl.when(jnp.logical_and(target >= 0, target < nx))
            def _():
                for step in steps:
                    to_part(at, step).start()

    for at in (0, 2, 1):
        target = gy + 1 - at

        @pl.when(jnp.logical_and(target >= 0, target < nx))
        def _():
            @pl.when(gx != target)
            def _():
                to_part(at, 0).start()

            @pl.when(gx == target)
            def _():
                parts[at, gx] = part_row[...]

    for at in (1, 0, 2):
        held = gx + at - 1

        @pl.when(jnp.logical_and(held >= 0, held < ny))
        def _():
            for step in range(1, nx):
                from_part(at, step).wait_recv()

            @pl.when(gy != held)
            def _():
                from_part(at, 0).wait_recv()

    coarsest = [jnp.sum(parts[at], axis=0) for at in range(3)]

    places = (
        (0, A1, 1, gy),
        (A1, H, 0, gy),
        (A1 + H, H, 2, gy),
        (A1 + 2 * H, H, 1, gy - 1),
        (A1 + 3 * H, H, 1, gy + 1),
    )
    for start, length, at, owner in places:
        span = pl.ds(start, length)
        one = lift1[36:37, span] != 0.0
        for piece in range(5):
            size = 8 if piece < 4 else 4
            _, c = rows_of(piece, size)
            spread = [
                jnp.sum(jnp.where(lane == 12 * owner + 2 * c + a, coarsest[at], 0.0), axis=1, keepdims=True)
                for a in range(2)
            ]
            here = pl.ds(8 * piece, size)
            cacc[here, span] = lift1[here, span] * jnp.where(one, spread[1], spread[0])
    ext[1] = ext[0] + fold_rows(cacc[...])
    coarse_apply(1)
    solved = ext[1, :, pl.ds(0, A1)]
    solved = solved + damping * (crhs[...] - (cst8 * solved + folded())) / cst8
    y2[...] = solved
    csol[...] = solved[0:6]

    entries = table(y2[...])
    tables = [y2[:, pl.ds(LANES * h, LANES)] for h in range(A1 // LANES)]

    def lift(x):
        for y in range(FY):
            taken = look_up(entries, ohm[x, :, pl.ds(NZ * y, HALF)], mem[x, pl.ds(y, 1), pl.ds(0, HALF)])
            for t in range(NZ // LANES):
                if t < HALF // LANES:
                    value = taken[:, LANES * t : LANES * (t + 1)]
                else:
                    index = mem[x, pl.ds(y, 1), pl.ds(LANES * t, LANES)]
                    value = pick(tables, jnp.broadcast_to(index, (8, LANES)))
                nodes[x, t, pl.ds(y, 8, stride=8), :] = value
        values = []
        for i in range(3):
            value = 0.0
            for c in range(6):
                taken = jnp.concatenate(
                    [nodes[x, t, pl.ds(8 * c, 8), :] for t in range(NZ // LANES)], axis=1
                )
                value = value + ten[6 * i + c, x].astype(F32) * taken
            values.append(value)
        put_field(3, x, values)

    slabs(3, lift)

    def sent_halos(first_number, last_number):
        for side in range(4):

            @pl.when(near[side][0])
            def _():
                for number in range(first_number, last_number):
                    halo(number, side).wait_send()

    def sent_lists():
        for side in range(4):

            @pl.when(near[side][0])
            def _():
                for number in range(2):
                    coarse_halo(number, side ^ 1).wait_send()

        for step in range(1, ny):
            to_row(step).wait_send()

    def sent_parts():
        for at in range(3):
            target = gy + 1 - at

            @pl.when(jnp.logical_and(target >= 0, target < nx))
            def _():
                for step in range(1, ny):
                    to_part(at, step).wait_send()

                @pl.when(gx != target)
                def _():
                    to_part(at, 0).wait_send()

    def corrected(x):
        total = outside(3, x)
        put_field(
            4,
            x,
            [
                field[1, c, x] + field[3, c, x] - smoothing * total[c] * wgt[c, x]
                for c in range(3)
            ],
        )

    inside(3)
    wait_halo(3)
    slabs(4, corrected)

    inside(4)
    sent_lists()
    sent_halos(0, 4)
    wait_halo(4)
    slabs(5, lambda x: put_field(5, x, smoothed(4, x)))

    def last(x):
        values = smoothed(5, x)
        for c in range(3):
            sol[c, x] = values[c]

    inside(5)
    sent_parts()
    wait_halo(5)
    slabs(None, last)

    sent_halos(4, 6)


def write_out(sol, csol, sol_h, csol_h, sem):
    copies = [pltpu.make_async_copy(sol, sol_h, sem.at[0]), pltpu.make_async_copy(csol, csol_h, sem.at[1])]
    for copy in copies:
        copy.start()
    for copy in copies:
        copy.wait()


def body(nx, ny, rhs, stiffness, couplings, tentative, members, cst, ccp, col, snd, ctn, cmb, inv):
    couplings = couplings.reshape(63, FX, FY, NZ)
    tentative = tentative.reshape(18, FX, FY, NZ)
    cmb = cmb.reshape(1, A1)
    operands = (rhs, stiffness, couplings, tentative, members, cst, ccp, col, snd, ctn, cmb, inv)
    dma = pltpu.SemaphoreType.DMA
    scratch = [pltpu.VMEM(operand.shape, operand.dtype) for operand in operands]
    scratch += [
        pltpu.VMEM((3, FX, FY, NZ), F32),
        pltpu.VMEM((FIELDS, 3, FX, FY, NZ), F32),
        pltpu.VMEM((2, 3, FX, NZ), F32),
        pltpu.VMEM((2, 3, FX, NZ), F32),
        pltpu.VMEM((FIELDS - WIDE, 4, 3, 16, NZ // 2), BF16),
        pltpu.VMEM((FIELDS - WIDE, 4, 3, 16, NZ // 2), BF16),
        pltpu.VMEM((WIDE, 4, 3, 16, NZ // 2), F32),
        pltpu.VMEM((WIDE, 4, 3, 16, NZ // 2), F32),
        pltpu.VMEM((3, FX, FY, NZ), F32),
        pltpu.VMEM((3, FX, FY, NZ), F32),
        pltpu.VMEM((FX, NZ // LANES, 8 * FY, LANES), F32),
        pltpu.VMEM((8, A1), F32),
        pltpu.VMEM((8, A1), F32),
        pltpu.VMEM((2, 8, A1 + 4 * H), F32),
        pltpu.VMEM((4, 8, H), F32),
        pltpu.VMEM((40, A1 + 4 * H), F32),
        pltpu.VMEM((40, A1 + 4 * H), F32),
        pltpu.VMEM((4, 40, H), F32),
        pltpu.VMEM((2, *inv.shape), BF16),
        pltpu.VMEM((FX, LANES, FY * NZ), BF16),
        pltpu.VMEM((K, LANES, A1), BF16),
        pltpu.VMEM((1, 2 * LANES), F32),
        pltpu.VMEM((ny, 1, 2 * LANES), F32),
        pltpu.VMEM((1, 2 * LANES), F32),
        pltpu.VMEM((3, nx, 1, 2 * LANES), F32),
        pltpu.SemaphoreType.REGULAR((3,)),
        dma((18,)),
        dma((FIELDS, 4)),
        dma((FIELDS, 4)),
        dma((2, 4)),
        dma((2, 4)),
        dma((ny,)),
        dma((ny,)),
        dma((3, ny)),
        dma((3, nx)),
    ]
    results = pl.pallas_call(
        functools.partial(kernel, nx, ny),
        out_shape=(pltpu.VMEM((3, FX, FY, NZ), F32), pltpu.VMEM((6, A1), F32)),
        in_specs=[pl.BlockSpec(memory_space=pl.ANY)] * len(operands),
        out_specs=(pl.BlockSpec(memory_space=pltpu.VMEM),) * 2,
        scratch_shapes=scratch,
        compiler_params=pltpu.CompilerParams(
            collective_id=0, has_side_effects=True, vmem_limit_bytes=56 * 1024 * 1024
        ),
    )(*operands)
    return pl.pallas_call(
        write_out,
        out_shape=tuple(jax.ShapeDtypeStruct(result.shape, result.dtype) for result in results),
        in_specs=[pl.BlockSpec(memory_space=pltpu.VMEM)] * 2,
        out_specs=(pl.BlockSpec(memory_space=pl.ANY),) * 2,
        scratch_shapes=[dma((2,))],
        compiler_params=pltpu.CompilerParams(vmem_limit_bytes=60 * 1024 * 1024),
    )(*[pltpu.with_memory_space_constraint(result, pltpu.VMEM) for result in results])


def solution(mesh):
    placed = (
        P(None, "gx", "gy", None),
        P(None, "gx", "gy", None),
        P(None, None, None, "gx", "gy", None),
        P(None, None, "gx", "gy", None),
        P("gx", "gy", None),
        P(None, ("gx", "gy")),
        P(None, None, ("gx", "gy")),
        P(None, ("gx", "gy")),
        P(None, ("gx", "gy")),
        P(None, ("gx", "gy")),
        P(("gx", "gy")),
        P("gy", "gx"),
    )
    return jax.shard_map(
        functools.partial(body, mesh.shape["gx"], mesh.shape["gy"]),
        mesh=mesh,
        in_specs=placed,
        out_specs=(P(None, "gx", "gy", None), P(None, ("gx", "gy"))),
        check_vma=False,
    )
```
